256 devices in a mesh: gx: 16 (over z_hi, x), gy: 16 (over z_lo, y, core).
Axes of the slice: x: 4, y: 4, z: 8 (z_hi: 4, z_lo: 2; z = z_hi * 2 + z_lo), core: 2. Of those that a mesh axis runs over, the one named last changes fastest.
Arguments:
- skip_feat: bfloat16 [64, 32, 128, 128], P(None, 'gx', 'gy'), may hold values from -6 to 6
- cotangent: bfloat16 [64, 32, 128, 128], P(None, 'gx', 'gy'), may hold values from -6 to 6
- w_coarse: bfloat16 [27, 64, 128], replicated, may hold values from -0.15625 to 0.15625
- w_dec: bfloat16 [27, 192, 64], replicated, may hold values from -0.078125 to 0.078125
Outputs:
- skip_grad: bfloat16 [64, 32, 128, 128], P(None, 'gx', 'gy')
- dec_total: float32 [27, 192, 64], replicated
- coarse_total: float32 [27, 64, 128], replicated
The draws below stay inside these ranges and needn't reach their ends.
All inputs are finite; a program needn't handle non-finite values.
Results may differ from the reference program's by a relative error of at most 0.01.
Values may be sent and summed in bfloat16 or wider, within the bound.
No kernel may reach another device: no remote copies, remote signals or barrier semaphores. Data moves between devices by JAX's collectives and lax.ppermute only.
A program may use at most 128 MiB of HBM per device.

```python
import math
import jax
import jax.numpy as jnp
from jax import lax

CSKIP = 64
CCOARSE = 128
CCAT = 192
NX = 32
NY = 128
NZ = 128


def steps_of(rng, shape, shards, smallest, largest):
    level, own = 1.0, jax.random.fold_in(rng, 6)
    for dim, shards_of in shards:
        heights = jnp.exp(jax.random.uniform(jax.random.fold_in(own, dim), (shards_of,), jnp.float32, smallest / len(shards), largest / len(shards)))
        level = level * jnp.repeat(heights, shape[dim] // shards_of).reshape([-1 if axis == dim else 1 for axis in range(len(shape))])
    return level


def noise(key, dims, scale, most, cuts=(), held_as=jnp.bfloat16):
    drawn = jax.random.normal(key, dims, jnp.float32) * scale
    if len(cuts) > 0:
        drawn = steps_of(key, dims, cuts, -0.22, 0.18) * drawn
    return jnp.clip(drawn, min=-most, max=most).astype(held_as)


def setup_inputs(seed: int = 0) -> dict:
    streams_of = jax.random.split(jax.random.key(seed), 5)
    skip_feat = noise(streams_of[0], (CSKIP, NX, NY, NZ), 1.0, 6.0, ((1, 16), (2, 16)))
    cotangent = noise(streams_of[1], (CSKIP, NX, NY, NZ), 1.0, 6.0, ((1, 16), (2, 16)))
    w_coarse = noise(streams_of[2], (27, CSKIP, CCOARSE), (27 * CSKIP) ** -0.5, 0.15625)
    w_dec = noise(streams_of[3], (27, CCAT, CSKIP), (27 * CCAT) ** -0.5, 0.078125)
    return {"skip_feat": skip_feat, "cotangent": cotangent, "w_coarse": w_coarse, "w_dec": w_dec}


def conv_cells(field, weights):
    in_chan = weights.shape[1]
    out_chan = weights.shape[2]
    kernel = weights.reshape(3, 3, 3, in_chan, out_chan).transpose(4, 3, 0, 1, 2)
    result = lax.conv_general_dilated(field[None], kernel, (1, 1, 1), 'SAME', dimension_numbers=('NCDHW', 'OIDHW', 'NCDHW'), precision=lax.Precision.HIGHEST)
    return result[0]

def block_pool(field):
    chans, size_x, size_y, size_z = field.shape
    return field.reshape(chans, size_x // 2, 2, size_y // 2, 2, size_z // 2, 2)

def upsample(field):
    chans, size_x, size_y, size_z = field.shape
    grown = jnp.broadcast_to(field[:, :, None, :, None, :, None], (chans, size_x, 2, size_y, 2, size_z, 2))
    return grown.reshape(chans, 2 * size_x, 2 * size_y, 2 * size_z)

def transpose_of(func, point, cot):
    return jax.vjp(func, point)[1](cot)[0]

def reference(skip_feat, cotangent, w_coarse, w_dec):
    factor = 1.0 / math.sqrt(NX * NY * NZ)
    pooled = block_pool(skip_feat.astype(jnp.float32)).mean(axis=(2, 4, 6)).astype(jnp.bfloat16)
    pooled_wide = pooled.astype(jnp.float32)
    coarse_weights = w_coarse.astype(jnp.float32)
    dec_weights = w_dec.astype(jnp.float32)
    pre_b = conv_cells(pooled_wide, coarse_weights)
    coarse_out = jax.nn.silu(pre_b).astype(jnp.bfloat16)
    joined = jnp.concatenate([upsample(coarse_out), skip_feat], axis=0).astype(jnp.float32)
    cot_wide = cotangent.astype(jnp.float32)
    joined_grad = transpose_of(lambda value: conv_cells(value, dec_weights), joined, cot_wide)
    dec_total = transpose_of(lambda weights: conv_cells(joined, weights), dec_weights, cot_wide) * factor
    coarse_grad = block_pool(joined_grad[:CCOARSE]).sum(axis=(2, 4, 6))
    sigmoid_pre = jax.nn.sigmoid(pre_b)
    pre_grad = (coarse_grad * sigmoid_pre * (1.0 + pre_b * (1.0 - sigmoid_pre))).astype(jnp.bfloat16)
    pre_wide = pre_grad.astype(jnp.float32)
    coarse_total = transpose_of(lambda weights: conv_cells(pooled_wide, weights), coarse_weights, pre_wide) * factor
    pooled_grad = transpose_of(lambda value: conv_cells(value, coarse_weights), pooled_wide, pre_wide)
    skip_grad = (joined_grad[CCOARSE:] + upsample(pooled_grad) * 0.125).astype(jnp.bfloat16)
    return (skip_grad, dec_total, coarse_total)
```

```python
import functools
import math

import jax
import jax.numpy as jnp
from jax import lax
from jax.experimental import pallas as pl
from jax.experimental.pallas import tpu as pltpu
from jax.sharding import PartitionSpec as P

LANES = 128
SKIP, COARSE, JOINED = 64, 128, 192
SIZE_X, SIZE_Y = 2, 8
BLOCKS, BLOCKS_C = SIZE_X * SIZE_Y, SIZE_Y // 2
TAPS = 27
DEC = TAPS * SKIP
PACKED = DEC + DEC // 2 + DEC
ROWS = 136
CHUNKS = 32
SENT = CHUNKS // 2 * ROWS
FACE, FACE_Y = SIZE_Y + BLOCKS_C // 2, SIZE_X + 1
BF16, F32 = jnp.bfloat16, jnp.float32


def params(mib):
    return pltpu.CompilerParams(vmem_limit_bytes=mib << 20)


def lane_of(shape):
    return lax.broadcasted_iota(jnp.int32, shape, len(shape) - 1)


def is_even(value):
    return (lane_of(value.shape) & 1) == 0


def paired(value):
    return value + jnp.where(is_even(value), pltpu.roll(value, LANES - 1, 1), pltpu.roll(value, 1, 1))


def pack(first, second):
    return jnp.where(is_even(first), first, second)


def unpack_pair(value):
    even = is_even(value)
    return (
        jnp.where(even, value, pltpu.roll(value, 1, 1)),
        jnp.where(even, pltpu.roll(value, LANES - 1, 1), value),
    )


def shifted(value, step):
    if step == 0:
        return value
    lane = lane_of(value.shape)
    inside = lane < LANES - step if step > 0 else lane >= -step
    return jnp.where(inside, pltpu.roll(value, (-step) % LANES, 1), 0.0)


def places():
    return lax.axis_index("gx"), lax.axis_index("gy")


def sides(place):
    odd = (place & 1).astype(F32)
    inner = jnp.where((place == 0) | (place == 15), 0.0, 1.0).astype(F32)
    return (odd, (1.0 - odd) * inner), (1.0 - odd, odd * inner)


def mixed(weights, first, second):
    return weights[0] * first.astype(F32) + weights[1] * second.astype(F32)


def split_kernel(
    skip_hbm, cot_hbm, skip_out, cot_out, pool_out, *refs,
):
    faces, (skip_ref, cot_ref, rows_ref, arrived) = refs[:8], refs[8:]
    ups = [(1 - (place & 1), place & 1) for place in places()]
    copies = [
        pltpu.make_async_copy(source, target, arrived.at[index])
        for index, (source, target) in enumerate(((cot_hbm, cot_ref), (skip_hbm, skip_ref)))
    ]
    for copy in copies:
        copy.start()

    def block_of(index):
        return rows_ref[pl.ds(index, SKIP, stride=BLOCKS), :]

    copies[0].wait()
    rows_ref[...] = cot_ref[...].astype(F32).reshape(SKIP * BLOCKS, LANES)
    for index in range(BLOCKS):
        cot_out[index] = block_of(index).astype(BF16)
    copies[1].wait()
    rows_ref[...] = skip_ref[...].astype(F32).reshape(SKIP * BLOCKS, LANES)
    pools = []
    for coarse in range(BLOCKS_C):
        total = None
        for index in (2 * coarse, 2 * coarse + 1, SIZE_Y + 2 * coarse, SIZE_Y + 2 * coarse + 1):
            block = block_of(index)
            skip_out[index] = block.astype(BF16)
            total = block if total is None else total + block
        pools.append(paired(total) * 0.125)
        pool_out[coarse] = pools[-1].astype(BF16)
    packed = [pack(pools[2 * index], pools[2 * index + 1]).astype(BF16) for index in range(BLOCKS_C // 2)]
    for which in range(2):
        up_x, up_y = ups[0][which], ups[1][which]
        for row in range(SIZE_Y):
            faces[which][row] = cot_out[up_x * SIZE_Y + row]
        for index, value in enumerate(packed):
            faces[which][SIZE_Y + index] = value
        row, row_c = up_y * (SIZE_Y - 1), up_y * (BLOCKS_C - 1)
        for plane in range(SIZE_X):
            faces[2 + which][plane] = cot_out[plane * SIZE_Y + row]
        faces[2 + which][SIZE_X] = pool_out[row_c]
        for other in range(2):
            corner = faces[4 + 2 * other + which]
            corner[0] = cot_out[ups[0][other] * SIZE_Y + row]
            corner[1] = pool_out[row_c]


def vmem():
    return pl.BlockSpec(memory_space=pltpu.VMEM)


def call(kernel, name, outs, scratch, mib, cost, *operands, held=pltpu.VMEM):
    return pl.pallas_call(
        kernel,
        out_shape=tuple(jax.ShapeDtypeStruct(shape, dtype) for shape, dtype in outs),
        in_specs=[pl.BlockSpec(memory_space=held)] * len(operands),
        out_specs=tuple(vmem() for _ in outs),
        scratch_shapes=[pltpu.VMEM(*form) if isinstance(form, tuple) else form for form in scratch],
        compiler_params=params(mib),
        cost_estimate=pl.CostEstimate(flops=cost[0], bytes_accessed=cost[1], transcendentals=0),
        name=name,
    )(*operands)


def grads_kernel(
    skip_ref, cot_ref, pool_ref, xone_ref, xtwo_ref, yone_ref, ytwo_ref, *refs,
):
    corner_refs, (wdec_ref, wpre_ref, wback_ref) = refs[:4], refs[4:7]
    send_out, keep_out, jskip_out, rim_out, two_out = refs[7:12]
    cells_ref, pooled_ref, joined_ref, jgrad_ref, full_ref, pre_ref = refs[12:]
    factor = 1.0 / math.sqrt(524288)
    place = places()
    xlow, xhigh = sides(place[0])
    ylow, yhigh = sides(place[1])

    def corner(xside, yside, index):
        first = mixed(yside, corner_refs[0][index], corner_refs[1][index])
        second = mixed(yside, corner_refs[2][index], corner_refs[3][index])
        return mixed(xside, first, second)

    def fine(plane, row):
        yside = {0: ylow, SIZE_Y + 1: yhigh}.get(row)
        xside = {0: xlow, SIZE_X + 1: xhigh}.get(plane)
        if xside and yside:
            return corner(xside, yside, 0)
        if yside:
            return mixed(yside, yone_ref[plane - 1], ytwo_ref[plane - 1])
        if xside:
            return mixed(xside, xone_ref[row - 1], xtwo_ref[row - 1])
        return cot_ref[(plane - 1) * SIZE_Y + row - 1].astype(F32)

    wide_pool = {}
    for row, yside in ((0, ylow), (BLOCKS_C + 1, yhigh)):
        wide_pool[0, row] = corner(xlow, yside, 1)
        wide_pool[1, row] = mixed(yside, yone_ref[SIZE_X], ytwo_ref[SIZE_X])
        wide_pool[2, row] = corner(xhigh, yside, 1)
    for plane, weights in ((0, xlow), (2, xhigh)):
        for index in range(BLOCKS_C // 2):
            at = SIZE_Y + index
            first, second = unpack_pair(mixed(weights, xone_ref[at], xtwo_ref[at]))
            wide_pool[plane, 2 * index + 1], wide_pool[plane, 2 * index + 2] = first, second
    for row in range(BLOCKS_C):
        wide_pool[1, row + 1] = pool_ref[row].astype(F32)

    for plane in range(3):
        for row in range(BLOCKS_C + 2):
            for k in range(3):
                value = shifted(wide_pool[plane, row], 2 * (k - 1)).astype(BF16)
                for j in range(3):
                    if 0 <= row - j < BLOCKS_C:
                        tap = 9 * plane + 3 * j + k
                        pooled_ref[tap * SKIP : (tap + 1) * SKIP, (row - j) * LANES : (row - j + 1) * LANES] = value
    pre_b = jnp.dot(wpre_ref[...], pooled_ref[...], preferred_element_type=F32)
    sig = 1.0 / (1.0 + jnp.exp(-pre_b))
    coarse_out = (pre_b * sig).astype(BF16)
    slope = sig * (1.0 + pre_b * (1.0 - sig))
    for index in range(BLOCKS):
        at = (index % SIZE_Y) // 2
        joined_ref[:COARSE, index * LANES : (index + 1) * LANES] = coarse_out[:, at * LANES : (at + 1) * LANES]
        joined_ref[COARSE:, index * LANES : (index + 1) * LANES] = skip_ref[index]
    for plane in range(SIZE_X + 2):
        for row in range(SIZE_Y + 2):
            wide = fine(plane, row)
            for k in range(3):
                value = shifted(wide, 1 - k).astype(BF16)
                for i in range(3):
                    for j in range(3):
                        x, y = plane - 2 + i, row - 2 + j
                        if 0 <= x < SIZE_X and 0 <= y < SIZE_Y:
                            tap, at = 9 * i + 3 * j + k, x * SIZE_Y + y
                            cells_ref[tap * SKIP : (tap + 1) * SKIP, at * LANES : (at + 1) * LANES] = value
    jgrad_ref[...] = jnp.dot(wdec_ref[...], cells_ref[...], preferred_element_type=F32)
    for index in range(BLOCKS):
        jskip_out[index] = jgrad_ref[COARSE:, index * LANES : (index + 1) * LANES]
    pre_parts = []
    for at in range(BLOCKS_C):
        total = None
        for index in (2 * at, 2 * at + 1, SIZE_Y + 2 * at, SIZE_Y + 2 * at + 1):
            part = jgrad_ref[:COARSE, index * LANES : (index + 1) * LANES]
            total = part if total is None else total + part
        pre_part = (paired(total) * slope[:, at * LANES : (at + 1) * LANES]).astype(BF16)
        pre_parts.append(pre_part)
        wide = pre_part.astype(F32)
        for k in range(3):
            pre_ref[k * COARSE : (k + 1) * COARSE, at * LANES : (at + 1) * LANES] = shifted(wide, 2 * (1 - k)).astype(BF16)
    pre_grad = jnp.concatenate(pre_parts, axis=1)

    terms = jnp.dot(wback_ref[...], pre_ref[...], preferred_element_type=F32) * 0.125

    def rim_row(i, row):
        total = None
        for j in range(3):
            if 0 <= row - j < BLOCKS_C:
                first = (3 * i + j) * SKIP
                part = terms[first : first + SKIP, (row - j) * LANES : (row - j + 1) * LANES]
                total = part if total is None else total + part
        return total

    for i in range(3):
        for row in range(BLOCKS_C):
            rim_out[BLOCKS_C * i + row] = rim_row(i, row + 1)
    odd = (place[1] & 1).astype(F32)
    for index in range(2):
        down, up = (
            pack(rim_row(0, row), rim_row(1, row)) if index == 0 else rim_row(2, row) for row in (0, BLOCKS_C + 1)
        )
        send_out[SENT + index * SKIP : SENT + (index + 1) * SKIP] = ((1.0 - odd) * up + odd * down).astype(BF16)
        two_out[index] = ((1.0 - odd) * down + odd * up).astype(BF16)

    across = (((1,), (1,)), ((), ()))
    dec = lax.dot_general(cells_ref[...], joined_ref[...], across, preferred_element_type=F32) * factor
    full_ref[:DEC] = dec[:, :LANES]
    full_ref[DEC : DEC + DEC // 2] = jnp.concatenate([dec[: DEC // 2, LANES:], dec[DEC // 2 :, LANES:]], axis=1)
    full_ref[DEC + DEC // 2 : PACKED] = lax.dot_general(
        pooled_ref[...], pre_grad, across, preferred_element_type=F32
    ) * (0.5 * factor)
    full_ref[PACKED:] = jnp.zeros((CHUNKS * ROWS - PACKED, LANES), F32)
    core, y, x = place[1] & 1, (place[1] >> 1) & 3, place[0] & 3
    for yr in range(4):
        leave = []
        for xr in range(4):
            at = (y ^ yr) * 4 + (x ^ xr)
            row = pl.multiple_of((at + 16 * core) * ROWS, ROWS)
            keep_out[yr, xr] = full_ref[pl.ds(row, ROWS), :]
            row = pl.multiple_of((at + 16 * (1 - core)) * ROWS, ROWS)
            leave.append(full_ref[pl.ds(row, ROWS), :])
        send_out[4 * yr * ROWS : 4 * (yr + 1) * ROWS] = jnp.concatenate(leave).astype(BF16)


def fold_kernel(rim_ref, yone_ref, ytwo_ref, rows_out, one_out, two_out):
    place = places()
    planes = [[rim_ref[BLOCKS_C * i + row] for row in range(BLOCKS_C)] for i in range(3)]
    for weights, row in zip(sides(place[1]), (0, BLOCKS_C - 1)):
        first, second = unpack_pair(mixed(weights, yone_ref[0], ytwo_ref[0]))
        third = mixed(weights, yone_ref[1], ytwo_ref[1])
        for i, terms in enumerate((first, second, third)):
            planes[i][row] = planes[i][row] + terms
    for row in range(BLOCKS_C):
        rows_out[row] = planes[1][row]
    odd = (place[0] & 1).astype(F32)
    for index in range(BLOCKS_C // 2):
        down, up = (pack(planes[i][2 * index], planes[i][2 * index + 1]) for i in (0, 2))
        one_out[index] = ((1.0 - odd) * up + odd * down).astype(BF16)
        two_out[index] = ((1.0 - odd) * down + odd * up).astype(BF16)


def skip_kernel(rows_ref, xone_ref, xtwo_ref, jskip_ref, out_ref, cells_ref):
    low, high = sides(places()[0])
    weights = (low[0] + high[0], low[1] + high[1])
    for pair in range(BLOCKS_C // 2):
        for at, terms in zip((2 * pair, 2 * pair + 1), unpack_pair(mixed(weights, xone_ref[pair], xtwo_ref[pair]))):
            total = rows_ref[at] + terms
            for index in (2 * at, 2 * at + 1, SIZE_Y + 2 * at, SIZE_Y + 2 * at + 1):
                cells_ref[pl.ds(index, SKIP, stride=BLOCKS), :] = jskip_ref[index] + total
    out_ref[...] = cells_ref[...].reshape(SKIP, SIZE_X, SIZE_Y, LANES).astype(BF16)


def unpack_kernel(a0_ref, a1_ref, b0_ref, b1_ref, core_ref, dec_out, coarse_out, full_ref):
    place = places()
    core, y, x = place[1] & 1, (place[1] >> 1) & 3, place[0] & 3
    for half, (refs, order) in enumerate((((a0_ref, a1_ref), ORDER_A), ((b0_ref, b1_ref), ORDER_B))):
        for index, yr in enumerate(order):
            for xr in range(2):
                at = (y ^ yr) * 4 + (x ^ (2 * half + xr))
                row = pl.multiple_of((at + 16 * core) * ROWS, ROWS)
                full_ref[pl.ds(row, ROWS), :] = refs[index // 2][index % 2, xr].astype(F32)
                row = pl.multiple_of((at + 16 * (1 - core)) * ROWS, ROWS)
                full_ref[pl.ds(row, ROWS), :] = core_ref[4 * half + index, xr].astype(F32)
    half = LANES // 2
    dec_out[:, :LANES] = full_ref[:DEC]
    dec_out[: DEC // 2, LANES:] = full_ref[DEC : DEC + DEC // 2, :half]
    dec_out[DEC // 2 :, LANES:] = full_ref[DEC : DEC + DEC // 2, half:]
    coarse_out[...] = full_ref[DEC + DEC // 2 : PACKED]


def swap(value, axis, flip):
    return lax.ppermute(value, axis, [(i, i ^ flip) for i in range(lax.axis_size(axis))])


def partner(index, which, count):
    return index ^ 1 if which == 0 else (index + 2 * (index % 2) - 1) % count


def swap_side(value, axis, which):
    count = lax.axis_size(axis)
    return lax.ppermute(value, axis, [(i, partner(i, which, count)) for i in range(count)])


def swap_corner(value, which_x, which_y):
    size_x, size_y = lax.axis_size("gx"), lax.axis_size("gy")
    pairs = [
        (i * size_y + j, partner(i, which_x, size_x) * size_y + partner(j, which_y, size_y))
        for i in range(size_x)
        for j in range(size_y)
    ]
    return lax.ppermute(value, ("gx", "gy"), pairs)


together = lax.optimization_barrier
A_FIRST, A_SECOND = 1, 3
B_FIRST, B_SECOND = 3, 1
ORDER_A = (0, A_SECOND, A_FIRST, 2)
ORDER_B = (0, B_SECOND, B_FIRST, 2)


def swap_y(value, flip):
    return swap(value, "gy", 2 * flip)


def wide(value):
    return value.astype(F32)


def body(skip_feat, cotangent, w_coarse, w_dec):
    w_join = w_dec.transpose(1, 0, 2).reshape(JOINED, DEC)
    w_pre = w_coarse.transpose(2, 0, 1).reshape(COARSE, DEC)
    w_back = w_coarse.reshape(9, 3, SKIP, COARSE).transpose(0, 2, 1, 3).reshape(9 * SKIP, 3 * COARSE)

    block = (SKIP, LANES)
    face, face_y, corner = (FACE,) + block, (FACE_Y,) + block, (2,) + block
    fine = (BLOCKS,) + block
    skip, cot, pooled, *faces = call(
        split_kernel, "split_blocks",
        (
            (fine, BF16), (fine, BF16), ((BLOCKS_C,) + block, BF16),
            (face, BF16), (face, BF16), (face_y, BF16), (face_y, BF16),
            (corner, BF16), (corner, BF16), (corner, BF16), (corner, BF16),
        ),
        (
            (skip_feat.shape, BF16), (skip_feat.shape, BF16), ((SKIP * BLOCKS, LANES), F32),
            pltpu.SemaphoreType.DMA((2,)),
        ),
        8, (1_000_000, 1_500_000), *(pltpu.with_memory_space_constraint(x, pltpu.HBM) for x in (skip_feat, cotangent)),
        held=pltpu.HBM,
    )
    xtwo = swap_side(faces[1], "gx", 1)
    corners = [swap_corner(faces[4 + 2 * i + j], i, j) for i, j in ((0, 0), (0, 1), (1, 0), (1, 1))]
    xone = swap_side(faces[0], "gx", 0)
    yone, ytwo = (swap_side(faces[2 + which], "gy", which) for which in range(2))
    chunks = (4, 4, ROWS, LANES)
    send, keep, jskip, own, rtwo = call(
        grads_kernel, "local_grads",
        (
            ((SENT + 2 * SKIP, LANES), BF16), (chunks, F32), (fine, F32),
            ((3 * BLOCKS_C,) + block, F32), (corner, BF16),
        ),
        (
            ((DEC, BLOCKS * LANES), BF16),
            ((DEC, BLOCKS_C * LANES), BF16),
            ((JOINED, BLOCKS * LANES), BF16),
            ((JOINED, BLOCKS * LANES), F32),
            ((CHUNKS * ROWS, LANES), F32),
            ((3 * COARSE, BLOCKS_C * LANES), BF16),
        ),
        36, (3_000_000_000, 8_000_000), skip, cot, pooled, xone, xtwo, yone, ytwo, *corners,
        w_join, w_pre, w_back,
    )

    send, rtwo = swap(send, "gy", 1), swap_side(rtwo, "gy", 1)
    part = keep + wide(send[:SENT].reshape(chunks))
    rone = send[SENT:].reshape(corner)
    a, b = part[:, :2], part[:, 2:]
    a_got = swap_y(jnp.stack([a[A_FIRST], a[2]]).astype(BF16), A_FIRST)
    b_got = swap_y(jnp.stack([b[B_FIRST], b[2]]).astype(BF16), B_FIRST)
    a_got, b_got, rone, rtwo = together((a_got, b_got, rone, rtwo))
    rows, qone, qtwo = call(
        fold_kernel, "fold_rim", (((BLOCKS_C,) + block, F32), (corner, BF16), (corner, BF16)), (), 8, (100_000, 600_000),
        own, rone, rtwo,
    )
    a_own, a_leave = a[0] + wide(a_got[0]), a[A_SECOND] + wide(a_got[1])
    b_own, b_leave = b[0] + wide(b_got[0]), b[B_SECOND] + wide(b_got[1])
    a_got, b_got = swap_y(a_leave.astype(BF16), A_SECOND), swap_y(b_leave.astype(BF16), B_SECOND)
    a_got, b_got, rows, qone, qtwo = together((a_got, b_got, rows, qone, qtwo))
    part = jnp.concatenate([a_own + wide(a_got), b_own + wide(b_got)])
    leave = part.astype(BF16)
    qtwo = swap_side(qtwo, "gx", 1)
    got = swap(jnp.concatenate([leave[1], qone.reshape(2 * SKIP, LANES)]), "gx", 1)
    got = [got[:ROWS], swap(leave[2], "gx", 2), swap(leave[3], "gx", 3), got[ROWS:].reshape(corner)]
    *got, qone, qtwo = together((*got, qtwo))
    (skip_grad,) = call(
        skip_kernel, "skip_gradient", (((SKIP, SIZE_X, SIZE_Y, LANES), BF16),), (((SKIP * BLOCKS, LANES), F32),),
        8, (1_000_000, 1_000_000), rows, qone, qtwo, jskip,
    )
    part = (part[0] + wide(got[0])) + (wide(got[1]) + wide(got[2]))
    mine = part.astype(BF16)
    got = [swap(mine, "gx", 4 * flip) for flip in (1, 2, 3)]
    *got, skip_grad = together((*got, skip_grad))
    part = (wide(mine) + wide(got[0])) + (wide(got[1]) + wide(got[2]))
    part = (part + swap(part, "gy", 8)).astype(BF16)
    part = jnp.stack(together([part] + [swap(part, "gx", flip) for flip in (1, 2, 3)]))
    a, b = part[:2], part[2:]
    a_got, b_got = together((swap_y(a, A_SECOND), swap_y(b, B_SECOND)))
    a_near, b_near = jnp.stack([a, a_got]), jnp.stack([b, b_got])
    a_far, b_far = together((swap_y(a_near, A_FIRST), swap_y(b_near, B_FIRST)))
    other = swap(jnp.concatenate([a_near, a_far, b_near, b_far]), "gy", 1)
    dec, coarse = call(
        unpack_kernel, "unpack", (((DEC, JOINED), F32), ((DEC, COARSE), F32)), (((CHUNKS * ROWS, LANES), F32),),
        16, (1_000_000, 5_000_000), a_near, a_far, b_near, b_far, other,
    )
    return (
        skip_grad,
        dec.reshape(TAPS, SKIP, JOINED).transpose(0, 2, 1),
        coarse.reshape(TAPS, SKIP, COARSE),
    )


def solution(mesh):
    placed = (P(None, "gx", "gy", None), P(None, "gx", "gy", None), P(), P())
    return jax.shard_map(
        body,
        mesh=mesh,
        in_specs=placed,
        out_specs=(P(None, "gx", "gy", None), P(), P()),
        check_vma=False,
    )
```

```python
import functools
import math

import jax
import jax.numpy as jnp
from jax import lax
from jax.experimental import pallas as pl
from jax.experimental.pallas import tpu as pltpu
from jax.sharding import PartitionSpec as P

LANES = 128
SKIP, COARSE, JOINED = 64, 128, 192
SIZE_X, SIZE_Y = 2, 8
BLOCKS, BLOCKS_C = SIZE_X * SIZE_Y, SIZE_Y // 2
TAPS = 27
DEC = TAPS * SKIP
PACKED = DEC + DEC // 2 + DEC
ROWS = 136
CHUNKS = 32
SENT = CHUNKS // 2 * ROWS
FACE, FACE_Y = SIZE_Y + BLOCKS_C // 2, SIZE_X + 2 + 2
BF16, F32 = jnp.bfloat16, jnp.float32


def params(mib):
    return pltpu.CompilerParams(vmem_limit_bytes=mib << 20)


def lane_of(shape):
    return lax.broadcasted_iota(jnp.int32, shape, len(shape) - 1)


def is_even(value):
    return (lane_of(value.shape) & 1) == 0


def paired(value):
    return value + jnp.where(is_even(value), pltpu.roll(value, LANES - 1, 1), pltpu.roll(value, 1, 1))


def pack(first, second):
    return jnp.where(is_even(first), first, second)


def unpack_pair(value):
    even = is_even(value)
    return (
        jnp.where(even, value, pltpu.roll(value, 1, 1)),
        jnp.where(even, pltpu.roll(value, LANES - 1, 1), value),
    )


def shifted(value, step):
    if step == 0:
        return value
    lane = lane_of(value.shape)
    inside = lane < LANES - step if step > 0 else lane >= -step
    return jnp.where(inside, pltpu.roll(value, (-step) % LANES, 1), 0.0)


def places():
    return lax.axis_index("gx"), lax.axis_index("gy")


def sides(place):
    odd = (place & 1).astype(F32)
    inner = jnp.where((place == 0) | (place == 15), 0.0, 1.0).astype(F32)
    return (odd, (1.0 - odd) * inner), (1.0 - odd, odd * inner)


def mixed(weights, first, second):
    return weights[0] * first.astype(F32) + weights[1] * second.astype(F32)


def split_kernel(skip_hbm, cot_hbm, skip_out, cot_out, pool_out, two_out, one_out, skip_ref, cot_ref, rows_ref, arrived):
    odd = places()[0] & 1
    copies = [
        pltpu.make_async_copy(source, target, arrived.at[index])
        for index, (source, target) in enumerate(((cot_hbm, cot_ref), (skip_hbm, skip_ref)))
    ]
    for copy in copies:
        copy.start()

    def block_of(index):
        return rows_ref[pl.ds(index, SKIP, stride=BLOCKS), :]

    copies[0].wait()
    rows_ref[...] = cot_ref[...].astype(F32).reshape(SKIP * BLOCKS, LANES)
    for index in range(BLOCKS):
        cot_out[index] = block_of(index).astype(BF16)
    for row in range(SIZE_Y):
        one_out[row] = cot_out[(1 - odd) * SIZE_Y + row]
        two_out[row] = cot_out[odd * SIZE_Y + row]
    copies[1].wait()
    rows_ref[...] = skip_ref[...].astype(F32).reshape(SKIP * BLOCKS, LANES)
    pools = []
    for coarse in range(BLOCKS_C):
        total = None
        for index in (2 * coarse, 2 * coarse + 1, SIZE_Y + 2 * coarse, SIZE_Y + 2 * coarse + 1):
            block = block_of(index)
            skip_out[index] = block.astype(BF16)
            total = block if total is None else total + block
        pools.append(paired(total) * 0.125)
        pool_out[coarse] = pools[-1].astype(BF16)
    for index in range(BLOCKS_C // 2):
        packed = pack(pools[2 * index], pools[2 * index + 1]).astype(BF16)
        one_out[SIZE_Y + index] = packed
        two_out[SIZE_Y + index] = packed


def vmem():
    return pl.BlockSpec(memory_space=pltpu.VMEM)


def call(kernel, name, outs, scratch, mib, cost, *operands, held=()):
    return pl.pallas_call(
        kernel,
        out_shape=tuple(jax.ShapeDtypeStruct(shape, dtype) for shape, dtype in outs),
        in_specs=[pl.BlockSpec(memory_space=space) for space in held or (pltpu.VMEM,) * len(operands)],
        out_specs=tuple(vmem() for _ in outs),
        scratch_shapes=[pltpu.VMEM(*form) if isinstance(form, tuple) else form for form in scratch],
        compiler_params=params(mib),
        cost_estimate=pl.CostEstimate(flops=cost[0], bytes_accessed=cost[1], transcendentals=0),
        name=name,
    )(*operands)


def faces_kernel(cot_ref, pool_ref, xtwo_ref, xone_ref, *refs):
    one_out, two_out = refs[-2:]
    place = places()
    low, high = sides(place[0])
    odd = place[1] & 1
    for out, up in ((one_out, 1 - odd), (two_out, odd)):
        row = up * (SIZE_Y - 1)
        out[0] = mixed(low, xone_ref[row], xtwo_ref[row]).astype(BF16)
        out[1] = cot_ref[row]
        out[2] = cot_ref[SIZE_Y + row]
        out[3] = mixed(high, xone_ref[row], xtwo_ref[row]).astype(BF16)
        pair = SIZE_Y + up * (BLOCKS_C // 2 - 1)
        upper = up.astype(F32)

        def pooled_of(weights):
            first, second = unpack_pair(mixed(weights, xone_ref[pair], xtwo_ref[pair]))
            return (1.0 - upper) * first + upper * second

        out[4] = pack(pooled_of(low), pool_ref[up * (BLOCKS_C - 1)].astype(F32)).astype(BF16)
        out[5] = pooled_of(high).astype(BF16)


def row_of(place, core, yp, xp):
    def ring(own, position):
        return own ^ (0, 1 + 2 * core, 3 - 2 * core, 2)[position]

    at = 16 * core + 4 * ring((place[1] >> 1) & 3, yp) + ring(place[0] & 3, xp)
    return pl.multiple_of(at * ROWS, ROWS)


def grads_kernel(
    skip_ref, cot_ref, pool_ref, xtwo_ref, xone_ref, ytwo_ref, yone_ref, *refs,
):
    wdec_ref, wpre_ref, wback_ref = refs[:3]
    send_out, keep_out, jskip_out, rim_out, two_out = refs[3:8]
    cells_ref, pooled_ref, joined_ref, jgrad_ref, full_ref, pre_ref = refs[8:]
    factor = 1.0 / math.sqrt(524288)
    place = places()
    xlow, xhigh = sides(place[0])
    ylow, yhigh = sides(place[1])

    def fine(plane, row):
        if row == 0:
            return mixed(ylow, yone_ref[plane], ytwo_ref[plane])
        if row == SIZE_Y + 1:
            return mixed(yhigh, yone_ref[plane], ytwo_ref[plane])
        if plane == 0:
            return mixed(xlow, xone_ref[row - 1], xtwo_ref[row - 1])
        if plane == SIZE_X + 1:
            return mixed(xhigh, xone_ref[row - 1], xtwo_ref[row - 1])
        return cot_ref[(plane - 1) * SIZE_Y + row - 1].astype(F32)

    wide_pool = {}
    for row, weights in ((0, ylow), (BLOCKS_C + 1, yhigh)):
        wide_pool[0, row], wide_pool[1, row] = unpack_pair(mixed(weights, yone_ref[4], ytwo_ref[4]))
        wide_pool[2, row] = mixed(weights, yone_ref[5], ytwo_ref[5])
    for plane, weights in ((0, xlow), (2, xhigh)):
        for index in range(BLOCKS_C // 2):
            at = SIZE_Y + index
            first, second = unpack_pair(mixed(weights, xone_ref[at], xtwo_ref[at]))
            wide_pool[plane, 2 * index + 1], wide_pool[plane, 2 * index + 2] = first, second
    for row in range(BLOCKS_C):
        wide_pool[1, row + 1] = pool_ref[row].astype(F32)

    for plane in range(3):
        for row in range(BLOCKS_C + 2):
            for k in range(3):
                value = shifted(wide_pool[plane, row], 2 * (k - 1)).astype(BF16)
                for j in range(3):
                    if 0 <= row - j < BLOCKS_C:
                        tap = 9 * plane + 3 * j + k
                        pooled_ref[tap * SKIP : (tap + 1) * SKIP, (row - j) * LANES : (row - j + 1) * LANES] = value
    pre_b = jnp.dot(wpre_ref[...], pooled_ref[...], preferred_element_type=F32)
    sig = 1.0 / (1.0 + jnp.exp(-pre_b))
    coarse_out = (pre_b * sig).astype(BF16)
    slope = sig * (1.0 + pre_b * (1.0 - sig))
    for index in range(BLOCKS):
        at = (index % SIZE_Y) // 2
        joined_ref[:COARSE, index * LANES : (index + 1) * LANES] = coarse_out[:, at * LANES : (at + 1) * LANES]
        joined_ref[COARSE:, index * LANES : (index + 1) * LANES] = skip_ref[index]
    for plane in range(SIZE_X + 2):
        for row in range(SIZE_Y + 2):
            wide = fine(plane, row)
            for k in range(3):
                value = shifted(wide, 1 - k).astype(BF16)
                for i in range(3):
                    for j in range(3):
                        x, y = plane - 2 + i, row - 2 + j
                        if 0 <= x < SIZE_X and 0 <= y < SIZE_Y:
                            tap, at = 9 * i + 3 * j + k, x * SIZE_Y + y
                            cells_ref[tap * SKIP : (tap + 1) * SKIP, at * LANES : (at + 1) * LANES] = value
    jgrad_ref[...] = jnp.dot(wdec_ref[...], cells_ref[...], preferred_element_type=F32)
    for index in range(BLOCKS):
        jskip_out[index] = jgrad_ref[COARSE:, index * LANES : (index + 1) * LANES]
    pre_parts = []
    for at in range(BLOCKS_C):
        total = None
        for index in (2 * at, 2 * at + 1, SIZE_Y + 2 * at, SIZE_Y + 2 * at + 1):
            part = jgrad_ref[:COARSE, index * LANES : (index + 1) * LANES]
            total = part if total is None else total + part
        pre_part = (paired(total) * slope[:, at * LANES : (at + 1) * LANES]).astype(BF16)
        pre_parts.append(pre_part)
        wide = pre_part.astype(F32)
        for k in range(3):
            pre_ref[k * COARSE : (k + 1) * COARSE, at * LANES : (at + 1) * LANES] = shifted(wide, 2 * (1 - k)).astype(BF16)
    pre_grad = jnp.concatenate(pre_parts, axis=1)

    terms = jnp.dot(wback_ref[...], pre_ref[...], preferred_element_type=F32) * 0.125

    def rim_row(i, row):
        total = None
        for j in range(3):
            if 0 <= row - j < BLOCKS_C:
                first = (3 * i + j) * SKIP
                part = terms[first : first + SKIP, (row - j) * LANES : (row - j + 1) * LANES]
                total = part if total is None else total + part
        return total

    for i in range(3):
        for row in range(BLOCKS_C):
            rim_out[BLOCKS_C * i + row] = rim_row(i, row + 1)
    odd = (place[1] & 1).astype(F32)
    for index in range(2):
        down, up = (
            pack(rim_row(0, row), rim_row(1, row)) if index == 0 else rim_row(2, row) for row in (0, BLOCKS_C + 1)
        )
        send_out[SENT + index * SKIP : SENT + (index + 1) * SKIP] = ((1.0 - odd) * up + odd * down).astype(BF16)
        two_out[index] = ((1.0 - odd) * down + odd * up).astype(BF16)

    across = (((1,), (1,)), ((), ()))
    dec = lax.dot_general(cells_ref[...], joined_ref[...], across, preferred_element_type=F32) * factor
    full_ref[:DEC] = dec[:, :LANES]
    full_ref[DEC : DEC + DEC // 2] = jnp.concatenate([dec[: DEC // 2, LANES:], dec[DEC // 2 :, LANES:]], axis=1)
    full_ref[DEC + DEC // 2 : PACKED] = lax.dot_general(
        pooled_ref[...], pre_grad, across, preferred_element_type=F32
    ) * (0.5 * factor)
    full_ref[PACKED:] = jnp.zeros((CHUNKS * ROWS - PACKED, LANES), F32)
    core = place[1] & 1
    for yp in range(4):
        leave = []
        for xp in range(4):
            keep_out[yp, xp] = full_ref[pl.ds(row_of(place, core, yp, xp), ROWS), :]
            leave.append(full_ref[pl.ds(row_of(place, 1 - core, yp, xp), ROWS), :])
        send_out[4 * yp * ROWS : 4 * (yp + 1) * ROWS] = jnp.concatenate(leave).astype(BF16)


def fold_kernel(rim_ref, yone_ref, ytwo_ref, rows_out, one_out, two_out):
    place = places()
    planes = [[rim_ref[BLOCKS_C * i + row] for row in range(BLOCKS_C)] for i in range(3)]
    for weights, row in zip(sides(place[1]), (0, BLOCKS_C - 1)):
        first, second = unpack_pair(mixed(weights, yone_ref[0], ytwo_ref[0]))
        third = mixed(weights, yone_ref[1], ytwo_ref[1])
        for i, terms in enumerate((first, second, third)):
            planes[i][row] = planes[i][row] + terms
    for row in range(BLOCKS_C):
        rows_out[row] = planes[1][row]
    odd = (place[0] & 1).astype(F32)
    for index in range(BLOCKS_C // 2):
        down, up = (pack(planes[i][2 * index], planes[i][2 * index + 1]) for i in (0, 2))
        one_out[index] = ((1.0 - odd) * up + odd * down).astype(BF16)
        two_out[index] = ((1.0 - odd) * down + odd * up).astype(BF16)


def skip_kernel(rows_ref, one0_ref, one1_ref, xtwo_ref, jskip_ref, out_ref, cells_ref):
    place = places()
    low, high = sides(place[0])
    core = (place[1] & 1).astype(F32)
    for pair in range(BLOCKS_C // 2):
        one = mixed((1.0 - core, core), one0_ref[pair], one1_ref[pair])
        terms_of = unpack_pair(mixed((low[0] + high[0], low[1] + high[1]), one, xtwo_ref[pair]))
        for at, terms in zip((2 * pair, 2 * pair + 1), terms_of):
            total = rows_ref[at] + terms
            for index in (2 * at, 2 * at + 1, SIZE_Y + 2 * at, SIZE_Y + 2 * at + 1):
                cells_ref[pl.ds(index, SKIP, stride=BLOCKS), :] = jskip_ref[index] + total
    out_ref[...] = cells_ref[...].reshape(SKIP, SIZE_X, SIZE_Y, LANES).astype(BF16)


def unpack_kernel(near_ref, far_ref, other_ref, dec_out, coarse_out, full_ref):
    place = places()
    core = place[1] & 1
    for yp in range(4):
        for xp in range(4):
            own = near_ref[yp, xp] if yp < 2 else far_ref[yp - 2, xp]
            full_ref[pl.ds(row_of(place, core, yp, xp), ROWS), :] = own.astype(F32)
            full_ref[pl.ds(row_of(place, 1 - core, yp, xp), ROWS), :] = other_ref[yp, xp].astype(F32)
    half = LANES // 2
    dec_out[:, :LANES] = full_ref[:DEC]
    dec_out[: DEC // 2, LANES:] = full_ref[DEC : DEC + DEC // 2, :half]
    dec_out[DEC // 2 :, LANES:] = full_ref[DEC : DEC + DEC // 2, half:]
    coarse_out[...] = full_ref[DEC + DEC // 2 : PACKED]


def swap(value, axis, flip):
    return lax.ppermute(value, axis, [(i, i ^ flip) for i in range(lax.axis_size(axis))])


def partner(index, which, count):
    return index ^ 1 if which == 0 else (index + 2 * (index % 2) - 1) % count


def swap_side(value, axis, which):
    count = lax.axis_size(axis)
    return lax.ppermute(value, axis, [(i, partner(i, which, count)) for i in range(count)])


together = lax.optimization_barrier


FIRST, SECOND = (3, 1), (1, 3)


def swap_round(value, flips):
    size_x, size_y = lax.axis_size("gx"), lax.axis_size("gy")
    pairs = [
        (i * size_y + j, (i ^ flips[j % 2][0]) * size_y + (j ^ flips[j % 2][1]))
        for i in range(size_x)
        for j in range(size_y)
    ]
    return lax.ppermute(value, ("gx", "gy"), pairs)


def along_y(value, flips):
    return swap_round(value, [(0, 2 * flip) for flip in flips])


def along_x(value, flips):
    return swap_round(value, [(flip, 0) for flip in flips])


Z_ROUNDS = [((4, 0), (0, 8)), ((12, 0), (4, 0)), ((0, 8), (12, 0))]


def wide(value):
    return value.astype(F32)


def body(skip_feat, cotangent, w_coarse, w_dec):
    w_join = w_dec.transpose(1, 0, 2).reshape(JOINED, DEC)
    w_pre = w_coarse.transpose(2, 0, 1).reshape(COARSE, DEC)
    w_back = w_coarse.reshape(9, 3, SKIP, COARSE).transpose(0, 2, 1, 3).reshape(9 * SKIP, 3 * COARSE)

    block = (SKIP, LANES)
    face, face_y, corner = (FACE,) + block, (FACE_Y,) + block, (2,) + block
    fine = (BLOCKS,) + block
    skip, cot, pooled, xtwo, xone = call(
        split_kernel, "split_blocks",
        ((fine, BF16), (fine, BF16), ((BLOCKS_C,) + block, BF16), (face, BF16), (face, BF16)),
        (
            (skip_feat.shape, BF16), (skip_feat.shape, BF16), ((SKIP * BLOCKS, LANES), F32),
            pltpu.SemaphoreType.DMA((2,)),
        ),
        8, (1_000_000, 1_500_000), *(pltpu.with_memory_space_constraint(x, pltpu.HBM) for x in (skip_feat, cotangent)),
        held=(pltpu.HBM,) * 2,
    )
    xtwo, xone = swap_side(xtwo, "gx", 1), swap_side(xone, "gx", 0)
    yone, ytwo = call(
        faces_kernel, "row_faces", ((face_y, BF16), (face_y, BF16)), (), 8, (100_000, 400_000),
        cot, pooled, xtwo, xone, w_join, w_pre, w_back, held=(pltpu.VMEM,) * 4 + (pl.ANY,) * 3,
    )
    yone, ytwo = swap_side(yone, "gy", 0), swap_side(ytwo, "gy", 1)
    chunks = (4, 4, ROWS, LANES)
    send, keep, jskip, own, rtwo = call(
        grads_kernel, "local_grads",
        (
            ((SENT + 2 * SKIP, LANES), BF16), (chunks, F32), (fine, F32),
            ((3 * BLOCKS_C,) + block, F32), (corner, BF16),
        ),
        (
            ((DEC, BLOCKS * LANES), BF16),
            ((DEC, BLOCKS_C * LANES), BF16),
            ((JOINED, BLOCKS * LANES), BF16),
            ((JOINED, BLOCKS * LANES), F32),
            ((CHUNKS * ROWS, LANES), F32),
            ((3 * COARSE, BLOCKS_C * LANES), BF16),
        ),
        36, (3_000_000_000, 8_000_000), skip, cot, pooled, xtwo, xone, ytwo, yone,
        w_join, w_pre, w_back,
    )

    send, rtwo = swap(send, "gy", 1), swap_side(rtwo, "gy", 1)
    part = keep + wide(send[:SENT].reshape(chunks))
    part = part[:2] + wide(along_y(part[2:].astype(BF16), FIRST))
    part = part[0] + wide(along_y(part[1].astype(BF16), SECOND))
    part = part[:2] + wide(along_x(part[2:].astype(BF16), FIRST))
    got, rone, rtwo = together((along_x(part[1].astype(BF16), SECOND), send[SENT:].reshape(corner), rtwo))
    part = part[0] + wide(got)
    part = part.astype(BF16)
    for flips in Z_ROUNDS:
        part = wide(part) + wide(swap_round(part, flips))
    part = part.astype(BF16)
    rows, qone, qtwo = call(
        fold_kernel, "fold_rim", (((BLOCKS_C,) + block, F32), (corner, BF16), (corner, BF16)), (), 8, (100_000, 600_000),
        own, rone, rtwo,
    )
    part, rows, qone, qtwo = together((part, rows, qone, qtwo))
    rim = qone.reshape(2 * SKIP, LANES)
    got = along_x(jnp.concatenate([part, rim]), SECOND)
    part = jnp.stack([part, got[:ROWS]])
    qone1 = got[ROWS:].reshape(corner)
    got = along_x(jnp.concatenate([part.reshape(2 * ROWS, LANES), rim]), FIRST)
    part = jnp.concatenate([part, got[: 2 * ROWS].reshape(2, ROWS, LANES)])
    qone2 = got[2 * ROWS :].reshape(corner)
    near = jnp.stack([part, along_y(part, SECOND)])
    far, qtwo = together((along_y(near, FIRST), swap_side(qtwo, "gx", 1)))
    other = swap(jnp.concatenate([near, far]), "gy", 1)
    (skip_grad,) = call(
        skip_kernel, "skip_gradient", (((SKIP, SIZE_X, SIZE_Y, LANES), BF16),), (((SKIP * BLOCKS, LANES), F32),),
        8, (1_000_000, 1_000_000), rows, qone1, qone2, qtwo, jskip,
    )
    dec, coarse = call(
        unpack_kernel, "unpack", (((DEC, JOINED), F32), ((DEC, COARSE), F32)), (((CHUNKS * ROWS, LANES), F32),),
        16, (1_000_000, 5_000_000), near, far, other,
    )
    return (
        skip_grad,
        dec.reshape(TAPS, SKIP, JOINED).transpose(0, 2, 1),
        coarse.reshape(TAPS, SKIP, COARSE),
    )


def solution(mesh):
    placed = (P(None, "gx", "gy", None), P(None, "gx", "gy", None), P(), P())
    return jax.shard_map(
        body,
        mesh=mesh,
        in_specs=placed,
        out_specs=(P(None, "gx", "gy", None), P(), P()),
        check_vma=False,
    )
```

```python
import functools
import math

import jax
import jax.numpy as jnp
from jax import lax
from jax.experimental import pallas as pl
from jax.experimental.pallas import tpu as pltpu
from jax.sharding import PartitionSpec as P

LANES = 128
SKIP, COARSE, JOINED = 64, 128, 192
SIZE_X, SIZE_Y = 2, 8
BLOCKS, BLOCKS_C = SIZE_X * SIZE_Y, SIZE_Y // 2
TAPS = 27
DEC = TAPS * SKIP
PACKED = DEC + DEC // 2 + DEC
ROWS = 136
CHUNKS = 32
SENT = CHUNKS // 2 * ROWS
FACE, FACE_Y = SIZE_Y + BLOCKS_C // 2, SIZE_X + 2 + 2
EDGE = 3
FACE_ROWS = (0, SIZE_Y - 1, None, *range(1, SIZE_Y - 1))
BF16, F32 = jnp.bfloat16, jnp.float32


def params(mib):
    return pltpu.CompilerParams(vmem_limit_bytes=mib << 20)


def lane_of(shape):
    return lax.broadcasted_iota(jnp.int32, shape, len(shape) - 1)


def is_even(value):
    return (lane_of(value.shape) & 1) == 0


def paired(value):
    return value + jnp.where(is_even(value), pltpu.roll(value, LANES - 1, 1), pltpu.roll(value, 1, 1))


def pack(first, second):
    return jnp.where(is_even(first), first, second)


def unpack_pair(value):
    even = is_even(value)
    return (
        jnp.where(even, value, pltpu.roll(value, 1, 1)),
        jnp.where(even, pltpu.roll(value, LANES - 1, 1), value),
    )


def shifted(value, step):
    if step == 0:
        return value
    lane = lane_of(value.shape)
    inside = lane < LANES - step if step > 0 else lane >= -step
    return jnp.where(inside, pltpu.roll(value, (-step) % LANES, 1), 0.0)


def places():
    return lax.axis_index("gx"), lax.axis_index("gy")


def half_of(place):
    gx, gy = place
    return (gy ^ (gy >> 1) ^ (gy >> 3) ^ (gx >> 2)) & 1


def sides(place):
    odd = (place & 1).astype(F32)
    inner = jnp.where((place == 0) | (place == 15), 0.0, 1.0).astype(F32)
    return (odd, (1.0 - odd) * inner), (1.0 - odd, odd * inner)


def mixed(weights, first, second):
    return weights[0] * first.astype(F32) + weights[1] * second.astype(F32)


def split_kernel(skip_hbm, cot_hbm, skip_out, cot_out, pool_out, edge_out, mid_out, one_out, skip_ref, cot_ref, rows_ref, arrived):
    odd = places()[0] & 1
    copies = [
        pltpu.make_async_copy(source, target, arrived.at[index])
        for index, (source, target) in enumerate(((cot_hbm, cot_ref), (skip_hbm, skip_ref)))
    ]
    for copy in copies:
        copy.start()

    def block_of(index):
        return rows_ref[pl.ds(index, SKIP, stride=BLOCKS), :]

    copies[0].wait()
    rows_ref[...] = cot_ref[...].astype(F32).reshape(SKIP * BLOCKS, LANES)
    for index in range(BLOCKS):
        cot_out[index] = block_of(index).astype(BF16)
    for at, row in enumerate(FACE_ROWS):
        if row is not None:
            one_out[at] = cot_out[(1 - odd) * SIZE_Y + row]
            two, two_at = (edge_out, at) if at < EDGE else (mid_out, at - EDGE)
            two[two_at] = cot_out[odd * SIZE_Y + row]
    copies[1].wait()
    rows_ref[...] = skip_ref[...].astype(F32).reshape(SKIP * BLOCKS, LANES)
    pools = []
    for coarse in range(BLOCKS_C):
        total = None
        for index in (2 * coarse, 2 * coarse + 1, SIZE_Y + 2 * coarse, SIZE_Y + 2 * coarse + 1):
            block = block_of(index)
            skip_out[index] = block.astype(BF16)
            total = block if total is None else total + block
        pools.append(paired(total) * 0.125)
        pool_out[coarse] = pools[-1].astype(BF16)
    outer, inner = (pack(pools[i], pools[j]).astype(BF16) for i, j in ((0, 3), (1, 2)))
    one_out[EDGE - 1], edge_out[EDGE - 1] = outer, outer
    one_out[FACE - 1], mid_out[FACE - EDGE - 1] = inner, inner


def vmem():
    return pl.BlockSpec(memory_space=pltpu.VMEM)


def call(kernel, name, outs, scratch, mib, cost, *operands, held=()):
    return pl.pallas_call(
        kernel,
        out_shape=tuple(jax.ShapeDtypeStruct(shape, dtype) for shape, dtype in outs),
        in_specs=[pl.BlockSpec(memory_space=space) for space in held or (pltpu.VMEM,) * len(operands)],
        out_specs=tuple(vmem() for _ in outs),
        scratch_shapes=[pltpu.VMEM(*form) if isinstance(form, tuple) else form for form in scratch],
        compiler_params=params(mib),
        cost_estimate=pl.CostEstimate(flops=cost[0], bytes_accessed=cost[1], transcendentals=0),
        name=name,
    )(*operands)


def weights_kernel(dec_hbm, coarse_hbm, join_out, pre_out, back_out, dec_ref, coarse_ref, arrived):
    copies = [
        pltpu.make_async_copy(source, target, arrived.at[index])
        for index, (source, target) in enumerate(((dec_hbm, dec_ref), (coarse_hbm, coarse_ref)))
    ]
    for copy in copies:
        copy.start()
    copies[0].wait()
    join_out[...] = dec_ref[...].T
    copies[1].wait()
    pre_out[...] = coarse_ref[...].T
    for pair in range(9):
        for k in range(3):
            first = (3 * pair + k) * SKIP
            back_out[pair * SKIP : (pair + 1) * SKIP, k * COARSE : (k + 1) * COARSE] = coarse_ref[first : first + SKIP]


def faces_kernel(cot_ref, pool_ref, xedge_ref, xone_ref, *refs):
    one_out, two_out = refs[-2:]
    place = places()
    low, high = sides(place[0])
    odd = place[1] & 1
    for out, up in ((one_out, 1 - odd), (two_out, odd)):
        row = up * (SIZE_Y - 1)
        out[0] = mixed(low, xone_ref[up], xedge_ref[up]).astype(BF16)
        out[1] = cot_ref[row]
        out[2] = cot_ref[SIZE_Y + row]
        out[3] = mixed(high, xone_ref[up], xedge_ref[up]).astype(BF16)
        upper = up.astype(F32)

        def pooled_of(weights):
            first, second = unpack_pair(mixed(weights, xone_ref[EDGE - 1], xedge_ref[EDGE - 1]))
            return (1.0 - upper) * first + upper * second

        out[4] = pack(pooled_of(low), pool_ref[up * (BLOCKS_C - 1)].astype(F32)).astype(BF16)
        out[5] = pooled_of(high).astype(BF16)


def grads_kernel(
    skip_ref, cot_ref, pool_ref, xedge_ref, xmid_ref, xone_ref, ytwo_ref, yone_ref, *refs,
):
    wdec_ref, wpre_ref, wback_ref = refs[:3]
    send_out, keep_out, jskip_out, rim_out, two_out = refs[3:8]
    cells_ref, pooled_ref, joined_ref, jgrad_ref, full_ref, pre_ref = refs[8:]
    factor = 1.0 / math.sqrt(524288)
    place = places()
    xlow, xhigh = sides(place[0])
    ylow, yhigh = sides(place[1])

    def face(xside, at):
        two = xedge_ref[at] if at < EDGE else xmid_ref[at - EDGE]
        return mixed(xside, xone_ref[at], two)

    def fine(plane, row):
        if row == 0:
            return mixed(ylow, yone_ref[plane], ytwo_ref[plane])
        if row == SIZE_Y + 1:
            return mixed(yhigh, yone_ref[plane], ytwo_ref[plane])
        if plane == 0:
            return face(xlow, FACE_ROWS.index(row - 1))
        if plane == SIZE_X + 1:
            return face(xhigh, FACE_ROWS.index(row - 1))
        return cot_ref[(plane - 1) * SIZE_Y + row - 1].astype(F32)

    wide_pool = {}
    for row, weights in ((0, ylow), (BLOCKS_C + 1, yhigh)):
        wide_pool[0, row], wide_pool[1, row] = unpack_pair(mixed(weights, yone_ref[4], ytwo_ref[4]))
        wide_pool[2, row] = mixed(weights, yone_ref[5], ytwo_ref[5])
    for plane, weights in ((0, xlow), (2, xhigh)):
        wide_pool[plane, 1], wide_pool[plane, 4] = unpack_pair(face(weights, EDGE - 1))
        wide_pool[plane, 2], wide_pool[plane, 3] = unpack_pair(face(weights, FACE - 1))
    for row in range(BLOCKS_C):
        wide_pool[1, row + 1] = pool_ref[row].astype(F32)

    for plane in range(3):
        for row in range(BLOCKS_C + 2):
            for k in range(3):
                value = shifted(wide_pool[plane, row], 2 * (k - 1)).astype(BF16)
                for j in range(3):
                    if 0 <= row - j < BLOCKS_C:
                        tap = 9 * plane + 3 * j + k
                        pooled_ref[tap * SKIP : (tap + 1) * SKIP, (row - j) * LANES : (row - j + 1) * LANES] = value
    pre_b = jnp.dot(wpre_ref[...], pooled_ref[...], preferred_element_type=F32)
    sig = 1.0 / (1.0 + jnp.exp(-pre_b))
    coarse_out = (pre_b * sig).astype(BF16)
    slope = sig * (1.0 + pre_b * (1.0 - sig))
    for index in range(BLOCKS):
        at = (index % SIZE_Y) // 2
        joined_ref[:COARSE, index * LANES : (index + 1) * LANES] = coarse_out[:, at * LANES : (at + 1) * LANES]
        joined_ref[COARSE:, index * LANES : (index + 1) * LANES] = skip_ref[index]
    for plane in range(SIZE_X + 2):
        for row in range(SIZE_Y + 2):
            wide = fine(plane, row)
            for k in range(3):
                value = shifted(wide, 1 - k).astype(BF16)
                for i in range(3):
                    for j in range(3):
                        x, y = plane - 2 + i, row - 2 + j
                        if 0 <= x < SIZE_X and 0 <= y < SIZE_Y:
                            tap, at = 9 * i + 3 * j + k, x * SIZE_Y + y
                            cells_ref[tap * SKIP : (tap + 1) * SKIP, at * LANES : (at + 1) * LANES] = value
    jgrad_ref[...] = jnp.dot(wdec_ref[...], cells_ref[...], preferred_element_type=F32)
    for index in range(BLOCKS):
        jskip_out[index] = jgrad_ref[COARSE:, index * LANES : (index + 1) * LANES]
    pre_parts = []
    for at in range(BLOCKS_C):
        total = None
        for index in (2 * at, 2 * at + 1, SIZE_Y + 2 * at, SIZE_Y + 2 * at + 1):
            part = jgrad_ref[:COARSE, index * LANES : (index + 1) * LANES]
            total = part if total is None else total + part
        pre_part = (paired(total) * slope[:, at * LANES : (at + 1) * LANES]).astype(BF16)
        pre_parts.append(pre_part)
        wide = pre_part.astype(F32)
        for k in range(3):
            pre_ref[k * COARSE : (k + 1) * COARSE, at * LANES : (at + 1) * LANES] = shifted(wide, 2 * (1 - k)).astype(BF16)
    pre_grad = jnp.concatenate(pre_parts, axis=1)

    terms = jnp.dot(wback_ref[...], pre_ref[...], preferred_element_type=F32) * 0.125

    def rim_row(i, row):
        total = None
        for j in range(3):
            if 0 <= row - j < BLOCKS_C:
                first = (3 * i + j) * SKIP
                part = terms[first : first + SKIP, (row - j) * LANES : (row - j + 1) * LANES]
                total = part if total is None else total + part
        return total

    for i in range(3):
        for row in range(BLOCKS_C):
            rim_out[BLOCKS_C * i + row] = rim_row(i, row + 1)
    odd = (place[1] & 1).astype(F32)
    for index in range(2):
        down, up = (
            pack(rim_row(0, row), rim_row(1, row)) if index == 0 else rim_row(2, row) for row in (0, BLOCKS_C + 1)
        )
        send_out[SENT + index * SKIP : SENT + (index + 1) * SKIP] = ((1.0 - odd) * up + odd * down).astype(BF16)
        two_out[index] = ((1.0 - odd) * down + odd * up).astype(BF16)

    across = (((1,), (1,)), ((), ()))
    dec = lax.dot_general(cells_ref[...], joined_ref[...], across, preferred_element_type=F32) * factor
    full_ref[:DEC] = dec[:, :LANES]
    full_ref[DEC : DEC + DEC // 2] = jnp.concatenate([dec[: DEC // 2, LANES:], dec[DEC // 2 :, LANES:]], axis=1)
    full_ref[DEC + DEC // 2 : PACKED] = lax.dot_general(
        pooled_ref[...], pre_grad, across, preferred_element_type=F32
    ) * (0.5 * factor)
    full_ref[PACKED:] = jnp.zeros((CHUNKS * ROWS - PACKED, LANES), F32)
    half, y, x = half_of(place), (place[1] >> 1) & 3, place[0] & 3
    for yr in range(4):
        leave = []
        for xr in range(4):
            at = (y ^ yr) * 4 + (x ^ xr)
            row = pl.multiple_of((at + 16 * half) * ROWS, ROWS)
            keep_out[yr, xr] = full_ref[pl.ds(row, ROWS), :]
            row = pl.multiple_of((at + 16 * (1 - half)) * ROWS, ROWS)
            leave.append(full_ref[pl.ds(row, ROWS), :])
        send_out[4 * yr * ROWS : 4 * (yr + 1) * ROWS] = jnp.concatenate(leave).astype(BF16)


def fold_kernel(rim_ref, yone_ref, ytwo_ref, rows_out, one_out, two_out):
    place = places()
    planes = [[rim_ref[BLOCKS_C * i + row] for row in range(BLOCKS_C)] for i in range(3)]
    for weights, row in zip(sides(place[1]), (0, BLOCKS_C - 1)):
        first, second = unpack_pair(mixed(weights, yone_ref[0], ytwo_ref[0]))
        third = mixed(weights, yone_ref[1], ytwo_ref[1])
        for i, terms in enumerate((first, second, third)):
            planes[i][row] = planes[i][row] + terms
    for row in range(BLOCKS_C):
        rows_out[row] = planes[1][row]
    odd = (place[0] & 1).astype(F32)
    for index in range(BLOCKS_C // 2):
        down, up = (pack(planes[i][2 * index], planes[i][2 * index + 1]) for i in (0, 2))
        one_out[index] = ((1.0 - odd) * up + odd * down).astype(BF16)
        two_out[index] = ((1.0 - odd) * down + odd * up).astype(BF16)


def skip_kernel(rows_ref, xone_ref, xtwo_ref, jskip_ref, out_ref, cells_ref):
    low, high = sides(places()[0])
    weights = (low[0] + high[0], low[1] + high[1])
    for pair in range(BLOCKS_C // 2):
        for at, terms in zip((2 * pair, 2 * pair + 1), unpack_pair(mixed(weights, xone_ref[pair], xtwo_ref[pair]))):
            total = rows_ref[at] + terms
            for index in (2 * at, 2 * at + 1, SIZE_Y + 2 * at, SIZE_Y + 2 * at + 1):
                cells_ref[pl.ds(index, SKIP, stride=BLOCKS), :] = jskip_ref[index] + total
    out_ref[...] = cells_ref[...].reshape(SKIP, SIZE_X, SIZE_Y, LANES).astype(BF16)


def unpack_kernel(a0_ref, a1_ref, b0_ref, b1_ref, core_ref, dec_out, coarse_out, full_ref):
    place = places()
    half, y, x = half_of(place), (place[1] >> 1) & 3, place[0] & 3
    for side, (refs, order) in enumerate((((a0_ref, a1_ref), ORDER_A), ((b0_ref, b1_ref), ORDER_B))):
        for index, yr in enumerate(order):
            for xr in range(2):
                at = (y ^ yr) * 4 + (x ^ (2 * side + xr))
                row = pl.multiple_of((at + 16 * half) * ROWS, ROWS)
                full_ref[pl.ds(row, ROWS), :] = refs[index // 2][index % 2, xr].astype(F32)
                row = pl.multiple_of((at + 16 * (1 - half)) * ROWS, ROWS)
                full_ref[pl.ds(row, ROWS), :] = core_ref[4 * side + index, xr].astype(F32)
    middle = LANES // 2
    dec_out[:, :LANES] = full_ref[:DEC]
    dec_out[: DEC // 2, LANES:] = full_ref[DEC : DEC + DEC // 2, :middle]
    dec_out[DEC // 2 :, LANES:] = full_ref[DEC : DEC + DEC // 2, middle:]
    coarse_out[...] = full_ref[DEC + DEC // 2 : PACKED]


def swap(value, axis, flip):
    return lax.ppermute(value, axis, [(i, i ^ flip) for i in range(lax.axis_size(axis))])


def in_hbm(*operands):
    return [pltpu.with_memory_space_constraint(operand, pltpu.HBM) for operand in operands]


def partner(index, which, count):
    return index ^ 1 if which == 0 else (index + 2 * (index % 2) - 1) % count


def swap_side(value, axis, which):
    count = lax.axis_size(axis)
    return lax.ppermute(value, axis, [(i, partner(i, which, count)) for i in range(count)])


together = lax.optimization_barrier


A_FIRST, A_SECOND = 1, 3
B_FIRST, B_SECOND = 3, 1
ORDER_A = (0, A_SECOND, A_FIRST, 2)
ORDER_B = (0, B_SECOND, B_FIRST, 2)


def swap_y(value, flip):
    return swap(value, "gy", 2 * flip + 1)


def swap_z(value, flip):
    size_x, size_y = lax.axis_size("gx"), lax.axis_size("gy")
    pairs = [(i * size_y + j, (i ^ (4 * flip)) * size_y + (j ^ (flip & 1))) for i in range(size_x) for j in range(size_y)]
    return lax.ppermute(value, ("gx", "gy"), pairs)


def wide(value):
    return value.astype(F32)


def body(skip_feat, cotangent, w_coarse, w_dec):
    w_join, w_pre, w_back = call(
        weights_kernel, "lay_weights",
        (((JOINED, DEC), BF16), ((COARSE, DEC), BF16), ((9 * SKIP, 3 * COARSE), BF16)),
        (((DEC, JOINED), BF16), ((DEC, COARSE), BF16), pltpu.SemaphoreType.DMA((2,))), 16, (1_000_000, 2_500_000),
        *in_hbm(w_dec.transpose(0, 2, 1).reshape(DEC, JOINED), w_coarse.reshape(DEC, COARSE)), held=(pltpu.HBM,) * 2,
    )

    block = (SKIP, LANES)
    face, face_y, corner = (FACE,) + block, (FACE_Y,) + block, (2,) + block
    fine = (BLOCKS,) + block
    skip, cot, pooled, xedge, xmid, xone = call(
        split_kernel, "split_blocks",
        (
            (fine, BF16), (fine, BF16), ((BLOCKS_C,) + block, BF16),
            ((EDGE,) + block, BF16), ((FACE - EDGE,) + block, BF16), (face, BF16),
        ),
        (
            (skip_feat.shape, BF16), (skip_feat.shape, BF16), ((SKIP * BLOCKS, LANES), F32),
            pltpu.SemaphoreType.DMA((2,)),
        ),
        8, (1_000_000, 1_500_000), *in_hbm(skip_feat, cotangent),
        held=(pltpu.HBM,) * 2,
    )
    xedge, xmid, xone = swap_side(xedge, "gx", 1), swap_side(xmid, "gx", 1), swap_side(xone, "gx", 0)
    yone, ytwo = call(
        faces_kernel, "row_faces", ((face_y, BF16), (face_y, BF16)), (), 8, (100_000, 400_000),
        cot, pooled, xedge, xone, w_join, w_pre, w_back, held=(pltpu.VMEM,) * 4 + (pl.ANY,) * 3,
    )
    yone, ytwo = swap_side(yone, "gy", 0), swap_side(ytwo, "gy", 1)
    chunks = (4, 4, ROWS, LANES)
    send, keep, jskip, own, rtwo = call(
        grads_kernel, "local_grads",
        (
            ((SENT + 2 * SKIP, LANES), BF16), (chunks, F32), (fine, F32),
            ((3 * BLOCKS_C,) + block, F32), (corner, BF16),
        ),
        (
            ((DEC, BLOCKS * LANES), BF16),
            ((DEC, BLOCKS_C * LANES), BF16),
            ((JOINED, BLOCKS * LANES), BF16),
            ((JOINED, BLOCKS * LANES), F32),
            ((CHUNKS * ROWS, LANES), F32),
            ((3 * COARSE, BLOCKS_C * LANES), BF16),
        ),
        36, (3_000_000_000, 8_000_000), skip, cot, pooled, xedge, xmid, xone, ytwo, yone,
        w_join, w_pre, w_back,
    )

    send = swap(send, "gy", 1)
    part = keep + wide(send[:SENT].reshape(chunks))
    rone = send[SENT:].reshape(corner)
    a, b = part[:, :2], part[:, 2:]
    a_got = swap_y(jnp.stack([a[A_FIRST], a[2]]).astype(BF16), A_FIRST)
    b_got = swap_y(jnp.stack([b[B_FIRST], b[2]]).astype(BF16), B_FIRST)
    a_got, b_got = together((a_got, b_got))
    a_own, a_leave = a[0] + wide(a_got[0]), a[A_SECOND] + wide(a_got[1])
    b_own, b_leave = b[0] + wide(b_got[0]), b[B_SECOND] + wide(b_got[1])
    a_got, b_got = swap_y(a_leave.astype(BF16), A_SECOND), swap_y(b_leave.astype(BF16), B_SECOND)
    a_got, b_got = together((a_got, b_got))
    part = jnp.concatenate([a_own + wide(a_got), b_own + wide(b_got)])
    leave, rtwo = together((part.astype(BF16), rtwo))
    got = [swap(leave[flip], "gx", flip) for flip in (1, 2, 3)]
    *got, rone, rtwo = together((*got, rone, swap_side(rtwo, "gy", 1)))
    rows, qone, qtwo = call(
        fold_kernel, "fold_rim", (((BLOCKS_C,) + block, F32), (corner, BF16), (corner, BF16)), (), 8, (100_000, 600_000),
        own, rone, rtwo,
    )
    part = (part[0] + wide(got[0])) + (wide(got[1]) + wide(got[2]))
    mine = part.astype(BF16)
    got = [swap_z(mine, flip) for flip in (1, 2, 3)]
    *got, rows, qone, qtwo = together((*got, rows, qone, qtwo))
    part = (wide(mine) + wide(got[0])) + (wide(got[1]) + wide(got[2]))
    part = (part + swap(part, "gy", 9)).astype(BF16)
    got = swap(jnp.concatenate([part, qone.reshape(2 * SKIP, LANES)]), "gx", 1)
    qone = got[ROWS:].reshape(corner)
    part = jnp.stack(together([part, got[:ROWS], swap(part, "gx", 2), swap(part, "gx", 3)]))
    a, b = part[:2], part[2:]
    a_got, b_got = together((swap_y(a, A_SECOND), swap_y(b, B_SECOND)))
    a_near, b_near = jnp.stack([a, a_got]), jnp.stack([b, b_got])
    a_near, b_near, qtwo = together((a_near, b_near, qtwo))
    qtwo = swap_side(qtwo, "gx", 1)
    a_far, b_far, qtwo = together((swap_y(a_near, A_FIRST), swap_y(b_near, B_FIRST), qtwo))
    other = swap(jnp.concatenate([a_near, a_far, b_near, b_far]), "gy", 1)
    (skip_grad,) = call(
        skip_kernel, "skip_gradient", (((SKIP, SIZE_X, SIZE_Y, LANES), BF16),), (((SKIP * BLOCKS, LANES), F32),),
        8, (1_000_000, 1_000_000), rows, qone, qtwo, jskip,
    )
    dec, coarse = call(
        unpack_kernel, "unpack", (((DEC, JOINED), F32), ((DEC, COARSE), F32)), (((CHUNKS * ROWS, LANES), F32),),
        16, (1_000_000, 5_000_000), a_near, a_far, b_near, b_far, other,
    )
    return (
        skip_grad,
        dec.reshape(TAPS, SKIP, JOINED).transpose(0, 2, 1),
        coarse.reshape(TAPS, SKIP, COARSE),
    )


def solution(mesh):
    placed = (P(None, "gx", "gy", None), P(None, "gx", "gy", None), P(), P())
    return jax.shard_map(
        body,
        mesh=mesh,
        in_specs=placed,
        out_specs=(P(None, "gx", "gy", None), P(), P()),
        check_vma=False,
    )
```

```python
import functools
import math

import jax
import jax.numpy as jnp
from jax import lax
from jax.experimental import pallas as pl
from jax.experimental.pallas import tpu as pltpu
from jax.sharding import PartitionSpec as P

LANES = 128
SKIP, COARSE, JOINED = 64, 128, 192
SIZE_X, SIZE_Y = 2, 8
BLOCKS, BLOCKS_C = SIZE_X * SIZE_Y, SIZE_Y // 2
TAPS = 27
DEC = TAPS * SKIP
PACKED = DEC + DEC // 2 + DEC
ROWS = 136
CHUNKS = 32
SENT = CHUNKS // 2 * ROWS
FACE, FACE_Y = SIZE_Y + BLOCKS_C // 2, SIZE_X + 2 + 2
EDGE = 3
FACE_ROWS = (0, SIZE_Y - 1, None, *range(1, SIZE_Y - 1))
BF16, F32 = jnp.bfloat16, jnp.float32


def params(mib):
    return pltpu.CompilerParams(vmem_limit_bytes=mib << 20)


def lane_of(shape):
    return lax.broadcasted_iota(jnp.int32, shape, len(shape) - 1)


def is_even(value):
    return (lane_of(value.shape) & 1) == 0


def paired(value):
    return value + jnp.where(is_even(value), pltpu.roll(value, LANES - 1, 1), pltpu.roll(value, 1, 1))


def pack(first, second):
    return jnp.where(is_even(first), first, second)


def unpack_pair(value):
    even = is_even(value)
    return (
        jnp.where(even, value, pltpu.roll(value, 1, 1)),
        jnp.where(even, pltpu.roll(value, LANES - 1, 1), value),
    )


def shifted(value, step):
    if step == 0:
        return value
    lane = lane_of(value.shape)
    inside = lane < LANES - step if step > 0 else lane >= -step
    return jnp.where(inside, pltpu.roll(value, (-step) % LANES, 1), 0.0)


def places():
    return lax.axis_index("gx"), lax.axis_index("gy")


def half_of(place):
    gx, gy = place
    return (gy ^ (gy >> 1) ^ (gy >> 3) ^ (gx >> 2)) & 1


def sides(place):
    odd = (place & 1).astype(F32)
    inner = jnp.where((place == 0) | (place == 15), 0.0, 1.0).astype(F32)
    return (odd, (1.0 - odd) * inner), (1.0 - odd, odd * inner)


def mixed(weights, first, second):
    return weights[0] * first.astype(F32) + weights[1] * second.astype(F32)


def split_kernel(skip_hbm, cot_hbm, skip_out, cot_out, pool_out, edge_out, mid_out, near_edge_out, near_mid_out, skip_ref, cot_ref, rows_ref, arrived):
    odd = places()[0] & 1
    copies = [
        pltpu.make_async_copy(source, target, arrived.at[index])
        for index, (source, target) in enumerate(((cot_hbm, cot_ref), (skip_hbm, skip_ref)))
    ]
    for copy in copies:
        copy.start()

    def block_of(index):
        return rows_ref[pl.ds(index, SKIP, stride=BLOCKS), :]

    copies[0].wait()
    rows_ref[...] = cot_ref[...].astype(F32).reshape(SKIP * BLOCKS, LANES)
    for index in range(BLOCKS):
        cot_out[index] = block_of(index).astype(BF16)
    for at, row in enumerate(FACE_ROWS):
        if row is not None:
            one, two, piece = (near_edge_out, edge_out, at) if at < EDGE else (near_mid_out, mid_out, at - EDGE)
            one[piece] = cot_out[(1 - odd) * SIZE_Y + row]
            two[piece] = cot_out[odd * SIZE_Y + row]
    copies[1].wait()
    rows_ref[...] = skip_ref[...].astype(F32).reshape(SKIP * BLOCKS, LANES)
    pools = []
    for coarse in range(BLOCKS_C):
        total = None
        for index in (2 * coarse, 2 * coarse + 1, SIZE_Y + 2 * coarse, SIZE_Y + 2 * coarse + 1):
            block = block_of(index)
            skip_out[index] = block.astype(BF16)
            total = block if total is None else total + block
        pools.append(paired(total) * 0.125)
        pool_out[coarse] = pools[-1].astype(BF16)
    outer, inner = (pack(pools[i], pools[j]).astype(BF16) for i, j in ((0, 3), (1, 2)))
    near_edge_out[EDGE - 1], edge_out[EDGE - 1] = outer, outer
    near_mid_out[FACE - EDGE - 1], mid_out[FACE - EDGE - 1] = inner, inner


def vmem():
    return pl.BlockSpec(memory_space=pltpu.VMEM)


def call(kernel, name, outs, scratch, mib, cost, *operands, held=()):
    return pl.pallas_call(
        kernel,
        out_shape=tuple(jax.ShapeDtypeStruct(shape, dtype) for shape, dtype in outs),
        in_specs=[pl.BlockSpec(memory_space=space) for space in held or (pltpu.VMEM,) * len(operands)],
        out_specs=tuple(vmem() for _ in outs),
        scratch_shapes=[pltpu.VMEM(*form) if isinstance(form, tuple) else form for form in scratch],
        compiler_params=params(mib),
        cost_estimate=pl.CostEstimate(flops=cost[0], bytes_accessed=cost[1], transcendentals=0),
        name=name,
    )(*operands)


def weights_kernel(dec_hbm, coarse_hbm, join_out, pre_out, back_out, dec_ref, coarse_ref, arrived):
    copies = [
        pltpu.make_async_copy(source, target, arrived.at[index])
        for index, (source, target) in enumerate(((dec_hbm, dec_ref), (coarse_hbm, coarse_ref)))
    ]
    for copy in copies:
        copy.start()
    copies[0].wait()
    join_out[...] = dec_ref[...].T
    copies[1].wait()
    pre_out[...] = coarse_ref[...].T
    for pair in range(9):
        for k in range(3):
            first = (3 * pair + k) * SKIP
            back_out[pair * SKIP : (pair + 1) * SKIP, k * COARSE : (k + 1) * COARSE] = coarse_ref[first : first + SKIP]


def faces_kernel(cot_ref, pool_ref, xedge_ref, xone_ref, *refs):
    one_out, two_out = refs[-2:]
    place = places()
    low, high = sides(place[0])
    odd = place[1] & 1
    for out, up in ((one_out, 1 - odd), (two_out, odd)):
        row = up * (SIZE_Y - 1)
        out[0] = mixed(low, xone_ref[up], xedge_ref[up]).astype(BF16)
        out[1] = cot_ref[row]
        out[2] = cot_ref[SIZE_Y + row]
        out[3] = mixed(high, xone_ref[up], xedge_ref[up]).astype(BF16)
        upper = up.astype(F32)

        def pooled_of(weights):
            first, second = unpack_pair(mixed(weights, xone_ref[EDGE - 1], xedge_ref[EDGE - 1]))
            return (1.0 - upper) * first + upper * second

        out[4] = pack(pooled_of(low), pool_ref[up * (BLOCKS_C - 1)].astype(F32)).astype(BF16)
        out[5] = pooled_of(high).astype(BF16)


def grads_kernel(
    skip_ref, cot_ref, pool_ref, xedge_ref, xmid_ref, oedge_ref, omid_ref, ytwo_ref, yone_ref, *refs,
):
    wdec_ref, wpre_ref, wback_ref = refs[:3]
    send_out, keep_out, jskip_out, rim_out, two_out = refs[3:8]
    cells_ref, pooled_ref, joined_ref, jgrad_ref, full_ref, pre_ref = refs[8:]
    factor = 1.0 / math.sqrt(524288)
    place = places()
    xlow, xhigh = sides(place[0])
    ylow, yhigh = sides(place[1])

    def face(xside, at):
        if at < EDGE:
            return mixed(xside, oedge_ref[at], xedge_ref[at])
        return mixed(xside, omid_ref[at - EDGE], xmid_ref[at - EDGE])

    def fine(plane, row):
        if row == 0:
            return mixed(ylow, yone_ref[plane], ytwo_ref[plane])
        if row == SIZE_Y + 1:
            return mixed(yhigh, yone_ref[plane], ytwo_ref[plane])
        if plane == 0:
            return face(xlow, FACE_ROWS.index(row - 1))
        if plane == SIZE_X + 1:
            return face(xhigh, FACE_ROWS.index(row - 1))
        return cot_ref[(plane - 1) * SIZE_Y + row - 1].astype(F32)

    wide_pool = {}
    for row, weights in ((0, ylow), (BLOCKS_C + 1, yhigh)):
        wide_pool[0, row], wide_pool[1, row] = unpack_pair(mixed(weights, yone_ref[4], ytwo_ref[4]))
        wide_pool[2, row] = mixed(weights, yone_ref[5], ytwo_ref[5])
    for plane, weights in ((0, xlow), (2, xhigh)):
        wide_pool[plane, 1], wide_pool[plane, 4] = unpack_pair(face(weights, EDGE - 1))
        wide_pool[plane, 2], wide_pool[plane, 3] = unpack_pair(face(weights, FACE - 1))
    for row in range(BLOCKS_C):
        wide_pool[1, row + 1] = pool_ref[row].astype(F32)

    for plane in range(3):
        for row in range(BLOCKS_C + 2):
            for k in range(3):
                value = shifted(wide_pool[plane, row], 2 * (k - 1)).astype(BF16)
                for j in range(3):
                    if 0 <= row - j < BLOCKS_C:
                        tap = 9 * plane + 3 * j + k
                        pooled_ref[tap * SKIP : (tap + 1) * SKIP, (row - j) * LANES : (row - j + 1) * LANES] = value
    pre_b = jnp.dot(wpre_ref[...], pooled_ref[...], preferred_element_type=F32)
    sig = 1.0 / (1.0 + jnp.exp(-pre_b))
    coarse_out = (pre_b * sig).astype(BF16)
    slope = sig * (1.0 + pre_b * (1.0 - sig))
    for index in range(BLOCKS):
        at = (index % SIZE_Y) // 2
        joined_ref[:COARSE, index * LANES : (index + 1) * LANES] = coarse_out[:, at * LANES : (at + 1) * LANES]
        joined_ref[COARSE:, index * LANES : (index + 1) * LANES] = skip_ref[index]
    for plane in range(SIZE_X + 2):
        for row in range(SIZE_Y + 2):
            wide = fine(plane, row)
            for k in range(3):
                value = shifted(wide, 1 - k).astype(BF16)
                for i in range(3):
                    for j in range(3):
                        x, y = plane - 2 + i, row - 2 + j
                        if 0 <= x < SIZE_X and 0 <= y < SIZE_Y:
                            tap, at = 9 * i + 3 * j + k, x * SIZE_Y + y
                            cells_ref[tap * SKIP : (tap + 1) * SKIP, at * LANES : (at + 1) * LANES] = value
    jgrad_ref[...] = jnp.dot(wdec_ref[...], cells_ref[...], preferred_element_type=F32)
    for index in range(BLOCKS):
        jskip_out[index] = jgrad_ref[COARSE:, index * LANES : (index + 1) * LANES]
    pre_parts = []
    for at in range(BLOCKS_C):
        total = None
        for index in (2 * at, 2 * at + 1, SIZE_Y + 2 * at, SIZE_Y + 2 * at + 1):
            part = jgrad_ref[:COARSE, index * LANES : (index + 1) * LANES]
            total = part if total is None else total + part
        pre_part = (paired(total) * slope[:, at * LANES : (at + 1) * LANES]).astype(BF16)
        pre_parts.append(pre_part)
        wide = pre_part.astype(F32)
        for k in range(3):
            pre_ref[k * COARSE : (k + 1) * COARSE, at * LANES : (at + 1) * LANES] = shifted(wide, 2 * (1 - k)).astype(BF16)
    pre_grad = jnp.concatenate(pre_parts, axis=1)

    terms = jnp.dot(wback_ref[...], pre_ref[...], preferred_element_type=F32) * 0.125

    def rim_row(i, row):
        total = None
        for j in range(3):
            if 0 <= row - j < BLOCKS_C:
                first = (3 * i + j) * SKIP
                part = terms[first : first + SKIP, (row - j) * LANES : (row - j + 1) * LANES]
                total = part if total is None else total + part
        return total

    for i in range(3):
        for row in range(BLOCKS_C):
            rim_out[BLOCKS_C * i + row] = rim_row(i, row + 1)
    odd = (place[1] & 1).astype(F32)
    for index in range(2):
        down, up = (
            pack(rim_row(0, row), rim_row(1, row)) if index == 0 else rim_row(2, row) for row in (0, BLOCKS_C + 1)
        )
        send_out[SENT + index * SKIP : SENT + (index + 1) * SKIP] = ((1.0 - odd) * up + odd * down).astype(BF16)
        two_out[index] = ((1.0 - odd) * down + odd * up).astype(BF16)

    across = (((1,), (1,)), ((), ()))
    dec = lax.dot_general(cells_ref[...], joined_ref[...], across, preferred_element_type=F32) * factor
    full_ref[:DEC] = dec[:, :LANES]
    full_ref[DEC : DEC + DEC // 2] = jnp.concatenate([dec[: DEC // 2, LANES:], dec[DEC // 2 :, LANES:]], axis=1)
    full_ref[DEC + DEC // 2 : PACKED] = lax.dot_general(
        pooled_ref[...], pre_grad, across, preferred_element_type=F32
    ) * (0.5 * factor)
    full_ref[PACKED:] = jnp.zeros((CHUNKS * ROWS - PACKED, LANES), F32)
    half, y, x = half_of(place), (place[1] >> 1) & 3, place[0] & 3
    for yr in range(4):
        leave = []
        for xr in range(4):
            at = (y ^ yr) * 4 + (x ^ xr)
            row = pl.multiple_of((at + 16 * half) * ROWS, ROWS)
            keep_out[yr, xr] = full_ref[pl.ds(row, ROWS), :]
            row = pl.multiple_of((at + 16 * (1 - half)) * ROWS, ROWS)
            leave.append(full_ref[pl.ds(row, ROWS), :])
        send_out[4 * yr * ROWS : 4 * (yr + 1) * ROWS] = jnp.concatenate(leave).astype(BF16)


def fold_kernel(rim_ref, yone_ref, ytwo_ref, rows_out, one_out, two_out):
    place = places()
    planes = [[rim_ref[BLOCKS_C * i + row] for row in range(BLOCKS_C)] for i in range(3)]
    for weights, row in zip(sides(place[1]), (0, BLOCKS_C - 1)):
        first, second = unpack_pair(mixed(weights, yone_ref[0], ytwo_ref[0]))
        third = mixed(weights, yone_ref[1], ytwo_ref[1])
        for i, terms in enumerate((first, second, third)):
            planes[i][row] = planes[i][row] + terms
    for row in range(BLOCKS_C):
        rows_out[row] = planes[1][row]
    odd = (place[0] & 1).astype(F32)
    for index in range(BLOCKS_C // 2):
        down, up = (pack(planes[i][2 * index], planes[i][2 * index + 1]) for i in (0, 2))
        one_out[index] = ((1.0 - odd) * up + odd * down).astype(BF16)
        two_out[index] = ((1.0 - odd) * down + odd * up).astype(BF16)


def skip_kernel(rows_ref, xone_ref, xtwo_ref, jskip_ref, out_ref, cells_ref):
    low, high = sides(places()[0])
    weights = (low[0] + high[0], low[1] + high[1])
    for pair in range(BLOCKS_C // 2):
        for at, terms in zip((2 * pair, 2 * pair + 1), unpack_pair(mixed(weights, xone_ref[pair], xtwo_ref[pair]))):
            total = rows_ref[at] + terms
            for index in (2 * at, 2 * at + 1, SIZE_Y + 2 * at, SIZE_Y + 2 * at + 1):
                cells_ref[pl.ds(index, SKIP, stride=BLOCKS), :] = jskip_ref[index] + total
    out_ref[...] = cells_ref[...].reshape(SKIP, SIZE_X, SIZE_Y, LANES).astype(BF16)


def unpack_kernel(a0_ref, a1_ref, b0_ref, b1_ref, core_ref, dec_out, coarse_out, full_ref):
    place = places()
    half, y, x = half_of(place), (place[1] >> 1) & 3, place[0] & 3
    for side, (refs, order) in enumerate((((a0_ref, a1_ref), ORDER_A), ((b0_ref, b1_ref), ORDER_B))):
        for index, yr in enumerate(order):
            for xr in range(2):
                at = (y ^ yr) * 4 + (x ^ (2 * side + xr))
                row = pl.multiple_of((at + 16 * half) * ROWS, ROWS)
                full_ref[pl.ds(row, ROWS), :] = refs[index // 2][index % 2, xr].astype(F32)
                row = pl.multiple_of((at + 16 * (1 - half)) * ROWS, ROWS)
                full_ref[pl.ds(row, ROWS), :] = core_ref[4 * side + index, xr].astype(F32)
    middle = LANES // 2
    dec_out[:, :LANES] = full_ref[:DEC]
    dec_out[: DEC // 2, LANES:] = full_ref[DEC : DEC + DEC // 2, :middle]
    dec_out[DEC // 2 :, LANES:] = full_ref[DEC : DEC + DEC // 2, middle:]
    coarse_out[...] = full_ref[DEC + DEC // 2 : PACKED]


def swap(value, axis, flip):
    return lax.ppermute(value, axis, [(i, i ^ flip) for i in range(lax.axis_size(axis))])


def in_hbm(*operands):
    return [pltpu.with_memory_space_constraint(operand, pltpu.HBM) for operand in operands]


def partner(index, which, count):
    return index ^ 1 if which == 0 else (index + 2 * (index % 2) - 1) % count


def swap_side(value, axis, which):
    count = lax.axis_size(axis)
    return lax.ppermute(value, axis, [(i, partner(i, which, count)) for i in range(count)])


together = lax.optimization_barrier


A_FIRST, A_SECOND = 1, 3
B_FIRST, B_SECOND = 3, 1
ORDER_A = (0, A_SECOND, A_FIRST, 2)
ORDER_B = (0, B_SECOND, B_FIRST, 2)


def swap_y(value, flip):
    return swap(value, "gy", 2 * flip + 1)


def swap_z(value, flip):
    size_x, size_y = lax.axis_size("gx"), lax.axis_size("gy")
    pairs = [(i * size_y + j, (i ^ (4 * flip)) * size_y + (j ^ (flip & 1))) for i in range(size_x) for j in range(size_y)]
    return lax.ppermute(value, ("gx", "gy"), pairs)


def wide(value):
    return value.astype(F32)


def body(skip_feat, cotangent, w_coarse, w_dec):
    w_join, w_pre, w_back = call(
        weights_kernel, "lay_weights",
        (((JOINED, DEC), BF16), ((COARSE, DEC), BF16), ((9 * SKIP, 3 * COARSE), BF16)),
        (((DEC, JOINED), BF16), ((DEC, COARSE), BF16), pltpu.SemaphoreType.DMA((2,))), 16, (1_000_000, 2_500_000),
        *in_hbm(w_dec.transpose(0, 2, 1).reshape(DEC, JOINED), w_coarse.reshape(DEC, COARSE)), held=(pltpu.HBM,) * 2,
    )

    block = (SKIP, LANES)
    face_y, corner = (FACE_Y,) + block, (2,) + block
    fine = (BLOCKS,) + block
    skip, cot, pooled, xedge, xmid, oedge, omid = call(
        split_kernel, "split_blocks",
        (
            (fine, BF16), (fine, BF16), ((BLOCKS_C,) + block, BF16),
            *(((rows,) + block, BF16) for rows in (EDGE, FACE - EDGE, EDGE, FACE - EDGE)),
        ),
        (
            (skip_feat.shape, BF16), (skip_feat.shape, BF16), ((SKIP * BLOCKS, LANES), F32),
            pltpu.SemaphoreType.DMA((2,)),
        ),
        8, (1_000_000, 1_500_000), *in_hbm(skip_feat, cotangent),
        held=(pltpu.HBM,) * 2,
    )
    xedge, xmid = swap_side(xedge, "gx", 1), swap_side(xmid, "gx", 1)
    oedge, omid = swap_side(oedge, "gx", 0), swap_side(omid, "gx", 0)
    yone, ytwo = call(
        faces_kernel, "row_faces", ((face_y, BF16), (face_y, BF16)), (), 8, (100_000, 400_000),
        cot, pooled, xedge, oedge, w_join, w_pre, w_back, held=(pltpu.VMEM,) * 4 + (pl.ANY,) * 3,
    )
    yone, ytwo = swap_side(yone, "gy", 0), swap_side(ytwo, "gy", 1)
    chunks = (4, 4, ROWS, LANES)
    send, keep, jskip, own, rtwo = call(
        grads_kernel, "local_grads",
        (
            ((SENT + 2 * SKIP, LANES), BF16), (chunks, F32), (fine, F32),
            ((3 * BLOCKS_C,) + block, F32), (corner, BF16),
        ),
        (
            ((DEC, BLOCKS * LANES), BF16),
            ((DEC, BLOCKS_C * LANES), BF16),
            ((JOINED, BLOCKS * LANES), BF16),
            ((JOINED, BLOCKS * LANES), F32),
            ((CHUNKS * ROWS, LANES), F32),
            ((3 * COARSE, BLOCKS_C * LANES), BF16),
        ),
        36, (3_000_000_000, 8_000_000), skip, cot, pooled, xedge, xmid, oedge, omid, ytwo, yone,
        w_join, w_pre, w_back,
    )

    send, rtwo = swap(send, "gy", 1), swap_side(rtwo, "gy", 1)
    part = keep + wide(send[:SENT].reshape(chunks))
    rone = send[SENT:].reshape(corner)
    a, b = part[:, :2], part[:, 2:]
    a_got = swap_y(jnp.stack([a[A_FIRST], a[2]]).astype(BF16), A_FIRST)
    b_got = swap_y(jnp.stack([b[B_FIRST], b[2]]).astype(BF16), B_FIRST)
    a_got, b_got, rone, rtwo = together((a_got, b_got, rone, rtwo))
    rows, qone, qtwo = call(
        fold_kernel, "fold_rim", (((BLOCKS_C,) + block, F32), (corner, BF16), (corner, BF16)), (), 8, (100_000, 600_000),
        own, rone, rtwo,
    )
    a_own, a_leave = a[0] + wide(a_got[0]), a[A_SECOND] + wide(a_got[1])
    b_own, b_leave = b[0] + wide(b_got[0]), b[B_SECOND] + wide(b_got[1])
    a_got, b_got = swap_y(a_leave.astype(BF16), A_SECOND), swap_y(b_leave.astype(BF16), B_SECOND)
    a_got, b_got, rows, qone, qtwo = together((a_got, b_got, rows, qone, qtwo))
    part = jnp.concatenate([a_own + wide(a_got), b_own + wide(b_got)])
    leave = part.astype(BF16)
    got = swap(jnp.concatenate([leave[1], qone.reshape(2 * SKIP, LANES)]), "gx", 1)
    got = [got[:ROWS], swap(leave[2], "gx", 2), swap(leave[3], "gx", 3), got[ROWS:].reshape(corner)]
    *got, qone = together(got)
    part = (part[0] + wide(got[0])) + (wide(got[1]) + wide(got[2]))
    mine = part.astype(BF16)
    got = [swap_z(mine, flip) for flip in (1, 2, 3)]
    part = (wide(mine) + wide(got[0])) + (wide(got[1]) + wide(got[2]))
    part = (part + swap(part, "gy", 9)).astype(BF16)
    got = together([swap(part, "gx", flip) for flip in (1, 3, 2)])
    part = jnp.stack([part, got[0], got[2], got[1]])
    a, b = part[:2], part[2:]
    a_got, b_got = together((swap_y(a, A_SECOND), swap_y(b, B_SECOND)))
    a_near, b_near = jnp.stack([a, a_got]), jnp.stack([b, b_got])
    qtwo = swap_side(qtwo, "gx", 1)
    a_far, b_far, qtwo = together((swap_y(a_near, A_FIRST), swap_y(b_near, B_FIRST), qtwo))
    other = swap(jnp.concatenate([a_near, a_far, b_near, b_far]), "gy", 1)
    (skip_grad,) = call(
        skip_kernel, "skip_gradient", (((SKIP, SIZE_X, SIZE_Y, LANES), BF16),), (((SKIP * BLOCKS, LANES), F32),),
        8, (1_000_000, 1_000_000), rows, qone, qtwo, jskip,
    )
    dec, coarse = call(
        unpack_kernel, "unpack", (((DEC, JOINED), F32), ((DEC, COARSE), F32)), (((CHUNKS * ROWS, LANES), F32),),
        16, (1_000_000, 5_000_000), a_near, a_far, b_near, b_far, other,
    )
    return (
        skip_grad,
        dec.reshape(TAPS, SKIP, JOINED).transpose(0, 2, 1),
        coarse.reshape(TAPS, SKIP, COARSE),
    )


def solution(mesh):
    placed = (P(None, "gx", "gy", None), P(None, "gx", "gy", None), P(), P())
    return jax.shard_map(
        body,
        mesh=mesh,
        in_specs=placed,
        out_specs=(P(None, "gx", "gy", None), P(), P()),
        check_vma=False,
    )
```

```python
import functools
import math

import jax
import jax.numpy as jnp
from jax import lax
from jax.experimental import pallas as pl
from jax.experimental.pallas import tpu as pltpu
from jax.sharding import PartitionSpec as P

LANES = 128
SKIP, COARSE, JOINED = 64, 128, 192
SIZE_X, SIZE_Y = 2, 8
BLOCKS, BLOCKS_C = SIZE_X * SIZE_Y, SIZE_Y // 2
TAPS = 27
DEC = TAPS * SKIP
PACKED = DEC + DEC // 2 + DEC
ROWS = 136
CHUNKS = 32
SENT = CHUNKS // 2 * ROWS
FACE, FACE_Y = SIZE_Y + BLOCKS_C // 2, SIZE_X + 2 + 2
EDGE = 3
RIM = BLOCKS_C // 2 + 1
FACE_ROWS = (0, SIZE_Y - 1, None, *range(1, SIZE_Y - 1))
BF16, F32 = jnp.bfloat16, jnp.float32


def params(mib):
    return pltpu.CompilerParams(vmem_limit_bytes=mib << 20)


def lane_of(shape):
    return lax.broadcasted_iota(jnp.int32, shape, len(shape) - 1)


def is_even(value):
    return (lane_of(value.shape) & 1) == 0


def paired(value):
    return value + jnp.where(is_even(value), pltpu.roll(value, LANES - 1, 1), pltpu.roll(value, 1, 1))


def pack(first, second):
    return jnp.where(is_even(first), first, second)


def unpack_pair(value):
    even = is_even(value)
    return (
        jnp.where(even, value, pltpu.roll(value, 1, 1)),
        jnp.where(even, pltpu.roll(value, LANES - 1, 1), value),
    )


def shifted(value, step):
    if step == 0:
        return value
    lane = lane_of(value.shape)
    inside = lane < LANES - step if step > 0 else lane >= -step
    return jnp.where(inside, pltpu.roll(value, (-step) % LANES, 1), 0.0)


def places():
    return lax.axis_index("gx"), lax.axis_index("gy")


def half_of(place):
    gx, gy = place
    return (gy ^ (gy >> 1) ^ (gy >> 3) ^ (gx >> 2)) & 1


def sides(place):
    odd = (place & 1).astype(F32)
    inner = jnp.where((place == 0) | (place == 15), 0.0, 1.0).astype(F32)
    return (odd, (1.0 - odd) * inner), (1.0 - odd, odd * inner)


def mixed(weights, first, second):
    return weights[0] * first.astype(F32) + weights[1] * second.astype(F32)


def split_kernel(skip_hbm, cot_hbm, skip_out, cot_out, pool_out, edge_out, mid_out, near_edge_out, near_mid_out, skip_ref, cot_ref, rows_ref, arrived):
    odd = places()[0] & 1
    copies = [
        pltpu.make_async_copy(source, target, arrived.at[index])
        for index, (source, target) in enumerate(((cot_hbm, cot_ref), (skip_hbm, skip_ref)))
    ]
    for copy in copies:
        copy.start()

    def block_of(index):
        return rows_ref[pl.ds(index, SKIP, stride=BLOCKS), :]

    copies[0].wait()
    rows_ref[...] = cot_ref[...].astype(F32).reshape(SKIP * BLOCKS, LANES)
    for index in range(BLOCKS):
        cot_out[index] = block_of(index).astype(BF16)
    for at, row in enumerate(FACE_ROWS):
        if row is not None:
            one, two, piece = (near_edge_out, edge_out, at) if at < EDGE else (near_mid_out, mid_out, at - EDGE)
            one[piece] = cot_out[(1 - odd) * SIZE_Y + row]
            two[piece] = cot_out[odd * SIZE_Y + row]
    copies[1].wait()
    rows_ref[...] = skip_ref[...].astype(F32).reshape(SKIP * BLOCKS, LANES)
    pools = []
    for coarse in range(BLOCKS_C):
        total = None
        for index in (2 * coarse, 2 * coarse + 1, SIZE_Y + 2 * coarse, SIZE_Y + 2 * coarse + 1):
            block = block_of(index)
            skip_out[index] = block.astype(BF16)
            total = block if total is None else total + block
        pools.append(paired(total) * 0.125)
        pool_out[coarse] = pools[-1].astype(BF16)
    outer, inner = (pack(pools[i], pools[j]).astype(BF16) for i, j in ((0, 3), (1, 2)))
    near_edge_out[EDGE - 1], edge_out[EDGE - 1] = outer, outer
    near_mid_out[FACE - EDGE - 1], mid_out[FACE - EDGE - 1] = inner, inner


def call(kernel, name, outs, scratch, mib, cost, *operands, held=(), gives=pltpu.VMEM):
    return pl.pallas_call(
        kernel,
        out_shape=tuple(jax.ShapeDtypeStruct(shape, dtype) for shape, dtype in outs),
        in_specs=[pl.BlockSpec(memory_space=space) for space in held or (pltpu.VMEM,) * len(operands)],
        out_specs=tuple(pl.BlockSpec(memory_space=gives) for _ in outs),
        scratch_shapes=[pltpu.VMEM(*form) if isinstance(form, tuple) else form for form in scratch],
        compiler_params=params(mib),
        cost_estimate=pl.CostEstimate(flops=cost[0], bytes_accessed=cost[1], transcendentals=0),
        name=name,
    )(*operands)


def weights_kernel(dec_hbm, coarse_hbm, join_out, pre_out, back_out, dec_ref, coarse_ref, arrived):
    copies = [
        pltpu.make_async_copy(source, target, arrived.at[index])
        for index, (source, target) in enumerate(((dec_hbm, dec_ref), (coarse_hbm, coarse_ref)))
    ]
    for copy in copies:
        copy.start()
    copies[0].wait()
    join_out[...] = dec_ref[...].T
    copies[1].wait()
    pre_out[...] = coarse_ref[...].T
    for pair in range(9):
        for k in range(3):
            first = (3 * pair + k) * SKIP
            back_out[pair * SKIP : (pair + 1) * SKIP, k * COARSE : (k + 1) * COARSE] = coarse_ref[first : first + SKIP]


def faces_kernel(cot_ref, pool_ref, xedge_ref, xone_ref, *refs):
    one_out, two_out = refs[-2:]
    place = places()
    low, high = sides(place[0])
    odd = place[1] & 1
    for out, up in ((one_out, 1 - odd), (two_out, odd)):
        row = up * (SIZE_Y - 1)
        out[0] = mixed(low, xone_ref[up], xedge_ref[up]).astype(BF16)
        out[1] = cot_ref[row]
        out[2] = cot_ref[SIZE_Y + row]
        out[3] = mixed(high, xone_ref[up], xedge_ref[up]).astype(BF16)
        upper = up.astype(F32)

        def pooled_of(weights):
            first, second = unpack_pair(mixed(weights, xone_ref[EDGE - 1], xedge_ref[EDGE - 1]))
            return (1.0 - upper) * first + upper * second

        out[4] = pack(pooled_of(low), pool_ref[up * (BLOCKS_C - 1)].astype(F32)).astype(BF16)
        out[5] = pooled_of(high).astype(BF16)


def grads_kernel(
    skip_ref, cot_ref, pool_ref, xedge_ref, xmid_ref, oedge_ref, omid_ref, ytwo_ref, yone_ref, *refs,
):
    wdec_ref, wpre_ref, wback_ref = refs[:3]
    send_out, keep_out, jskip_out, rim_out, one_out, two_out = refs[3:9]
    cells_ref, pooled_ref, joined_ref, jgrad_ref, full_ref, pre_ref = refs[9:]
    factor = 1.0 / math.sqrt(524288)
    place = places()
    xlow, xhigh = sides(place[0])
    ylow, yhigh = sides(place[1])

    def face(xside, at):
        if at < EDGE:
            return mixed(xside, oedge_ref[at], xedge_ref[at])
        return mixed(xside, omid_ref[at - EDGE], xmid_ref[at - EDGE])

    def fine(plane, row):
        if row == 0:
            return mixed(ylow, yone_ref[plane], ytwo_ref[plane])
        if row == SIZE_Y + 1:
            return mixed(yhigh, yone_ref[plane], ytwo_ref[plane])
        if plane == 0:
            return face(xlow, FACE_ROWS.index(row - 1))
        if plane == SIZE_X + 1:
            return face(xhigh, FACE_ROWS.index(row - 1))
        return cot_ref[(plane - 1) * SIZE_Y + row - 1].astype(F32)

    wide_pool = {}
    for row, weights in ((0, ylow), (BLOCKS_C + 1, yhigh)):
        wide_pool[0, row], wide_pool[1, row] = unpack_pair(mixed(weights, yone_ref[4], ytwo_ref[4]))
        wide_pool[2, row] = mixed(weights, yone_ref[5], ytwo_ref[5])
    for plane, weights in ((0, xlow), (2, xhigh)):
        wide_pool[plane, 1], wide_pool[plane, 4] = unpack_pair(face(weights, EDGE - 1))
        wide_pool[plane, 2], wide_pool[plane, 3] = unpack_pair(face(weights, FACE - 1))
    for row in range(BLOCKS_C):
        wide_pool[1, row + 1] = pool_ref[row].astype(F32)

    for plane in range(3):
        for row in range(BLOCKS_C + 2):
            for k in range(3):
                value = shifted(wide_pool[plane, row], 2 * (k - 1)).astype(BF16)
                for j in range(3):
                    if 0 <= row - j < BLOCKS_C:
                        tap = 9 * plane + 3 * j + k
                        pooled_ref[tap * SKIP : (tap + 1) * SKIP, (row - j) * LANES : (row - j + 1) * LANES] = value
    pre_b = jnp.dot(wpre_ref[...], pooled_ref[...], preferred_element_type=F32)
    sig = 1.0 / (1.0 + jnp.exp(-pre_b))
    coarse_out = (pre_b * sig).astype(BF16)
    slope = sig * (1.0 + pre_b * (1.0 - sig))
    for index in range(BLOCKS):
        at = (index % SIZE_Y) // 2
        joined_ref[:COARSE, index * LANES : (index + 1) * LANES] = coarse_out[:, at * LANES : (at + 1) * LANES]
        joined_ref[COARSE:, index * LANES : (index + 1) * LANES] = skip_ref[index]
    for plane in range(SIZE_X + 2):
        for row in range(SIZE_Y + 2):
            wide = fine(plane, row)
            for k in range(3):
                value = shifted(wide, 1 - k).astype(BF16)
                for i in range(3):
                    for j in range(3):
                        x, y = plane - 2 + i, row - 2 + j
                        if 0 <= x < SIZE_X and 0 <= y < SIZE_Y:
                            tap, at = 9 * i + 3 * j + k, x * SIZE_Y + y
                            cells_ref[tap * SKIP : (tap + 1) * SKIP, at * LANES : (at + 1) * LANES] = value
    jgrad_ref[...] = jnp.dot(wdec_ref[...], cells_ref[...], preferred_element_type=F32)
    for index in range(BLOCKS):
        jskip_out[index] = jgrad_ref[COARSE:, index * LANES : (index + 1) * LANES]
    pre_parts = []
    for at in range(BLOCKS_C):
        total = None
        for index in (2 * at, 2 * at + 1, SIZE_Y + 2 * at, SIZE_Y + 2 * at + 1):
            part = jgrad_ref[:COARSE, index * LANES : (index + 1) * LANES]
            total = part if total is None else total + part
        pre_part = (paired(total) * slope[:, at * LANES : (at + 1) * LANES]).astype(BF16)
        pre_parts.append(pre_part)
        wide = pre_part.astype(F32)
        for k in range(3):
            pre_ref[k * COARSE : (k + 1) * COARSE, at * LANES : (at + 1) * LANES] = shifted(wide, 2 * (1 - k)).astype(BF16)
    pre_grad = jnp.concatenate(pre_parts, axis=1)

    terms = jnp.dot(wback_ref[...], pre_ref[...], preferred_element_type=F32) * 0.125

    def rim_row(i, row):
        total = None
        for j in range(3):
            if 0 <= row - j < BLOCKS_C:
                first = (3 * i + j) * SKIP
                part = terms[first : first + SKIP, (row - j) * LANES : (row - j + 1) * LANES]
                total = part if total is None else total + part
        return total

    for row in range(BLOCKS_C + 2):
        rim_out[row] = rim_row(1, row)
    odd = (place[0] & 1).astype(F32)
    for index in range(RIM):
        down, up = (pack(rim_row(i, 2 * index), rim_row(i, 2 * index + 1)) for i in (0, 2))
        one_out[index] = ((1.0 - odd) * up + odd * down).astype(BF16)
        two_out[index] = ((1.0 - odd) * down + odd * up).astype(BF16)

    across = (((1,), (1,)), ((), ()))
    dec = lax.dot_general(cells_ref[...], joined_ref[...], across, preferred_element_type=F32) * factor
    full_ref[:DEC] = dec[:, :LANES]
    full_ref[DEC : DEC + DEC // 2] = jnp.concatenate([dec[: DEC // 2, LANES:], dec[DEC // 2 :, LANES:]], axis=1)
    full_ref[DEC + DEC // 2 : PACKED] = lax.dot_general(
        pooled_ref[...], pre_grad, across, preferred_element_type=F32
    ) * (0.5 * factor)
    full_ref[PACKED:] = jnp.zeros((CHUNKS * ROWS - PACKED, LANES), F32)
    half, y, x = half_of(place), (place[1] >> 1) & 3, place[0] & 3
    for yr in range(4):
        leave = []
        for xr in range(4):
            at = (y ^ yr) * 4 + (x ^ xr)
            row = pl.multiple_of((at + 16 * half) * ROWS, ROWS)
            keep_out[yr, xr] = full_ref[pl.ds(row, ROWS), :]
            row = pl.multiple_of((at + 16 * (1 - half)) * ROWS, ROWS)
            leave.append(full_ref[pl.ds(row, ROWS), :])
        send_out[4 * yr * ROWS : 4 * (yr + 1) * ROWS] = jnp.concatenate(leave).astype(BF16)


def fold_kernel(rim_ref, xone_ref, xtwo_ref, rows_out, one_out, two_out):
    place = places()
    low, high = sides(place[0])
    weights = (low[0] + high[0], low[1] + high[1])
    rows = []
    for index in range(RIM):
        first, second = unpack_pair(mixed(weights, xone_ref[index], xtwo_ref[index]))
        rows += [rim_ref[2 * index] + first, rim_ref[2 * index + 1] + second]
    for row in range(BLOCKS_C):
        rows_out[row] = rows[row + 1]
    odd = (place[1] & 1).astype(F32)
    down, up = rows[0], rows[-1]
    one_out[...] = ((1.0 - odd) * up + odd * down).astype(BF16)
    two_out[...] = ((1.0 - odd) * down + odd * up).astype(BF16)


def skip_kernel(rows_ref, yone_ref, ytwo_ref, jskip_ref, out_ref, cells_ref):
    low, high = sides(places()[1])
    for at in range(BLOCKS_C):
        total = rows_ref[at]
        if at == 0:
            total = total + mixed(low, yone_ref[...], ytwo_ref[...])
        if at == BLOCKS_C - 1:
            total = total + mixed(high, yone_ref[...], ytwo_ref[...])
        for index in (2 * at, 2 * at + 1, SIZE_Y + 2 * at, SIZE_Y + 2 * at + 1):
            cells_ref[pl.ds(index, SKIP, stride=BLOCKS), :] = jskip_ref[index] + total
    out_ref[...] = cells_ref[...].reshape(SKIP, SIZE_X, SIZE_Y, LANES).astype(BF16)


def unpack_kernel(a0_ref, a1_ref, b0_ref, b1_ref, other_ref, dec_hbm, coarse_hbm, full_ref, dec_ref, sent):
    place = places()
    half, y, x = half_of(place), (place[1] >> 1) & 3, place[0] & 3
    for side, (refs, order) in enumerate((((a0_ref, a1_ref), ORDER_A), ((b0_ref, b1_ref), ORDER_B))):
        for index, yr in enumerate(order):
            for xr in range(2):
                at = (y ^ yr) * 4 + (x ^ (2 * side + xr))
                row = pl.multiple_of((at + 16 * half) * ROWS, ROWS)
                full_ref[pl.ds(row, ROWS), :] = refs[index // 2][index % 2, xr].astype(F32)
                row = pl.multiple_of((at + 16 * (1 - half)) * ROWS, ROWS)
                full_ref[pl.ds(row, ROWS), :] = other_ref[4 * side + index, xr].astype(F32)
    middle, part = LANES // 2, DEC // 2
    copies = [pltpu.make_async_copy(full_ref.at[pl.ds(DEC + part, DEC)], coarse_hbm, sent.at[0])]
    copies[0].start()
    for index in range(2):
        rows = slice(index * part, (index + 1) * part)
        dec_ref[rows, :LANES] = full_ref[rows]
        dec_ref[rows, LANES:] = full_ref[DEC : DEC + part, index * middle : (index + 1) * middle]
        window = pl.ds(index * part, part)
        copies.append(pltpu.make_async_copy(dec_ref.at[window], dec_hbm.at[window], sent.at[1 + index]))
        copies[-1].start()
    for copy in copies:
        copy.wait()


def swap(value, axis, flip):
    return lax.ppermute(value, axis, [(i, i ^ flip) for i in range(lax.axis_size(axis))])


def in_hbm(*operands):
    return [pltpu.with_memory_space_constraint(operand, pltpu.HBM) for operand in operands]


def partner(index, which, count):
    return index ^ 1 if which == 0 else (index + 2 * (index % 2) - 1) % count


def swap_side(value, axis, which):
    count = lax.axis_size(axis)
    return lax.ppermute(value, axis, [(i, partner(i, which, count)) for i in range(count)])


together = lax.optimization_barrier


A_FIRST, A_SECOND = 1, 3
B_FIRST, B_SECOND = 3, 1
ORDER_A = (0, A_SECOND, A_FIRST, 2)
ORDER_B = (0, B_SECOND, B_FIRST, 2)


def swap_y(value, flip):
    return swap(value, "gy", 2 * flip + 1)


def swap_z(value, flip):
    size_x, size_y = lax.axis_size("gx"), lax.axis_size("gy")
    pairs = [(i * size_y + j, (i ^ (4 * flip)) * size_y + (j ^ (flip & 1))) for i in range(size_x) for j in range(size_y)]
    return lax.ppermute(value, ("gx", "gy"), pairs)


def wide(value):
    return value.astype(F32)


def body(skip_feat, cotangent, w_coarse, w_dec):
    w_join, w_pre, w_back = call(
        weights_kernel, "lay_weights",
        (((JOINED, DEC), BF16), ((COARSE, DEC), BF16), ((9 * SKIP, 3 * COARSE), BF16)),
        (((DEC, JOINED), BF16), ((DEC, COARSE), BF16), pltpu.SemaphoreType.DMA((2,))), 16, (1_000_000, 2_500_000),
        *in_hbm(w_dec.transpose(0, 2, 1).reshape(DEC, JOINED), w_coarse.reshape(DEC, COARSE)), held=(pltpu.HBM,) * 2,
    )

    block = (SKIP, LANES)
    face_y, rim = (FACE_Y,) + block, (RIM,) + block
    fine = (BLOCKS,) + block
    skip, cot, pooled, xedge, xmid, oedge, omid = call(
        split_kernel, "split_blocks",
        (
            (fine, BF16), (fine, BF16), ((BLOCKS_C,) + block, BF16),
            *(((rows,) + block, BF16) for rows in (EDGE, FACE - EDGE, EDGE, FACE - EDGE)),
        ),
        (
            (skip_feat.shape, BF16), (skip_feat.shape, BF16), ((SKIP * BLOCKS, LANES), F32),
            pltpu.SemaphoreType.DMA((2,)),
        ),
        8, (1_000_000, 1_500_000), *in_hbm(skip_feat, cotangent),
        held=(pltpu.HBM,) * 2,
    )
    xedge, xmid = swap_side(xedge, "gx", 1), swap_side(xmid, "gx", 1)
    oedge, omid = swap_side(oedge, "gx", 0), swap_side(omid, "gx", 0)
    yone, ytwo = call(
        faces_kernel, "row_faces", ((face_y, BF16), (face_y, BF16)), (), 8, (100_000, 400_000),
        cot, pooled, xedge, oedge, w_join, w_pre, w_back, held=(pltpu.VMEM,) * 4 + (pl.ANY,) * 3,
    )
    yone, ytwo = swap_side(yone, "gy", 0), swap_side(ytwo, "gy", 1)
    chunks = (4, 4, ROWS, LANES)
    send, keep, jskip, own, rone, rtwo = call(
        grads_kernel, "local_grads",
        (
            ((SENT, LANES), BF16), (chunks, F32), (fine, F32),
            ((BLOCKS_C + 2,) + block, F32), (rim, BF16), (rim, BF16),
        ),
        (
            ((DEC, BLOCKS * LANES), BF16),
            ((DEC, BLOCKS_C * LANES), BF16),
            ((JOINED, BLOCKS * LANES), BF16),
            ((JOINED, BLOCKS * LANES), F32),
            ((CHUNKS * ROWS, LANES), F32),
            ((3 * COARSE, BLOCKS_C * LANES), BF16),
        ),
        36, (3_000_000_000, 8_000_000), skip, cot, pooled, xedge, xmid, oedge, omid, ytwo, yone,
        w_join, w_pre, w_back,
    )

    part = keep + wide(swap(send, "gy", 1).reshape(chunks))
    a, b = part[:, :2], part[:, 2:]
    a_got = swap_y(jnp.stack([a[A_FIRST], a[2]]).astype(BF16), A_FIRST)
    b_got = swap_y(jnp.stack([b[B_FIRST], b[2]]).astype(BF16), B_FIRST)
    a_got, b_got = together((a_got, b_got))
    a_own, a_leave = a[0] + wide(a_got[0]), a[A_SECOND] + wide(a_got[1])
    b_own, b_leave = b[0] + wide(b_got[0]), b[B_SECOND] + wide(b_got[1])
    a_got, b_got = swap_y(a_leave.astype(BF16), A_SECOND), swap_y(b_leave.astype(BF16), B_SECOND)
    a_got, b_got = together((a_got, b_got))
    rtwo = swap_side(rtwo, "gx", 1)
    part = jnp.concatenate([a_own + wide(a_got), b_own + wide(b_got)])
    leave = part.astype(BF16)
    got = swap(jnp.concatenate([leave[1], rone.reshape(RIM * SKIP, LANES)]), "gx", 1)
    got = [got[:ROWS], swap(leave[2], "gx", 2), swap(leave[3], "gx", 3), got[ROWS:].reshape(rim)]
    *got, rone, rtwo = together((*got, rtwo))
    rows, qone, qtwo = call(
        fold_kernel, "fold_rim", (((BLOCKS_C,) + block, F32), (block, BF16), (block, BF16)), (), 8, (100_000, 600_000),
        own, rone, rtwo,
    )
    part = (part[0] + wide(got[0])) + (wide(got[1]) + wide(got[2]))
    mine = part.astype(BF16)
    got = [swap_z(mine, flip) for flip in (1, 2, 3)]
    *got, rows, qone, qtwo = together((*got, rows, qone, qtwo))
    part = (wide(mine) + wide(got[0])) + (wide(got[1]) + wide(got[2]))
    got, qone, qtwo = together((swap(part, "gy", 9), swap_side(qone, "gy", 0), swap_side(qtwo, "gy", 1)))
    part = (part + got).astype(BF16)
    got = together([swap(part, "gx", flip) for flip in (1, 3, 2)])
    part = jnp.stack([part, got[0], got[2], got[1]])
    a, b = part[:2], part[2:]
    a_got, b_got = together((swap_y(a, A_SECOND), swap_y(b, B_SECOND)))
    a_near, b_near = jnp.stack([a, a_got]), jnp.stack([b, b_got])
    a_far, b_far = together((swap_y(a_near, A_FIRST), swap_y(b_near, B_FIRST)))
    other = swap(jnp.concatenate([a_near, a_far, b_near, b_far]), "gy", 1)
    (skip_grad,) = call(
        skip_kernel, "skip_gradient", (((SKIP, SIZE_X, SIZE_Y, LANES), BF16),), (((SKIP * BLOCKS, LANES), F32),),
        8, (1_000_000, 1_000_000), rows, qone, qtwo, jskip,
    )
    dec, coarse = call(
        unpack_kernel, "unpack", (((DEC, JOINED), F32), ((DEC, COARSE), F32)),
        (((CHUNKS * ROWS, LANES), F32), ((DEC, JOINED), F32), pltpu.SemaphoreType.DMA((3,))),
        16, (1_000_000, 5_000_000), a_near, a_far, b_near, b_far, other, gives=pltpu.HBM,
    )
    return (
        skip_grad,
        dec.reshape(TAPS, SKIP, JOINED).transpose(0, 2, 1),
        coarse.reshape(TAPS, SKIP, COARSE),
    )


def solution(mesh):
    placed = (P(None, "gx", "gy", None), P(None, "gx", "gy", None), P(), P())
    return jax.shard_map(
        body,
        mesh=mesh,
        in_specs=placed,
        out_specs=(P(None, "gx", "gy", None), P(), P()),
        check_vma=False,
    )
```

```python
import functools
import math

import jax
import jax.numpy as jnp
from jax import lax
from jax.experimental import pallas as pl
from jax.experimental.pallas import tpu as pltpu
from jax.sharding import PartitionSpec as P

LANES = 128
SKIP, COARSE, JOINED = 64, 128, 192
SIZE_X, SIZE_Y = 2, 8
BLOCKS, BLOCKS_C = SIZE_X * SIZE_Y, SIZE_Y // 2
TAPS = 27
DEC = TAPS * SKIP
PACKED = DEC + DEC // 2 + DEC
ROWS = 136
CHUNKS = 32
SENT = CHUNKS // 2 * ROWS
FACE, FACE_Y = SIZE_Y + BLOCKS_C // 2, SIZE_X + 2 + 2
EDGE = 3
RIM = BLOCKS_C // 2 + 1
FACE_ROWS = (0, SIZE_Y - 1, None, *range(1, SIZE_Y - 1))
BF16, F32 = jnp.bfloat16, jnp.float32


def params(mib):
    return pltpu.CompilerParams(vmem_limit_bytes=mib << 20)


def lane_of(shape):
    return lax.broadcasted_iota(jnp.int32, shape, len(shape) - 1)


def is_even(value):
    return (lane_of(value.shape) & 1) == 0


def paired(value):
    return value + jnp.where(is_even(value), pltpu.roll(value, LANES - 1, 1), pltpu.roll(value, 1, 1))


def pack(first, second):
    return jnp.where(is_even(first), first, second)


def unpack_pair(value):
    even = is_even(value)
    return (
        jnp.where(even, value, pltpu.roll(value, 1, 1)),
        jnp.where(even, pltpu.roll(value, LANES - 1, 1), value),
    )


def shifted(value, step):
    if step == 0:
        return value
    lane = lane_of(value.shape)
    inside = lane < LANES - step if step > 0 else lane >= -step
    return jnp.where(inside, pltpu.roll(value, (-step) % LANES, 1), 0.0)


def places():
    return lax.axis_index("gx"), lax.axis_index("gy")


def half_of(place):
    gx, gy = place
    return (gy ^ (gy >> 1) ^ (gy >> 3) ^ (gx >> 2)) & 1


def sides(place):
    odd = (place & 1).astype(F32)
    inner = jnp.where((place == 0) | (place == 15), 0.0, 1.0).astype(F32)
    return (odd, (1.0 - odd) * inner), (1.0 - odd, odd * inner)


def mixed(weights, first, second):
    return weights[0] * first.astype(F32) + weights[1] * second.astype(F32)


def split_kernel(skip_hbm, cot_hbm, skip_out, cot_out, pool_out, edge_out, mid_out, near_edge_out, near_mid_out, skip_ref, cot_ref, rows_ref, arrived):
    odd = places()[0] & 1
    copies = [
        pltpu.make_async_copy(source, target, arrived.at[index])
        for index, (source, target) in enumerate(((cot_hbm, cot_ref), (skip_hbm, skip_ref)))
    ]
    for copy in copies:
        copy.start()

    def block_of(index):
        return rows_ref[pl.ds(index, SKIP, stride=BLOCKS), :]

    copies[0].wait()
    rows_ref[...] = cot_ref[...].astype(F32).reshape(SKIP * BLOCKS, LANES)
    for index in range(BLOCKS):
        cot_out[index] = block_of(index).astype(BF16)
    for at, row in enumerate(FACE_ROWS):
        if row is not None:
            one, two, piece = (near_edge_out, edge_out, at) if at < EDGE else (near_mid_out, mid_out, at - EDGE)
            one[piece] = cot_out[(1 - odd) * SIZE_Y + row]
            two[piece] = cot_out[odd * SIZE_Y + row]
    copies[1].wait()
    rows_ref[...] = skip_ref[...].astype(F32).reshape(SKIP * BLOCKS, LANES)
    pools = []
    for coarse in range(BLOCKS_C):
        total = None
        for index in (2 * coarse, 2 * coarse + 1, SIZE_Y + 2 * coarse, SIZE_Y + 2 * coarse + 1):
            block = block_of(index)
            skip_out[index] = block.astype(BF16)
            total = block if total is None else total + block
        pools.append(paired(total) * 0.125)
        pool_out[coarse] = pools[-1].astype(BF16)
    outer, inner = (pack(pools[i], pools[j]).astype(BF16) for i, j in ((0, 3), (1, 2)))
    near_edge_out[EDGE - 1], edge_out[EDGE - 1] = outer, outer
    near_mid_out[FACE - EDGE - 1], mid_out[FACE - EDGE - 1] = inner, inner


def call(kernel, name, outs, scratch, mib, cost, *operands, held=(), gives=pltpu.VMEM):
    return pl.pallas_call(
        kernel,
        out_shape=tuple(jax.ShapeDtypeStruct(shape, dtype) for shape, dtype in outs),
        in_specs=[pl.BlockSpec(memory_space=space) for space in held or (pltpu.VMEM,) * len(operands)],
        out_specs=tuple(pl.BlockSpec(memory_space=gives) for _ in outs),
        scratch_shapes=[pltpu.VMEM(*form) if isinstance(form, tuple) else form for form in scratch],
        compiler_params=params(mib),
        cost_estimate=pl.CostEstimate(flops=cost[0], bytes_accessed=cost[1], transcendentals=0),
        name=name,
    )(*operands)


def weights_kernel(dec_hbm, coarse_hbm, join_out, pre_out, back_out, dec_ref, coarse_ref, arrived):
    copies = [
        pltpu.make_async_copy(source, target, arrived.at[index])
        for index, (source, target) in enumerate(((dec_hbm, dec_ref), (coarse_hbm, coarse_ref)))
    ]
    for copy in copies:
        copy.start()
    copies[0].wait()
    join_out[...] = dec_ref[...].T
    copies[1].wait()
    pre_out[...] = coarse_ref[...].T
    for pair in range(9):
        for k in range(3):
            first = (3 * pair + k) * SKIP
            back_out[pair * SKIP : (pair + 1) * SKIP, k * COARSE : (k + 1) * COARSE] = coarse_ref[first : first + SKIP]


def faces_kernel(cot_ref, pool_ref, xedge_ref, xone_ref, *refs):
    one_out, two_out = refs[-2:]
    place = places()
    low, high = sides(place[0])
    odd = place[1] & 1
    for out, up in ((one_out, 1 - odd), (two_out, odd)):
        row = up * (SIZE_Y - 1)
        out[0] = mixed(low, xone_ref[up], xedge_ref[up]).astype(BF16)
        out[1] = cot_ref[row]
        out[2] = cot_ref[SIZE_Y + row]
        out[3] = mixed(high, xone_ref[up], xedge_ref[up]).astype(BF16)
        upper = up.astype(F32)

        def pooled_of(weights):
            first, second = unpack_pair(mixed(weights, xone_ref[EDGE - 1], xedge_ref[EDGE - 1]))
            return (1.0 - upper) * first + upper * second

        out[4] = pack(pooled_of(low), pool_ref[up * (BLOCKS_C - 1)].astype(F32)).astype(BF16)
        out[5] = pooled_of(high).astype(BF16)


def grads_kernel(
    skip_ref, cot_ref, pool_ref, xedge_ref, xmid_ref, oedge_ref, omid_ref, ytwo_ref, yone_ref, *refs,
):
    wdec_ref, wpre_ref, wback_ref = refs[:3]
    send_out, keep_out, jskip_out, rim_out, one_out, two_out = refs[3:9]
    cells_ref, pooled_ref, joined_ref, jgrad_ref, full_ref, pre_ref = refs[9:]
    factor = 1.0 / math.sqrt(524288)
    place = places()
    xlow, xhigh = sides(place[0])
    ylow, yhigh = sides(place[1])

    def face(xside, at):
        if at < EDGE:
            return mixed(xside, oedge_ref[at], xedge_ref[at])
        return mixed(xside, omid_ref[at - EDGE], xmid_ref[at - EDGE])

    def fine(plane, row):
        if row == 0:
            return mixed(ylow, yone_ref[plane], ytwo_ref[plane])
        if row == SIZE_Y + 1:
            return mixed(yhigh, yone_ref[plane], ytwo_ref[plane])
        if plane == 0:
            return face(xlow, FACE_ROWS.index(row - 1))
        if plane == SIZE_X + 1:
            return face(xhigh, FACE_ROWS.index(row - 1))
        return cot_ref[(plane - 1) * SIZE_Y + row - 1].astype(F32)

    wide_pool = {}
    for row, weights in ((0, ylow), (BLOCKS_C + 1, yhigh)):
        wide_pool[0, row], wide_pool[1, row] = unpack_pair(mixed(weights, yone_ref[4], ytwo_ref[4]))
        wide_pool[2, row] = mixed(weights, yone_ref[5], ytwo_ref[5])
    for plane, weights in ((0, xlow), (2, xhigh)):
        wide_pool[plane, 1], wide_pool[plane, 4] = unpack_pair(face(weights, EDGE - 1))
        wide_pool[plane, 2], wide_pool[plane, 3] = unpack_pair(face(weights, FACE - 1))
    for row in range(BLOCKS_C):
        wide_pool[1, row + 1] = pool_ref[row].astype(F32)

    for plane in range(3):
        for row in range(BLOCKS_C + 2):
            for k in range(3):
                value = shifted(wide_pool[plane, row], 2 * (k - 1)).astype(BF16)
                for j in range(3):
                    if 0 <= row - j < BLOCKS_C:
                        tap = 9 * plane + 3 * j + k
                        pooled_ref[tap * SKIP : (tap + 1) * SKIP, (row - j) * LANES : (row - j + 1) * LANES] = value
    pre_b = jnp.dot(wpre_ref[...], pooled_ref[...], preferred_element_type=F32)
    sig = 1.0 / (1.0 + jnp.exp(-pre_b))
    coarse_out = (pre_b * sig).astype(BF16)
    slope = sig * (1.0 + pre_b * (1.0 - sig))
    for index in range(BLOCKS):
        at = (index % SIZE_Y) // 2
        joined_ref[:COARSE, index * LANES : (index + 1) * LANES] = coarse_out[:, at * LANES : (at + 1) * LANES]
        joined_ref[COARSE:, index * LANES : (index + 1) * LANES] = skip_ref[index]
    for plane in range(SIZE_X + 2):
        for row in range(SIZE_Y + 2):
            wide = fine(plane, row)
            for k in range(3):
                value = shifted(wide, 1 - k).astype(BF16)
                for i in range(3):
                    for j in range(3):
                        x, y = plane - 2 + i, row - 2 + j
                        if 0 <= x < SIZE_X and 0 <= y < SIZE_Y:
                            tap, at = 9 * i + 3 * j + k, x * SIZE_Y + y
                            cells_ref[tap * SKIP : (tap + 1) * SKIP, at * LANES : (at + 1) * LANES] = value
    jgrad_ref[...] = jnp.dot(wdec_ref[...], cells_ref[...], preferred_element_type=F32)
    for index in range(BLOCKS):
        jskip_out[index] = jgrad_ref[COARSE:, index * LANES : (index + 1) * LANES]
    pre_parts = []
    for at in range(BLOCKS_C):
        total = None
        for index in (2 * at, 2 * at + 1, SIZE_Y + 2 * at, SIZE_Y + 2 * at + 1):
            part = jgrad_ref[:COARSE, index * LANES : (index + 1) * LANES]
            total = part if total is None else total + part
        pre_part = (paired(total) * slope[:, at * LANES : (at + 1) * LANES]).astype(BF16)
        pre_parts.append(pre_part)
        wide = pre_part.astype(F32)
        for k in range(3):
            pre_ref[k * COARSE : (k + 1) * COARSE, at * LANES : (at + 1) * LANES] = shifted(wide, 2 * (1 - k)).astype(BF16)
    pre_grad = jnp.concatenate(pre_parts, axis=1)

    terms = jnp.dot(wback_ref[...], pre_ref[...], preferred_element_type=F32) * 0.125

    def rim_row(i, row):
        total = None
        for j in range(3):
            if 0 <= row - j < BLOCKS_C:
                first = (3 * i + j) * SKIP
                part = terms[first : first + SKIP, (row - j) * LANES : (row - j + 1) * LANES]
                total = part if total is None else total + part
        return total

    for row in range(BLOCKS_C + 2):
        rim_out[row] = rim_row(1, row)
    odd = (place[0] & 1).astype(F32)
    for index in range(RIM):
        down, up = (pack(rim_row(i, 2 * index), rim_row(i, 2 * index + 1)) for i in (0, 2))
        one_out[index] = ((1.0 - odd) * up + odd * down).astype(BF16)
        two_out[index] = ((1.0 - odd) * down + odd * up).astype(BF16)

    across = (((1,), (1,)), ((), ()))
    dec = lax.dot_general(cells_ref[...], joined_ref[...], across, preferred_element_type=F32) * factor
    full_ref[:DEC] = dec[:, :LANES]
    full_ref[DEC : DEC + DEC // 2] = jnp.concatenate([dec[: DEC // 2, LANES:], dec[DEC // 2 :, LANES:]], axis=1)
    full_ref[DEC + DEC // 2 : PACKED] = lax.dot_general(
        pooled_ref[...], pre_grad, across, preferred_element_type=F32
    ) * (0.5 * factor)
    full_ref[PACKED:] = jnp.zeros((CHUNKS * ROWS - PACKED, LANES), F32)
    half, y, x = half_of(place), (place[1] >> 1) & 3, place[0] & 3
    for yr in range(4):
        leave = []
        for xr in range(4):
            at = (y ^ yr) * 4 + (x ^ xr)
            row = pl.multiple_of((at + 16 * half) * ROWS, ROWS)
            keep_out[yr, xr] = full_ref[pl.ds(row, ROWS), :]
            row = pl.multiple_of((at + 16 * (1 - half)) * ROWS, ROWS)
            leave.append(full_ref[pl.ds(row, ROWS), :])
        send_out[4 * yr * ROWS : 4 * (yr + 1) * ROWS] = jnp.concatenate(leave).astype(BF16)


def fold_kernel(rim_ref, xone_ref, xtwo_ref, rows_out, one_out, two_out):
    place = places()
    low, high = sides(place[0])
    weights = (low[0] + high[0], low[1] + high[1])
    rows = []
    for index in range(RIM):
        first, second = unpack_pair(mixed(weights, xone_ref[index], xtwo_ref[index]))
        rows += [rim_ref[2 * index] + first, rim_ref[2 * index + 1] + second]
    for row in range(BLOCKS_C):
        rows_out[row] = rows[row + 1]
    odd = (place[1] & 1).astype(F32)
    down, up = rows[0], rows[-1]
    one_out[...] = ((1.0 - odd) * up + odd * down).astype(BF16)
    two_out[...] = ((1.0 - odd) * down + odd * up).astype(BF16)


def skip_kernel(rows_ref, yone_ref, ytwo_ref, jskip_ref, out_ref, cells_ref):
    low, high = sides(places()[1])
    for at in range(BLOCKS_C):
        total = rows_ref[at]
        if at == 0:
            total = total + mixed(low, yone_ref[...], ytwo_ref[...])
        if at == BLOCKS_C - 1:
            total = total + mixed(high, yone_ref[...], ytwo_ref[...])
        for index in (2 * at, 2 * at + 1, SIZE_Y + 2 * at, SIZE_Y + 2 * at + 1):
            cells_ref[pl.ds(index, SKIP, stride=BLOCKS), :] = jskip_ref[index] + total
    out_ref[...] = cells_ref[...].reshape(SKIP, SIZE_X, SIZE_Y, LANES).astype(BF16)


def unpack_kernel(a0_ref, a1_ref, b0_ref, b1_ref, other_ref, dec_hbm, coarse_hbm, full_ref, dec_ref, sent):
    place = places()
    half, y, x = half_of(place), (place[1] >> 1) & 3, place[0] & 3
    for side, (refs, order) in enumerate((((a0_ref, a1_ref), ORDER_A), ((b0_ref, b1_ref), ORDER_B))):
        for index, yr in enumerate(order):
            for xr in range(2):
                at = (y ^ yr) * 4 + (x ^ (2 * side + xr))
                row = pl.multiple_of((at + 16 * half) * ROWS, ROWS)
                full_ref[pl.ds(row, ROWS), :] = refs[index // 2][index % 2, xr].astype(F32)
                row = pl.multiple_of((at + 16 * (1 - half)) * ROWS, ROWS)
                full_ref[pl.ds(row, ROWS), :] = other_ref[4 * side + index, xr].astype(F32)
    middle, part = LANES // 2, DEC // 2
    copies = [pltpu.make_async_copy(full_ref.at[pl.ds(DEC + part, DEC)], coarse_hbm, sent.at[0])]
    copies[0].start()
    for index in range(2):
        rows = slice(index * part, (index + 1) * part)
        dec_ref[rows, :LANES] = full_ref[rows]
        dec_ref[rows, LANES:] = full_ref[DEC : DEC + part, index * middle : (index + 1) * middle]
        window = pl.ds(index * part, part)
        copies.append(pltpu.make_async_copy(dec_ref.at[window], dec_hbm.at[window], sent.at[1 + index]))
        copies[-1].start()
    for copy in copies:
        copy.wait()


def swap(value, axis, flip):
    return lax.ppermute(value, axis, [(i, i ^ flip) for i in range(lax.axis_size(axis))])


def in_hbm(*operands):
    return [pltpu.with_memory_space_constraint(operand, pltpu.HBM) for operand in operands]


def partner(index, which, count):
    return index ^ 1 if which == 0 else (index + 2 * (index % 2) - 1) % count


def swap_side(value, axis, which):
    count = lax.axis_size(axis)
    return lax.ppermute(value, axis, [(i, partner(i, which, count)) for i in range(count)])


together = lax.optimization_barrier


A_FIRST, A_SECOND = 1, 3
B_FIRST, B_SECOND = 3, 1
ORDER_A = (0, A_SECOND, A_FIRST, 2)
ORDER_B = (0, B_SECOND, B_FIRST, 2)


def swap_y(value, flip):
    return swap(value, "gy", 2 * flip + 1)


def swap_z(value, flip):
    size_x, size_y = lax.axis_size("gx"), lax.axis_size("gy")
    pairs = [(i * size_y + j, (i ^ (4 * flip)) * size_y + (j ^ (flip & 1))) for i in range(size_x) for j in range(size_y)]
    return lax.ppermute(value, ("gx", "gy"), pairs)


def wide(value):
    return value.astype(F32)


def body(skip_feat, cotangent, w_coarse, w_dec):
    w_join, w_pre, w_back = call(
        weights_kernel, "lay_weights",
        (((JOINED, DEC), BF16), ((COARSE, DEC), BF16), ((9 * SKIP, 3 * COARSE), BF16)),
        (((DEC, JOINED), BF16), ((DEC, COARSE), BF16), pltpu.SemaphoreType.DMA((2,))), 16, (1_000_000, 2_500_000),
        *in_hbm(w_dec.transpose(0, 2, 1).reshape(DEC, JOINED), w_coarse.reshape(DEC, COARSE)), held=(pltpu.HBM,) * 2,
    )

    block = (SKIP, LANES)
    face_y, rim = (FACE_Y,) + block, (RIM,) + block
    fine = (BLOCKS,) + block
    skip, cot, pooled, xedge, xmid, oedge, omid = call(
        split_kernel, "split_blocks",
        (
            (fine, BF16), (fine, BF16), ((BLOCKS_C,) + block, BF16),
            *(((rows,) + block, BF16) for rows in (EDGE, FACE - EDGE, EDGE, FACE - EDGE)),
        ),
        (
            (skip_feat.shape, BF16), (skip_feat.shape, BF16), ((SKIP * BLOCKS, LANES), F32),
            pltpu.SemaphoreType.DMA((2,)),
        ),
        8, (1_000_000, 1_500_000), *in_hbm(skip_feat, cotangent),
        held=(pltpu.HBM,) * 2,
    )
    xedge, xmid = swap_side(xedge, "gx", 1), swap_side(xmid, "gx", 1)
    oedge, omid = swap_side(oedge, "gx", 0), swap_side(omid, "gx", 0)
    yone, ytwo = call(
        faces_kernel, "row_faces", ((face_y, BF16), (face_y, BF16)), (), 8, (100_000, 400_000),
        cot, pooled, xedge, oedge, w_join, w_pre, w_back, held=(pltpu.VMEM,) * 4 + (pl.ANY,) * 3,
    )
    yone, ytwo = swap_side(yone, "gy", 0), swap_side(ytwo, "gy", 1)
    chunks = (4, 4, ROWS, LANES)
    send, keep, jskip, own, rone, rtwo = call(
        grads_kernel, "local_grads",
        (
            ((SENT, LANES), BF16), (chunks, F32), (fine, F32),
            ((BLOCKS_C + 2,) + block, F32), (rim, BF16), (rim, BF16),
        ),
        (
            ((DEC, BLOCKS * LANES), BF16),
            ((DEC, BLOCKS_C * LANES), BF16),
            ((JOINED, BLOCKS * LANES), BF16),
            ((JOINED, BLOCKS * LANES), F32),
            ((CHUNKS * ROWS, LANES), F32),
            ((3 * COARSE, BLOCKS_C * LANES), BF16),
        ),
        36, (3_000_000_000, 8_000_000), skip, cot, pooled, xedge, xmid, oedge, omid, ytwo, yone,
        w_join, w_pre, w_back,
    )

    part = keep + wide(swap(send, "gy", 1).reshape(chunks))
    a, b = part[:, :2], part[:, 2:]
    a_got = swap_y(jnp.stack([a[A_FIRST], a[2]]).astype(BF16), A_FIRST)
    b_got = swap_y(jnp.stack([b[B_FIRST], b[2]]).astype(BF16), B_FIRST)
    a_got, b_got = together((a_got, b_got))
    a_own, a_leave = a[0] + wide(a_got[0]), a[A_SECOND] + wide(a_got[1])
    b_own, b_leave = b[0] + wide(b_got[0]), b[B_SECOND] + wide(b_got[1])
    a_got, b_got = swap_y(a_leave.astype(BF16), A_SECOND), swap_y(b_leave.astype(BF16), B_SECOND)
    a_got, b_got = together((a_got, b_got))
    rtwo = swap_side(rtwo, "gx", 1)
    part = jnp.concatenate([a_own + wide(a_got), b_own + wide(b_got)])
    leave = part.astype(BF16)
    got = swap(jnp.concatenate([leave[1], rone.reshape(RIM * SKIP, LANES)]), "gx", 1)
    got = [got[:ROWS], swap(leave[2], "gx", 2), swap(leave[3], "gx", 3), got[ROWS:].reshape(rim)]
    *got, rone, rtwo = together((*got, rtwo))
    rows, qone, qtwo = call(
        fold_kernel, "fold_rim", (((BLOCKS_C,) + block, F32), (block, BF16), (block, BF16)), (), 8, (100_000, 600_000),
        own, rone, rtwo,
    )
    part = (part[0] + wide(got[0])) + (wide(got[1]) + wide(got[2]))
    mine = part.astype(BF16)
    got = [swap_z(mine, flip) for flip in (1, 2, 3)]
    *got, rows, qone, qtwo = together((*got, rows, qone, qtwo))
    part = (wide(mine) + wide(got[0])) + (wide(got[1]) + wide(got[2]))
    part = (part + swap(part, "gy", 9)).astype(BF16)
    got = together([swap(part, "gx", flip) for flip in (1, 3, 2)])
    part = jnp.stack([part, got[0], got[2], got[1]])
    a, b = part[:2], part[2:]
    a_got, b_got = together((swap_y(a, A_SECOND), swap_y(b, B_SECOND)))
    a_near, b_near = jnp.stack([a, a_got]), jnp.stack([b, b_got])
    a_far, b_far, qone, qtwo = together((swap_y(a_near, A_FIRST), swap_y(b_near, B_FIRST), swap_side(qone, "gy", 0), swap_side(qtwo, "gy", 1)))
    other = swap(jnp.concatenate([a_near, a_far, b_near, b_far]), "gy", 1)
    (skip_grad,) = call(
        skip_kernel, "skip_gradient", (((SKIP, SIZE_X, SIZE_Y, LANES), BF16),), (((SKIP * BLOCKS, LANES), F32),),
        8, (1_000_000, 1_000_000), rows, qone, qtwo, jskip,
    )
    dec, coarse = call(
        unpack_kernel, "unpack", (((DEC, JOINED), F32), ((DEC, COARSE), F32)),
        (((CHUNKS * ROWS, LANES), F32), ((DEC, JOINED), F32), pltpu.SemaphoreType.DMA((3,))),
        16, (1_000_000, 5_000_000), a_near, a_far, b_near, b_far, other, gives=pltpu.HBM,
    )
    return (
        skip_grad,
        dec.reshape(TAPS, SKIP, JOINED).transpose(0, 2, 1),
        coarse.reshape(TAPS, SKIP, COARSE),
    )


def solution(mesh):
    placed = (P(None, "gx", "gy", None), P(None, "gx", "gy", None), P(), P())
    return jax.shard_map(
        body,
        mesh=mesh,
        in_specs=placed,
        out_specs=(P(None, "gx", "gy", None), P(), P()),
        check_vma=False,
    )
```

```python
import functools
import math

import jax
import jax.numpy as jnp
from jax import lax
from jax.experimental import pallas as pl
from jax.experimental.pallas import tpu as pltpu
from jax.sharding import PartitionSpec as P

LANES = 128
SKIP, COARSE, JOINED = 64, 128, 192
SIZE_X, SIZE_Y = 2, 8
BLOCKS, BLOCKS_C = SIZE_X * SIZE_Y, SIZE_Y // 2
TAPS = 27
DEC = TAPS * SKIP
PACKED = DEC + DEC // 2 + DEC
ROWS = 136
CHUNKS = 32
SENT = CHUNKS // 2 * ROWS
FACE, FACE_Y = SIZE_Y + BLOCKS_C // 2, SIZE_X + 2 + 2
EDGE = 3
RIM = BLOCKS_C // 2 + 1
FACE_ROWS = (0, SIZE_Y - 1, None, *range(1, SIZE_Y - 1))
BF16, F32 = jnp.bfloat16, jnp.float32


def params(mib):
    return pltpu.CompilerParams(vmem_limit_bytes=mib << 20)


def lane_of(shape):
    return lax.broadcasted_iota(jnp.int32, shape, len(shape) - 1)


def is_even(value):
    return (lane_of(value.shape) & 1) == 0


def paired(value):
    return value + jnp.where(is_even(value), pltpu.roll(value, LANES - 1, 1), pltpu.roll(value, 1, 1))


def pack(first, second):
    return jnp.where(is_even(first), first, second)


def unpack_pair(value):
    even = is_even(value)
    return (
        jnp.where(even, value, pltpu.roll(value, 1, 1)),
        jnp.where(even, pltpu.roll(value, LANES - 1, 1), value),
    )


def shifted(value, step):
    if step == 0:
        return value
    lane = lane_of(value.shape)
    inside = lane < LANES - step if step > 0 else lane >= -step
    return jnp.where(inside, pltpu.roll(value, (-step) % LANES, 1), 0.0)


def places():
    return lax.axis_index("gx"), lax.axis_index("gy")


def half_of(place):
    gx, gy = place
    return (gy ^ (gy >> 1) ^ (gy >> 3) ^ gx ^ (gx >> 2)) & 1


def sides(place):
    odd = (place & 1).astype(F32)
    inner = jnp.where((place == 0) | (place == 15), 0.0, 1.0).astype(F32)
    return (odd, (1.0 - odd) * inner), (1.0 - odd, odd * inner)


def mixed(weights, first, second):
    return weights[0] * first.astype(F32) + weights[1] * second.astype(F32)


def split_kernel(skip_hbm, cot_hbm, skip_out, cot_out, pool_out, edge_out, mid_out, near_edge_out, near_mid_out, skip_ref, cot_ref, rows_ref, arrived):
    odd = places()[0] & 1
    copies = [
        pltpu.make_async_copy(source, target, arrived.at[index])
        for index, (source, target) in enumerate(((cot_hbm, cot_ref), (skip_hbm, skip_ref)))
    ]
    for copy in copies:
        copy.start()

    def block_of(index):
        return rows_ref[pl.ds(index, SKIP, stride=BLOCKS), :]

    copies[0].wait()
    rows_ref[...] = cot_ref[...].astype(F32).reshape(SKIP * BLOCKS, LANES)
    for index in range(BLOCKS):
        cot_out[index] = block_of(index).astype(BF16)
    for at, row in enumerate(FACE_ROWS):
        if row is not None:
            one, two, piece = (near_edge_out, edge_out, at) if at < EDGE else (near_mid_out, mid_out, at - EDGE)
            one[piece] = cot_out[(1 - odd) * SIZE_Y + row]
            two[piece] = cot_out[odd * SIZE_Y + row]
    copies[1].wait()
    rows_ref[...] = skip_ref[...].astype(F32).reshape(SKIP * BLOCKS, LANES)
    pools = []
    for coarse in range(BLOCKS_C):
        total = None
        for index in (2 * coarse, 2 * coarse + 1, SIZE_Y + 2 * coarse, SIZE_Y + 2 * coarse + 1):
            block = block_of(index)
            skip_out[index] = block.astype(BF16)
            total = block if total is None else total + block
        pools.append(paired(total) * 0.125)
        pool_out[coarse] = pools[-1].astype(BF16)
    outer, inner = (pack(pools[i], pools[j]).astype(BF16) for i, j in ((0, 3), (1, 2)))
    near_edge_out[EDGE - 1], edge_out[EDGE - 1] = outer, outer
    near_mid_out[FACE - EDGE - 1], mid_out[FACE - EDGE - 1] = inner, inner


def call(kernel, name, outs, scratch, mib, cost, *operands, held=(), gives=pltpu.VMEM):
    return pl.pallas_call(
        kernel,
        out_shape=tuple(jax.ShapeDtypeStruct(shape, dtype) for shape, dtype in outs),
        in_specs=[pl.BlockSpec(memory_space=space) for space in held or (pltpu.VMEM,) * len(operands)],
        out_specs=tuple(pl.BlockSpec(memory_space=gives) for _ in outs),
        scratch_shapes=[pltpu.VMEM(*form) if isinstance(form, tuple) else form for form in scratch],
        compiler_params=params(mib),
        cost_estimate=pl.CostEstimate(flops=cost[0], bytes_accessed=cost[1], transcendentals=0),
        name=name,
    )(*operands)


def weights_kernel(dec_hbm, coarse_hbm, join_out, pre_out, back_out, dec_ref, coarse_ref, arrived):
    copies = [
        pltpu.make_async_copy(source, target, arrived.at[index])
        for index, (source, target) in enumerate(((dec_hbm, dec_ref), (coarse_hbm, coarse_ref)))
    ]
    for copy in copies:
        copy.start()
    copies[0].wait()
    join_out[...] = dec_ref[...].T
    copies[1].wait()
    pre_out[...] = coarse_ref[...].T
    for pair in range(9):
        for k in range(3):
            first = (3 * pair + k) * SKIP
            back_out[pair * SKIP : (pair + 1) * SKIP, k * COARSE : (k + 1) * COARSE] = coarse_ref[first : first + SKIP]


def faces_kernel(cot_ref, pool_ref, xedge_ref, xone_ref, *refs):
    one_out, two_out = refs[-2:]
    place = places()
    low, high = sides(place[0])
    odd = place[1] & 1
    for out, up in ((one_out, 1 - odd), (two_out, odd)):
        row = up * (SIZE_Y - 1)
        out[0] = mixed(low, xone_ref[up], xedge_ref[up]).astype(BF16)
        out[1] = cot_ref[row]
        out[2] = cot_ref[SIZE_Y + row]
        out[3] = mixed(high, xone_ref[up], xedge_ref[up]).astype(BF16)
        upper = up.astype(F32)

        def pooled_of(weights):
            first, second = unpack_pair(mixed(weights, xone_ref[EDGE - 1], xedge_ref[EDGE - 1]))
            return (1.0 - upper) * first + upper * second

        out[4] = pack(pooled_of(low), pool_ref[up * (BLOCKS_C - 1)].astype(F32)).astype(BF16)
        out[5] = pooled_of(high).astype(BF16)


def grads_kernel(
    skip_ref, cot_ref, pool_ref, xedge_ref, xmid_ref, oedge_ref, omid_ref, ytwo_ref, yone_ref, *refs,
):
    wdec_ref, wpre_ref, wback_ref = refs[:3]
    send_out, keep_out, jskip_out, rim_out, two_out = refs[3:8]
    cells_ref, pooled_ref, joined_ref, jgrad_ref, full_ref, pre_ref = refs[8:]
    factor = 1.0 / math.sqrt(524288)
    place = places()
    xlow, xhigh = sides(place[0])
    ylow, yhigh = sides(place[1])

    def face(xside, at):
        if at < EDGE:
            return mixed(xside, oedge_ref[at], xedge_ref[at])
        return mixed(xside, omid_ref[at - EDGE], xmid_ref[at - EDGE])

    def fine(plane, row):
        if row == 0:
            return mixed(ylow, yone_ref[plane], ytwo_ref[plane])
        if row == SIZE_Y + 1:
            return mixed(yhigh, yone_ref[plane], ytwo_ref[plane])
        if plane == 0:
            return face(xlow, FACE_ROWS.index(row - 1))
        if plane == SIZE_X + 1:
            return face(xhigh, FACE_ROWS.index(row - 1))
        return cot_ref[(plane - 1) * SIZE_Y + row - 1].astype(F32)

    wide_pool = {}
    for row, weights in ((0, ylow), (BLOCKS_C + 1, yhigh)):
        wide_pool[0, row], wide_pool[1, row] = unpack_pair(mixed(weights, yone_ref[4], ytwo_ref[4]))
        wide_pool[2, row] = mixed(weights, yone_ref[5], ytwo_ref[5])
    for plane, weights in ((0, xlow), (2, xhigh)):
        wide_pool[plane, 1], wide_pool[plane, 4] = unpack_pair(face(weights, EDGE - 1))
        wide_pool[plane, 2], wide_pool[plane, 3] = unpack_pair(face(weights, FACE - 1))
    for row in range(BLOCKS_C):
        wide_pool[1, row + 1] = pool_ref[row].astype(F32)

    for plane in range(3):
        for row in range(BLOCKS_C + 2):
            for k in range(3):
                value = shifted(wide_pool[plane, row], 2 * (k - 1)).astype(BF16)
                for j in range(3):
                    if 0 <= row - j < BLOCKS_C:
                        tap = 9 * plane + 3 * j + k
                        pooled_ref[tap * SKIP : (tap + 1) * SKIP, (row - j) * LANES : (row - j + 1) * LANES] = value
    pre_b = jnp.dot(wpre_ref[...], pooled_ref[...], preferred_element_type=F32)
    sig = 1.0 / (1.0 + jnp.exp(-pre_b))
    coarse_out = (pre_b * sig).astype(BF16)
    slope = sig * (1.0 + pre_b * (1.0 - sig))
    for index in range(BLOCKS):
        at = (index % SIZE_Y) // 2
        joined_ref[:COARSE, index * LANES : (index + 1) * LANES] = coarse_out[:, at * LANES : (at + 1) * LANES]
        joined_ref[COARSE:, index * LANES : (index + 1) * LANES] = skip_ref[index]
    for plane in range(SIZE_X + 2):
        for row in range(SIZE_Y + 2):
            wide = fine(plane, row)
            for k in range(3):
                value = shifted(wide, 1 - k).astype(BF16)
                for i in range(3):
                    for j in range(3):
                        x, y = plane - 2 + i, row - 2 + j
                        if 0 <= x < SIZE_X and 0 <= y < SIZE_Y:
                            tap, at = 9 * i + 3 * j + k, x * SIZE_Y + y
                            cells_ref[tap * SKIP : (tap + 1) * SKIP, at * LANES : (at + 1) * LANES] = value
    jgrad_ref[...] = jnp.dot(wdec_ref[...], cells_ref[...], preferred_element_type=F32)
    for index in range(BLOCKS):
        jskip_out[index] = jgrad_ref[COARSE:, index * LANES : (index + 1) * LANES]
    pre_parts = []
    for at in range(BLOCKS_C):
        total = None
        for index in (2 * at, 2 * at + 1, SIZE_Y + 2 * at, SIZE_Y + 2 * at + 1):
            part = jgrad_ref[:COARSE, index * LANES : (index + 1) * LANES]
            total = part if total is None else total + part
        pre_part = (paired(total) * slope[:, at * LANES : (at + 1) * LANES]).astype(BF16)
        pre_parts.append(pre_part)
        wide = pre_part.astype(F32)
        for k in range(3):
            pre_ref[k * COARSE : (k + 1) * COARSE, at * LANES : (at + 1) * LANES] = shifted(wide, 2 * (1 - k)).astype(BF16)
    pre_grad = jnp.concatenate(pre_parts, axis=1)

    terms = jnp.dot(wback_ref[...], pre_ref[...], preferred_element_type=F32) * 0.125

    def rim_row(i, row):
        total = None
        for j in range(3):
            if 0 <= row - j < BLOCKS_C:
                first = (3 * i + j) * SKIP
                part = terms[first : first + SKIP, (row - j) * LANES : (row - j + 1) * LANES]
                total = part if total is None else total + part
        return total

    for row in range(BLOCKS_C + 2):
        rim_out[row] = rim_row(1, row)
    odd = (place[0] & 1).astype(F32)
    for index in range(RIM):
        down, up = (pack(rim_row(i, 2 * index), rim_row(i, 2 * index + 1)) for i in (0, 2))
        first = SENT + index * SKIP
        send_out[first : first + SKIP] = ((1.0 - odd) * up + odd * down).astype(BF16)
        two_out[index] = ((1.0 - odd) * down + odd * up).astype(BF16)

    across = (((1,), (1,)), ((), ()))
    dec = lax.dot_general(cells_ref[...], joined_ref[...], across, preferred_element_type=F32) * factor
    full_ref[:DEC] = dec[:, :LANES]
    full_ref[DEC : DEC + DEC // 2] = jnp.concatenate([dec[: DEC // 2, LANES:], dec[DEC // 2 :, LANES:]], axis=1)
    full_ref[DEC + DEC // 2 : PACKED] = lax.dot_general(
        pooled_ref[...], pre_grad, across, preferred_element_type=F32
    ) * (0.5 * factor)
    full_ref[PACKED:] = jnp.zeros((CHUNKS * ROWS - PACKED, LANES), F32)
    half, y, x = half_of(place), (place[1] >> 1) & 3, place[0] & 3
    for yr in range(4):
        leave = []
        for xr in range(4):
            at = (y ^ yr) * 4 + (x ^ xr)
            row = pl.multiple_of((at + 16 * half) * ROWS, ROWS)
            keep_out[yr, xr] = full_ref[pl.ds(row, ROWS), :]
            row = pl.multiple_of((at + 16 * (1 - half)) * ROWS, ROWS)
            leave.append(full_ref[pl.ds(row, ROWS), :])
        send_out[4 * yr * ROWS : 4 * (yr + 1) * ROWS] = jnp.concatenate(leave).astype(BF16)


def fold_kernel(rim_ref, xone_ref, xtwo_ref, rows_out, one_out, two_out):
    place = places()
    low, high = sides(place[0])
    weights = (low[0] + high[0], low[1] + high[1])
    rows = []
    for index in range(RIM):
        first, second = unpack_pair(mixed(weights, xone_ref[index], xtwo_ref[index]))
        rows += [rim_ref[2 * index] + first, rim_ref[2 * index + 1] + second]
    for row in range(BLOCKS_C):
        rows_out[row] = rows[row + 1]
    odd = (place[1] & 1).astype(F32)
    down, up = rows[0], rows[-1]
    one_out[...] = ((1.0 - odd) * up + odd * down).astype(BF16)
    two_out[...] = ((1.0 - odd) * down + odd * up).astype(BF16)


def skip_kernel(rows_ref, yone_ref, ytwo_ref, jskip_ref, out_ref, cells_ref):
    low, high = sides(places()[1])
    for at in range(BLOCKS_C):
        total = rows_ref[at]
        if at == 0:
            total = total + mixed(low, yone_ref[...], ytwo_ref[...])
        if at == BLOCKS_C - 1:
            total = total + mixed(high, yone_ref[...], ytwo_ref[...])
        for index in (2 * at, 2 * at + 1, SIZE_Y + 2 * at, SIZE_Y + 2 * at + 1):
            cells_ref[pl.ds(index, SKIP, stride=BLOCKS), :] = jskip_ref[index] + total
    out_ref[...] = cells_ref[...].reshape(SKIP, SIZE_X, SIZE_Y, LANES).astype(BF16)


def unpack_kernel(a0_ref, a1_ref, b0_ref, b1_ref, other_ref, dec_hbm, coarse_hbm, full_ref, dec_ref, sent):
    place = places()
    half, y, x = half_of(place), (place[1] >> 1) & 3, place[0] & 3
    for side, (refs, order) in enumerate((((a0_ref, a1_ref), ORDER_A), ((b0_ref, b1_ref), ORDER_B))):
        for index, yr in enumerate(order):
            for xr in range(2):
                at = (y ^ yr) * 4 + (x ^ (2 * side + xr))
                row = pl.multiple_of((at + 16 * half) * ROWS, ROWS)
                full_ref[pl.ds(row, ROWS), :] = refs[index // 2][index % 2, xr].astype(F32)
                row = pl.multiple_of((at + 16 * (1 - half)) * ROWS, ROWS)
                full_ref[pl.ds(row, ROWS), :] = other_ref[4 * side + index, xr].astype(F32)
    middle, part = LANES // 2, DEC // 2
    copies = [pltpu.make_async_copy(full_ref.at[pl.ds(DEC + part, DEC)], coarse_hbm, sent.at[0])]
    copies[0].start()
    for index in range(2):
        rows = slice(index * part, (index + 1) * part)
        dec_ref[rows, :LANES] = full_ref[rows]
        dec_ref[rows, LANES:] = full_ref[DEC : DEC + part, index * middle : (index + 1) * middle]
        window = pl.ds(index * part, part)
        copies.append(pltpu.make_async_copy(dec_ref.at[window], dec_hbm.at[window], sent.at[1 + index]))
        copies[-1].start()
    for copy in copies:
        copy.wait()


def swap(value, axis, flip):
    return lax.ppermute(value, axis, [(i, i ^ flip) for i in range(lax.axis_size(axis))])


def in_hbm(*operands):
    return [pltpu.with_memory_space_constraint(operand, pltpu.HBM) for operand in operands]


def partner(index, which, count):
    return index ^ 1 if which == 0 else (index + 2 * (index % 2) - 1) % count


def swap_side(value, axis, which):
    count = lax.axis_size(axis)
    return lax.ppermute(value, axis, [(i, partner(i, which, count)) for i in range(count)])


together = lax.optimization_barrier


A_FIRST, A_SECOND = 1, 3
B_FIRST, B_SECOND = 3, 1
ORDER_A = (0, A_SECOND, A_FIRST, 2)
ORDER_B = (0, B_SECOND, B_FIRST, 2)


def swap_y(value, flip):
    return swap(value, "gy", 2 * flip + 1)


def swap_far(value, flip_x, cross):
    size_x, size_y = lax.axis_size("gx"), lax.axis_size("gy")
    pairs = [(i * size_y + j, (i ^ flip_x) * size_y + (j ^ cross)) for i in range(size_x) for j in range(size_y)]
    return lax.ppermute(value, ("gx", "gy"), pairs)


def swap_x(value, flip):
    return swap_far(value, flip, flip & 1)


def swap_z(value, flip):
    return swap_far(value, 4 * flip, flip & 1)


def wide(value):
    return value.astype(F32)


def body(skip_feat, cotangent, w_coarse, w_dec):
    w_join, w_pre, w_back = call(
        weights_kernel, "lay_weights",
        (((JOINED, DEC), BF16), ((COARSE, DEC), BF16), ((9 * SKIP, 3 * COARSE), BF16)),
        (((DEC, JOINED), BF16), ((DEC, COARSE), BF16), pltpu.SemaphoreType.DMA((2,))), 16, (1_000_000, 2_500_000),
        *in_hbm(w_dec.transpose(0, 2, 1).reshape(DEC, JOINED), w_coarse.reshape(DEC, COARSE)), held=(pltpu.HBM,) * 2,
    )

    block = (SKIP, LANES)
    face_y, rim = (FACE_Y,) + block, (RIM,) + block
    fine = (BLOCKS,) + block
    skip, cot, pooled, xedge, xmid, oedge, omid = call(
        split_kernel, "split_blocks",
        (
            (fine, BF16), (fine, BF16), ((BLOCKS_C,) + block, BF16),
            *(((rows,) + block, BF16) for rows in (EDGE, FACE - EDGE, EDGE, FACE - EDGE)),
        ),
        (
            (skip_feat.shape, BF16), (skip_feat.shape, BF16), ((SKIP * BLOCKS, LANES), F32),
            pltpu.SemaphoreType.DMA((2,)),
        ),
        8, (1_000_000, 1_500_000), *in_hbm(skip_feat, cotangent),
        held=(pltpu.HBM,) * 2,
    )
    xedge, xmid = swap_side(xedge, "gx", 1), swap_side(xmid, "gx", 1)
    oedge, omid = swap_side(oedge, "gx", 0), swap_side(omid, "gx", 0)
    yone, ytwo = call(
        faces_kernel, "row_faces", ((face_y, BF16), (face_y, BF16)), (), 8, (100_000, 400_000),
        cot, pooled, xedge, oedge, w_join, w_pre, w_back, held=(pltpu.VMEM,) * 4 + (pl.ANY,) * 3,
    )
    yone, ytwo = swap_side(yone, "gy", 0), swap_side(ytwo, "gy", 1)
    chunks = (4, 4, ROWS, LANES)
    send, keep, jskip, own, rtwo = call(
        grads_kernel, "local_grads",
        (
            ((SENT + RIM * SKIP, LANES), BF16), (chunks, F32), (fine, F32),
            ((BLOCKS_C + 2,) + block, F32), (rim, BF16),
        ),
        (
            ((DEC, BLOCKS * LANES), BF16),
            ((DEC, BLOCKS_C * LANES), BF16),
            ((JOINED, BLOCKS * LANES), BF16),
            ((JOINED, BLOCKS * LANES), F32),
            ((CHUNKS * ROWS, LANES), F32),
            ((3 * COARSE, BLOCKS_C * LANES), BF16),
        ),
        36, (3_000_000_000, 8_000_000), skip, cot, pooled, xedge, xmid, oedge, omid, ytwo, yone,
        w_join, w_pre, w_back,
    )

    send = swap(send, "gy", 1)
    part = keep + wide(send[:SENT].reshape(chunks))
    a, b = part[:, :2], part[:, 2:]
    a_got = swap_y(jnp.stack([a[A_FIRST], a[2]]).astype(BF16), A_FIRST)
    b_got = swap_y(jnp.stack([b[B_FIRST], b[2]]).astype(BF16), B_FIRST)
    a_got, b_got = together((a_got, b_got))
    a_own, a_leave = a[0] + wide(a_got[0]), a[A_SECOND] + wide(a_got[1])
    b_own, b_leave = b[0] + wide(b_got[0]), b[B_SECOND] + wide(b_got[1])
    a_got, b_got = swap_y(a_leave.astype(BF16), A_SECOND), swap_y(b_leave.astype(BF16), B_SECOND)
    a_got, b_got = together((a_got, b_got))
    rtwo = swap_side(rtwo, "gx", 1)
    part = jnp.concatenate([a_own + wide(a_got), b_own + wide(b_got)])
    leave = part.astype(BF16)
    got = swap_x(jnp.concatenate([leave[1], send[SENT:]]), 1)
    got = [got[:ROWS], swap_x(leave[2], 2), swap_x(leave[3], 3), got[ROWS:].reshape(rim)]
    *got, rone, rtwo = together((*got, rtwo))
    rows, qone, qtwo = call(
        fold_kernel, "fold_rim", (((BLOCKS_C,) + block, F32), (block, BF16), (block, BF16)), (), 8, (100_000, 600_000),
        own, rone, rtwo,
    )
    part = (part[0] + wide(got[0])) + (wide(got[1]) + wide(got[2]))
    mine = part.astype(BF16)
    got = [swap_z(mine, flip) for flip in (1, 2, 3)]
    *got, rows, qone, qtwo = together((*got, rows, qone, qtwo))
    part = (wide(mine) + wide(got[0])) + (wide(got[1]) + wide(got[2]))
    part = (part + swap(part, "gy", 9)).astype(BF16)
    got = together([swap_x(part, flip) for flip in (1, 3, 2)])
    part = jnp.stack([part, got[0], got[2], got[1]])
    a, b = part[:2], part[2:]
    a_got, b_got = together((swap_y(a, A_SECOND), swap_y(b, B_SECOND)))
    a_near, b_near = jnp.stack([a, a_got]), jnp.stack([b, b_got])
    a_far, b_far, qone, qtwo = together((swap_y(a_near, A_FIRST), swap_y(b_near, B_FIRST), swap_side(qone, "gy", 0), swap_side(qtwo, "gy", 1)))
    other = swap(jnp.concatenate([a_near, a_far, b_near, b_far]), "gy", 1)
    (skip_grad,) = call(
        skip_kernel, "skip_gradient", (((SKIP, SIZE_X, SIZE_Y, LANES), BF16),), (((SKIP * BLOCKS, LANES), F32),),
        8, (1_000_000, 1_000_000), rows, qone, qtwo, jskip,
    )
    dec, coarse = call(
        unpack_kernel, "unpack", (((DEC, JOINED), F32), ((DEC, COARSE), F32)),
        (((CHUNKS * ROWS, LANES), F32), ((DEC, JOINED), F32), pltpu.SemaphoreType.DMA((3,))),
        16, (1_000_000, 5_000_000), a_near, a_far, b_near, b_far, other, gives=pltpu.HBM,
    )
    return (
        skip_grad,
        dec.reshape(TAPS, SKIP, JOINED).transpose(0, 2, 1),
        coarse.reshape(TAPS, SKIP, COARSE),
    )


def solution(mesh):
    placed = (P(None, "gx", "gy", None), P(None, "gx", "gy", None), P(), P())
    return jax.shard_map(
        body,
        mesh=mesh,
        in_specs=placed,
        out_specs=(P(None, "gx", "gy", None), P(), P()),
        check_vma=False,
    )
```

```python
import functools
import math

import jax
import jax.numpy as jnp
from jax import lax
from jax.experimental import pallas as pl
from jax.experimental.pallas import tpu as pltpu
from jax.sharding import PartitionSpec as P

LANES = 128
SKIP, COARSE, JOINED = 64, 128, 192
SIZE_X, SIZE_Y = 2, 8
BLOCKS, BLOCKS_C = SIZE_X * SIZE_Y, SIZE_Y // 2
TAPS = 27
DEC = TAPS * SKIP
PACKED = DEC + DEC // 2 + DEC
ROWS = 136
CHUNKS = 32
SENT = CHUNKS // 2 * ROWS
FACE, FACE_Y = SIZE_Y + BLOCKS_C // 2, SIZE_X + 2 + 2
EDGE = 3
RIM = BLOCKS_C // 2 + 1
FACE_ROWS = (0, SIZE_Y - 1, None, *range(1, SIZE_Y - 1))
BF16, F32 = jnp.bfloat16, jnp.float32


def params(mib):
    return pltpu.CompilerParams(vmem_limit_bytes=mib << 20)


def lane_of(shape):
    return lax.broadcasted_iota(jnp.int32, shape, len(shape) - 1)


def is_even(value):
    return (lane_of(value.shape) & 1) == 0


def paired(value):
    return value + jnp.where(is_even(value), pltpu.roll(value, LANES - 1, 1), pltpu.roll(value, 1, 1))


def pack(first, second):
    return jnp.where(is_even(first), first, second)


def unpack_pair(value):
    even = is_even(value)
    return (
        jnp.where(even, value, pltpu.roll(value, 1, 1)),
        jnp.where(even, pltpu.roll(value, LANES - 1, 1), value),
    )


def shifted(value, step):
    if step == 0:
        return value
    lane = lane_of(value.shape)
    inside = lane < LANES - step if step > 0 else lane >= -step
    return jnp.where(inside, pltpu.roll(value, (-step) % LANES, 1), 0.0)


def places():
    return lax.axis_index("gx"), lax.axis_index("gy")


def half_of(place):
    gx, gy = place
    return (gy ^ (gy >> 1) ^ (gy >> 3) ^ gx ^ (gx >> 2)) & 1


def sides(place):
    odd = (place & 1).astype(F32)
    inner = jnp.where((place == 0) | (place == 15), 0.0, 1.0).astype(F32)
    return (odd, (1.0 - odd) * inner), (1.0 - odd, odd * inner)


def mixed(weights, first, second):
    return weights[0] * first.astype(F32) + weights[1] * second.astype(F32)


def split_kernel(skip_hbm, cot_hbm, skip_out, cot_out, pool_out, edge_out, mid_out, near_edge_out, near_mid_out, skip_ref, cot_ref, rows_ref, arrived):
    odd = places()[0] & 1
    copies = [
        pltpu.make_async_copy(source, target, arrived.at[index])
        for index, (source, target) in enumerate(((cot_hbm, cot_ref), (skip_hbm, skip_ref)))
    ]
    for copy in copies:
        copy.start()

    def block_of(index):
        return rows_ref[pl.ds(index, SKIP, stride=BLOCKS), :]

    copies[0].wait()
    rows_ref[...] = cot_ref[...].astype(F32).reshape(SKIP * BLOCKS, LANES)
    for index in range(BLOCKS):
        cot_out[index] = block_of(index).astype(BF16)
    for at, row in enumerate(FACE_ROWS):
        if row is not None:
            one, two, piece = (near_edge_out, edge_out, at) if at < EDGE else (near_mid_out, mid_out, at - EDGE)
            one[piece] = cot_out[(1 - odd) * SIZE_Y + row]
            two[piece] = cot_out[odd * SIZE_Y + row]
    copies[1].wait()
    rows_ref[...] = skip_ref[...].astype(F32).reshape(SKIP * BLOCKS, LANES)
    pools = []
    for coarse in range(BLOCKS_C):
        total = None
        for index in (2 * coarse, 2 * coarse + 1, SIZE_Y + 2 * coarse, SIZE_Y + 2 * coarse + 1):
            block = block_of(index)
            skip_out[index] = block.astype(BF16)
            total = block if total is None else total + block
        pools.append(paired(total) * 0.125)
        pool_out[coarse] = pools[-1].astype(BF16)
    outer, inner = (pack(pools[i], pools[j]).astype(BF16) for i, j in ((0, 3), (1, 2)))
    near_edge_out[EDGE - 1], edge_out[EDGE - 1] = outer, outer
    near_mid_out[FACE - EDGE - 1], mid_out[FACE - EDGE - 1] = inner, inner


def call(kernel, name, outs, scratch, mib, cost, *operands, held=(), gives=pltpu.VMEM):
    return pl.pallas_call(
        kernel,
        out_shape=tuple(jax.ShapeDtypeStruct(shape, dtype) for shape, dtype in outs),
        in_specs=[pl.BlockSpec(memory_space=space) for space in held or (pltpu.VMEM,) * len(operands)],
        out_specs=tuple(pl.BlockSpec(memory_space=gives) for _ in outs),
        scratch_shapes=[pltpu.VMEM(*form) if isinstance(form, tuple) else form for form in scratch],
        compiler_params=params(mib),
        cost_estimate=pl.CostEstimate(flops=cost[0], bytes_accessed=cost[1], transcendentals=0),
        name=name,
    )(*operands)


def weights_kernel(dec_hbm, coarse_hbm, join_out, pre_out, back_out, dec_ref, coarse_ref, arrived):
    copies = [
        pltpu.make_async_copy(source, target, arrived.at[index])
        for index, (source, target) in enumerate(((dec_hbm, dec_ref), (coarse_hbm, coarse_ref)))
    ]
    for copy in copies:
        copy.start()
    copies[0].wait()
    join_out[...] = dec_ref[...].T
    copies[1].wait()
    pre_out[...] = coarse_ref[...].T
    for pair in range(9):
        for k in range(3):
            first = (3 * pair + k) * SKIP
            back_out[pair * SKIP : (pair + 1) * SKIP, k * COARSE : (k + 1) * COARSE] = coarse_ref[first : first + SKIP]


def faces_kernel(cot_ref, pool_ref, xedge_ref, xone_ref, *refs):
    one_out, two_out = refs[-2:]
    place = places()
    low, high = sides(place[0])
    odd = place[1] & 1
    for out, up in ((one_out, 1 - odd), (two_out, odd)):
        row = up * (SIZE_Y - 1)
        out[0] = mixed(low, xone_ref[up], xedge_ref[up]).astype(BF16)
        out[1] = cot_ref[row]
        out[2] = cot_ref[SIZE_Y + row]
        out[3] = mixed(high, xone_ref[up], xedge_ref[up]).astype(BF16)
        upper = up.astype(F32)

        def pooled_of(weights):
            first, second = unpack_pair(mixed(weights, xone_ref[EDGE - 1], xedge_ref[EDGE - 1]))
            return (1.0 - upper) * first + upper * second

        out[4] = pack(pooled_of(low), pool_ref[up * (BLOCKS_C - 1)].astype(F32)).astype(BF16)
        out[5] = pooled_of(high).astype(BF16)


def grads_kernel(
    skip_ref, cot_ref, pool_ref, xedge_ref, xmid_ref, oedge_ref, omid_ref, ytwo_ref, yone_ref, *refs,
):
    wdec_ref, wpre_ref, wback_ref = refs[:3]
    send_out, keep_out, jskip_out, rim_out, two_out = refs[3:8]
    cells_ref, pooled_ref, joined_ref, jgrad_ref, full_ref, pre_ref = refs[8:]
    factor = 1.0 / math.sqrt(524288)
    place = places()
    xlow, xhigh = sides(place[0])
    ylow, yhigh = sides(place[1])

    def face(xside, at):
        if at < EDGE:
            return mixed(xside, oedge_ref[at], xedge_ref[at])
        return mixed(xside, omid_ref[at - EDGE], xmid_ref[at - EDGE])

    def fine(plane, row):
        if row == 0:
            return mixed(ylow, yone_ref[plane], ytwo_ref[plane])
        if row == SIZE_Y + 1:
            return mixed(yhigh, yone_ref[plane], ytwo_ref[plane])
        if plane == 0:
            return face(xlow, FACE_ROWS.index(row - 1))
        if plane == SIZE_X + 1:
            return face(xhigh, FACE_ROWS.index(row - 1))
        return cot_ref[(plane - 1) * SIZE_Y + row - 1].astype(F32)

    wide_pool = {}
    for row, weights in ((0, ylow), (BLOCKS_C + 1, yhigh)):
        wide_pool[0, row], wide_pool[1, row] = unpack_pair(mixed(weights, yone_ref[4], ytwo_ref[4]))
        wide_pool[2, row] = mixed(weights, yone_ref[5], ytwo_ref[5])
    for plane, weights in ((0, xlow), (2, xhigh)):
        wide_pool[plane, 1], wide_pool[plane, 4] = unpack_pair(face(weights, EDGE - 1))
        wide_pool[plane, 2], wide_pool[plane, 3] = unpack_pair(face(weights, FACE - 1))
    for row in range(BLOCKS_C):
        wide_pool[1, row + 1] = pool_ref[row].astype(F32)

    for plane in range(3):
        for row in range(BLOCKS_C + 2):
            for k in range(3):
                value = shifted(wide_pool[plane, row], 2 * (k - 1)).astype(BF16)
                for j in range(3):
                    if 0 <= row - j < BLOCKS_C:
                        tap = 9 * plane + 3 * j + k
                        pooled_ref[tap * SKIP : (tap + 1) * SKIP, (row - j) * LANES : (row - j + 1) * LANES] = value
    pre_b = jnp.dot(wpre_ref[...], pooled_ref[...], preferred_element_type=F32)
    sig = 1.0 / (1.0 + jnp.exp(-pre_b))
    coarse_out = (pre_b * sig).astype(BF16)
    slope = sig * (1.0 + pre_b * (1.0 - sig))
    for index in range(BLOCKS):
        at = (index % SIZE_Y) // 2
        joined_ref[:COARSE, index * LANES : (index + 1) * LANES] = coarse_out[:, at * LANES : (at + 1) * LANES]
        joined_ref[COARSE:, index * LANES : (index + 1) * LANES] = skip_ref[index]
    for plane in range(SIZE_X + 2):
        for row in range(SIZE_Y + 2):
            wide = fine(plane, row)
            for k in range(3):
                value = shifted(wide, 1 - k).astype(BF16)
                for i in range(3):
                    for j in range(3):
                        x, y = plane - 2 + i, row - 2 + j
                        if 0 <= x < SIZE_X and 0 <= y < SIZE_Y:
                            tap, at = 9 * i + 3 * j + k, x * SIZE_Y + y
                            cells_ref[tap * SKIP : (tap + 1) * SKIP, at * LANES : (at + 1) * LANES] = value
    jgrad_ref[...] = jnp.dot(wdec_ref[...], cells_ref[...], preferred_element_type=F32)
    for index in range(BLOCKS):
        jskip_out[index] = jgrad_ref[COARSE:, index * LANES : (index + 1) * LANES]
    pre_parts = []
    for at in range(BLOCKS_C):
        total = None
        for index in (2 * at, 2 * at + 1, SIZE_Y + 2 * at, SIZE_Y + 2 * at + 1):
            part = jgrad_ref[:COARSE, index * LANES : (index + 1) * LANES]
            total = part if total is None else total + part
        pre_part = (paired(total) * slope[:, at * LANES : (at + 1) * LANES]).astype(BF16)
        pre_parts.append(pre_part)
        wide = pre_part.astype(F32)
        for k in range(3):
            pre_ref[k * COARSE : (k + 1) * COARSE, at * LANES : (at + 1) * LANES] = shifted(wide, 2 * (1 - k)).astype(BF16)
    pre_grad = jnp.concatenate(pre_parts, axis=1)

    terms = jnp.dot(wback_ref[...], pre_ref[...], preferred_element_type=F32) * 0.125

    def rim_row(i, row):
        total = None
        for j in range(3):
            if 0 <= row - j < BLOCKS_C:
                first = (3 * i + j) * SKIP
                part = terms[first : first + SKIP, (row - j) * LANES : (row - j + 1) * LANES]
                total = part if total is None else total + part
        return total

    for row in range(BLOCKS_C + 2):
        rim_out[row] = rim_row(1, row)
    odd = (place[0] & 1).astype(F32)
    for index in range(RIM):
        down, up = (pack(rim_row(i, 2 * index), rim_row(i, 2 * index + 1)) for i in (0, 2))
        first = SENT + index * SKIP
        send_out[first : first + SKIP] = ((1.0 - odd) * up + odd * down).astype(BF16)
        two_out[index] = ((1.0 - odd) * down + odd * up).astype(BF16)

    across = (((1,), (1,)), ((), ()))
    dec = lax.dot_general(cells_ref[...], joined_ref[...], across, preferred_element_type=F32) * factor
    full_ref[:DEC] = dec[:, :LANES]
    full_ref[DEC : DEC + DEC // 2] = jnp.concatenate([dec[: DEC // 2, LANES:], dec[DEC // 2 :, LANES:]], axis=1)
    full_ref[DEC + DEC // 2 : PACKED] = lax.dot_general(
        pooled_ref[...], pre_grad, across, preferred_element_type=F32
    ) * (0.5 * factor)
    full_ref[PACKED:] = jnp.zeros((CHUNKS * ROWS - PACKED, LANES), F32)
    half, y, x = half_of(place), (place[1] >> 1) & 3, place[0] & 3
    for yr in range(4):
        leave = []
        for xr in range(4):
            at = (y ^ yr) * 4 + (x ^ xr)
            row = pl.multiple_of((at + 16 * half) * ROWS, ROWS)
            keep_out[yr, xr] = full_ref[pl.ds(row, ROWS), :]
            row = pl.multiple_of((at + 16 * (1 - half)) * ROWS, ROWS)
            leave.append(full_ref[pl.ds(row, ROWS), :])
        send_out[4 * yr * ROWS : 4 * (yr + 1) * ROWS] = jnp.concatenate(leave).astype(BF16)


def fold_kernel(rim_ref, xone_ref, xtwo_ref, rows_out, one_out, two_out):
    place = places()
    low, high = sides(place[0])
    weights = (low[0] + high[0], low[1] + high[1])
    rows = []
    for index in range(RIM):
        first, second = unpack_pair(mixed(weights, xone_ref[index], xtwo_ref[index]))
        rows += [rim_ref[2 * index] + first, rim_ref[2 * index + 1] + second]
    for row in range(BLOCKS_C):
        rows_out[row] = rows[row + 1]
    odd = (place[1] & 1).astype(F32)
    down, up = rows[0], rows[-1]
    one_out[...] = ((1.0 - odd) * up + odd * down).astype(BF16)
    two_out[...] = ((1.0 - odd) * down + odd * up).astype(BF16)


def skip_kernel(rows_ref, yone_ref, ytwo_ref, jskip_ref, out_ref, cells_ref):
    low, high = sides(places()[1])
    for at in range(BLOCKS_C):
        total = rows_ref[at]
        if at == 0:
            total = total + mixed(low, yone_ref[...], ytwo_ref[...])
        if at == BLOCKS_C - 1:
            total = total + mixed(high, yone_ref[...], ytwo_ref[...])
        for index in (2 * at, 2 * at + 1, SIZE_Y + 2 * at, SIZE_Y + 2 * at + 1):
            cells_ref[pl.ds(index, SKIP, stride=BLOCKS), :] = jskip_ref[index] + total
    out_ref[...] = cells_ref[...].reshape(SKIP, SIZE_X, SIZE_Y, LANES).astype(BF16)


def unpack_kernel(a0_ref, a1_ref, b0_ref, b1_ref, other_ref, dec_hbm, coarse_hbm, full_ref, dec_ref, sent):
    place = places()
    half, y, x = half_of(place), (place[1] >> 1) & 3, place[0] & 3
    for side, (refs, order) in enumerate((((a0_ref, a1_ref), ORDER_A), ((b0_ref, b1_ref), ORDER_B))):
        for index, yr in enumerate(order):
            for xr in range(2):
                at = (y ^ yr) * 4 + (x ^ (2 * side + xr))
                row = pl.multiple_of((at + 16 * half) * ROWS, ROWS)
                full_ref[pl.ds(row, ROWS), :] = refs[index // 2][index % 2, xr].astype(F32)
                row = pl.multiple_of((at + 16 * (1 - half)) * ROWS, ROWS)
                full_ref[pl.ds(row, ROWS), :] = other_ref[4 * side + index, xr].astype(F32)
    middle, part = LANES // 2, DEC // 2
    copies = [pltpu.make_async_copy(full_ref.at[pl.ds(DEC + part, DEC)], coarse_hbm, sent.at[0])]
    copies[0].start()
    for index in range(2):
        rows = slice(index * part, (index + 1) * part)
        dec_ref[rows, :LANES] = full_ref[rows]
        dec_ref[rows, LANES:] = full_ref[DEC : DEC + part, index * middle : (index + 1) * middle]
        window = pl.ds(index * part, part)
        copies.append(pltpu.make_async_copy(dec_ref.at[window], dec_hbm.at[window], sent.at[1 + index]))
        copies[-1].start()
    for copy in copies:
        copy.wait()


def swap(value, axis, flip):
    return lax.ppermute(value, axis, [(i, i ^ flip) for i in range(lax.axis_size(axis))])


def in_hbm(*operands):
    return [pltpu.with_memory_space_constraint(operand, pltpu.HBM) for operand in operands]


def partner(index, which, count):
    return index ^ 1 if which == 0 else (index + 2 * (index % 2) - 1) % count


def swap_side(value, axis, which):
    count = lax.axis_size(axis)
    return lax.ppermute(value, axis, [(i, partner(i, which, count)) for i in range(count)])


together = lax.optimization_barrier


A_FIRST, A_SECOND = 1, 3
B_FIRST, B_SECOND = 3, 1
ORDER_A = (0, A_SECOND, A_FIRST, 2)
ORDER_B = (0, B_SECOND, B_FIRST, 2)


def swap_y(value, flip):
    return swap(value, "gy", 2 * flip + 1)


def swap_far(value, flip_x, cross):
    size_x, size_y = lax.axis_size("gx"), lax.axis_size("gy")
    pairs = [(i * size_y + j, (i ^ flip_x) * size_y + (j ^ cross)) for i in range(size_x) for j in range(size_y)]
    return lax.ppermute(value, ("gx", "gy"), pairs)


def swap_x(value, flip):
    return swap_far(value, flip, flip & 1)


def swap_z(value, flip):
    return swap_far(value, 4 * flip, flip & 1)


def wide(value):
    return value.astype(F32)


def body(skip_feat, cotangent, w_coarse, w_dec):
    w_join, w_pre, w_back = call(
        weights_kernel, "lay_weights",
        (((JOINED, DEC), BF16), ((COARSE, DEC), BF16), ((9 * SKIP, 3 * COARSE), BF16)),
        (((DEC, JOINED), BF16), ((DEC, COARSE), BF16), pltpu.SemaphoreType.DMA((2,))), 16, (1_000_000, 2_500_000),
        *in_hbm(w_dec.transpose(0, 2, 1).reshape(DEC, JOINED), w_coarse.reshape(DEC, COARSE)), held=(pltpu.HBM,) * 2,
    )

    block = (SKIP, LANES)
    face_y, rim = (FACE_Y,) + block, (RIM,) + block
    fine = (BLOCKS,) + block
    skip, cot, pooled, xedge, xmid, oedge, omid = call(
        split_kernel, "split_blocks",
        (
            (fine, BF16), (fine, BF16), ((BLOCKS_C,) + block, BF16),
            *(((rows,) + block, BF16) for rows in (EDGE, FACE - EDGE, EDGE, FACE - EDGE)),
        ),
        (
            (skip_feat.shape, BF16), (skip_feat.shape, BF16), ((SKIP * BLOCKS, LANES), F32),
            pltpu.SemaphoreType.DMA((2,)),
        ),
        8, (1_000_000, 1_500_000), *in_hbm(skip_feat, cotangent),
        held=(pltpu.HBM,) * 2,
    )
    xedge, xmid = swap_side(xedge, "gx", 1), swap_side(xmid, "gx", 1)
    oedge, omid = swap_side(oedge, "gx", 0), swap_side(omid, "gx", 0)
    yone, ytwo = call(
        faces_kernel, "row_faces", ((face_y, BF16), (face_y, BF16)), (), 8, (100_000, 400_000),
        cot, pooled, xedge, oedge, w_join, w_pre, w_back, held=(pltpu.VMEM,) * 4 + (pl.ANY,) * 3,
    )
    yone, ytwo = swap_side(yone, "gy", 0), swap_side(ytwo, "gy", 1)
    chunks = (4, 4, ROWS, LANES)
    send, keep, jskip, own, rtwo = call(
        grads_kernel, "local_grads",
        (
            ((SENT + RIM * SKIP, LANES), BF16), (chunks, F32), (fine, F32),
            ((BLOCKS_C + 2,) + block, F32), (rim, BF16),
        ),
        (
            ((DEC, BLOCKS * LANES), BF16),
            ((DEC, BLOCKS_C * LANES), BF16),
            ((JOINED, BLOCKS * LANES), BF16),
            ((JOINED, BLOCKS * LANES), F32),
            ((CHUNKS * ROWS, LANES), F32),
            ((3 * COARSE, BLOCKS_C * LANES), BF16),
        ),
        36, (3_000_000_000, 8_000_000), skip, cot, pooled, xedge, xmid, oedge, omid, ytwo, yone,
        w_join, w_pre, w_back,
    )

    send = swap(send, "gy", 1)
    part = keep + wide(send[:SENT].reshape(chunks))
    a, b = part[:, :2], part[:, 2:]
    a_got = swap_y(jnp.stack([a[A_FIRST], a[2]]).astype(BF16), A_FIRST)
    b_got = swap_y(jnp.stack([b[B_FIRST], b[2]]).astype(BF16), B_FIRST)
    a_got, b_got = together((a_got, b_got))
    a_own, a_leave = a[0] + wide(a_got[0]), a[A_SECOND] + wide(a_got[1])
    b_own, b_leave = b[0] + wide(b_got[0]), b[B_SECOND] + wide(b_got[1])
    a_got, b_got = swap_y(a_leave.astype(BF16), A_SECOND), swap_y(b_leave.astype(BF16), B_SECOND)
    a_got, b_got = together((a_got, b_got))
    rtwo = swap_side(rtwo, "gx", 1)
    part = jnp.concatenate([a_own + wide(a_got), b_own + wide(b_got)])
    leave = part.astype(BF16)
    got = swap_x(jnp.concatenate([leave[1], send[SENT:]]), 1)
    got = [got[:ROWS], swap_x(leave[2], 2), swap_x(leave[3], 3), got[ROWS:].reshape(rim)]
    *got, rone, rtwo = together((*got, rtwo))
    rows, qone, qtwo = call(
        fold_kernel, "fold_rim", (((BLOCKS_C,) + block, F32), (block, BF16), (block, BF16)), (), 8, (100_000, 600_000),
        own, rone, rtwo,
    )
    part = (part[0] + wide(got[0])) + (wide(got[1]) + wide(got[2]))
    mine = part.astype(BF16)
    got = [swap_z(mine, flip) for flip in (1, 2, 3)]
    *got, rows, qone, qtwo = together((*got, rows, qone, qtwo))
    part = (wide(mine) + wide(got[0])) + (wide(got[1]) + wide(got[2]))
    mine = part.astype(BF16)
    part = (wide(mine) + wide(swap(mine, "gy", 9))).astype(BF16)
    got = together([swap_x(part, flip) for flip in (1, 3, 2)])
    part = jnp.stack([part, got[0], got[2], got[1]])
    a, b = part[:2], part[2:]
    a_got, b_got = together((swap_y(a, A_SECOND), swap_y(b, B_SECOND)))
    a_near, b_near = jnp.stack([a, a_got]), jnp.stack([b, b_got])
    a_far, b_far, qone, qtwo = together((swap_y(a_near, A_FIRST), swap_y(b_near, B_FIRST), swap_side(qone, "gy", 0), swap_side(qtwo, "gy", 1)))
    other = swap(jnp.concatenate([a_near, a_far, b_near, b_far]), "gy", 1)
    (skip_grad,) = call(
        skip_kernel, "skip_gradient", (((SKIP, SIZE_X, SIZE_Y, LANES), BF16),), (((SKIP * BLOCKS, LANES), F32),),
        8, (1_000_000, 1_000_000), rows, qone, qtwo, jskip,
    )
    dec, coarse = call(
        unpack_kernel, "unpack", (((DEC, JOINED), F32), ((DEC, COARSE), F32)),
        (((CHUNKS * ROWS, LANES), F32), ((DEC, JOINED), F32), pltpu.SemaphoreType.DMA((3,))),
        16, (1_000_000, 5_000_000), a_near, a_far, b_near, b_far, other, gives=pltpu.HBM,
    )
    return (
        skip_grad,
        dec.reshape(TAPS, SKIP, JOINED).transpose(0, 2, 1),
        coarse.reshape(TAPS, SKIP, COARSE),
    )


def solution(mesh):
    placed = (P(None, "gx", "gy", None), P(None, "gx", "gy", None), P(), P())
    return jax.shard_map(
        body,
        mesh=mesh,
        in_specs=placed,
        out_specs=(P(None, "gx", "gy", None), P(), P()),
        check_vma=False,
    )
```

```python
import functools
import math

import jax
import jax.numpy as jnp
from jax import lax
from jax.experimental import pallas as pl
from jax.experimental.pallas import tpu as pltpu
from jax.sharding import PartitionSpec as P

LANES = 128
SKIP, COARSE, JOINED = 64, 128, 192
SIZE_X, SIZE_Y = 2, 8
BLOCKS, BLOCKS_C = SIZE_X * SIZE_Y, SIZE_Y // 2
TAPS = 27
DEC = TAPS * SKIP
PACKED = DEC + DEC // 2 + DEC
ROWS = 136
CHUNKS = 32
SENT = CHUNKS // 2 * ROWS
FACE, FACE_Y = SIZE_Y + BLOCKS_C // 2, SIZE_X + 2 + 2
EDGE = 3
RIM = BLOCKS_C // 2 + 1
FACE_ROWS = (0, SIZE_Y - 1, None, *range(1, SIZE_Y - 1))
BF16, F32 = jnp.bfloat16, jnp.float32


def params(mib):
    return pltpu.CompilerParams(vmem_limit_bytes=mib << 20)


def lane_of(shape):
    return lax.broadcasted_iota(jnp.int32, shape, len(shape) - 1)


def is_even(value):
    return (lane_of(value.shape) & 1) == 0


def paired(value):
    return value + jnp.where(is_even(value), pltpu.roll(value, LANES - 1, 1), pltpu.roll(value, 1, 1))


def pack(first, second):
    return jnp.where(is_even(first), first, second)


def unpack_pair(value):
    even = is_even(value)
    return (
        jnp.where(even, value, pltpu.roll(value, 1, 1)),
        jnp.where(even, pltpu.roll(value, LANES - 1, 1), value),
    )


def shifted(value, step):
    if step == 0:
        return value
    lane = lane_of(value.shape)
    inside = lane < LANES - step if step > 0 else lane >= -step
    return jnp.where(inside, pltpu.roll(value, (-step) % LANES, 1), 0.0)


def places():
    return lax.axis_index("gx"), lax.axis_index("gy")


def half_of(place):
    gx, gy = place
    return (gy ^ (gy >> 1) ^ (gy >> 3) ^ gx ^ (gx >> 2)) & 1


def sides(place):
    odd = (place & 1).astype(F32)
    inner = jnp.where((place == 0) | (place == 15), 0.0, 1.0).astype(F32)
    return (odd, (1.0 - odd) * inner), (1.0 - odd, odd * inner)


def mixed(weights, first, second):
    return weights[0] * first.astype(F32) + weights[1] * second.astype(F32)


def split_kernel(skip_hbm, cot_hbm, skip_out, cot_out, pool_out, edge_out, mid_out, near_edge_out, near_mid_out, skip_ref, cot_ref, rows_ref, arrived):
    odd = places()[0] & 1
    copies = [
        pltpu.make_async_copy(source, target, arrived.at[index])
        for index, (source, target) in enumerate(((cot_hbm, cot_ref), (skip_hbm, skip_ref)))
    ]
    for copy in copies:
        copy.start()

    def block_of(index):
        return rows_ref[pl.ds(index, SKIP, stride=BLOCKS), :]

    copies[0].wait()
    rows_ref[...] = cot_ref[...].astype(F32).reshape(SKIP * BLOCKS, LANES)
    for index in range(BLOCKS):
        cot_out[index] = block_of(index).astype(BF16)
    for at, row in enumerate(FACE_ROWS):
        if row is not None:
            one, two, piece = (near_edge_out, edge_out, at) if at < EDGE else (near_mid_out, mid_out, at - EDGE)
            one[piece] = cot_out[(1 - odd) * SIZE_Y + row]
            two[piece] = cot_out[odd * SIZE_Y + row]
    copies[1].wait()
    rows_ref[...] = skip_ref[...].astype(F32).reshape(SKIP * BLOCKS, LANES)
    pools = []
    for coarse in range(BLOCKS_C):
        total = None
        for index in (2 * coarse, 2 * coarse + 1, SIZE_Y + 2 * coarse, SIZE_Y + 2 * coarse + 1):
            block = block_of(index)
            skip_out[index] = block.astype(BF16)
            total = block if total is None else total + block
        pools.append(paired(total) * 0.125)
        pool_out[coarse] = pools[-1].astype(BF16)
    outer, inner = (pack(pools[i], pools[j]).astype(BF16) for i, j in ((0, 3), (1, 2)))
    near_edge_out[EDGE - 1], edge_out[EDGE - 1] = outer, outer
    near_mid_out[FACE - EDGE - 1], mid_out[FACE - EDGE - 1] = inner, inner


def call(kernel, name, outs, scratch, mib, cost, *operands, held=(), gives=pltpu.VMEM):
    return pl.pallas_call(
        kernel,
        out_shape=tuple(jax.ShapeDtypeStruct(shape, dtype) for shape, dtype in outs),
        in_specs=[pl.BlockSpec(memory_space=space) for space in held or (pltpu.VMEM,) * len(operands)],
        out_specs=tuple(pl.BlockSpec(memory_space=gives) for _ in outs),
        scratch_shapes=[pltpu.VMEM(*form) if isinstance(form, tuple) else form for form in scratch],
        compiler_params=params(mib),
        cost_estimate=pl.CostEstimate(flops=cost[0], bytes_accessed=cost[1], transcendentals=0),
        name=name,
    )(*operands)


def weights_kernel(dec_hbm, coarse_hbm, join_out, pre_out, back_out, dec_ref, coarse_ref, arrived):
    copies = [
        pltpu.make_async_copy(source, target, arrived.at[index])
        for index, (source, target) in enumerate(((dec_hbm, dec_ref), (coarse_hbm, coarse_ref)))
    ]
    for copy in copies:
        copy.start()
    copies[0].wait()
    join_out[...] = dec_ref[...].T
    copies[1].wait()
    pre_out[...] = coarse_ref[...].T
    for pair in range(9):
        for k in range(3):
            first = (3 * pair + k) * SKIP
            back_out[pair * SKIP : (pair + 1) * SKIP, k * COARSE : (k + 1) * COARSE] = coarse_ref[first : first + SKIP]


def faces_kernel(cot_ref, pool_ref, xedge_ref, xone_ref, *refs):
    one_out, two_out = refs[-2:]
    place = places()
    low, high = sides(place[0])
    odd = place[1] & 1
    for out, up in ((one_out, 1 - odd), (two_out, odd)):
        row = up * (SIZE_Y - 1)
        out[0] = mixed(low, xone_ref[up], xedge_ref[up]).astype(BF16)
        out[1] = cot_ref[row]
        out[2] = cot_ref[SIZE_Y + row]
        out[3] = mixed(high, xone_ref[up], xedge_ref[up]).astype(BF16)
        upper = up.astype(F32)

        def pooled_of(weights):
            first, second = unpack_pair(mixed(weights, xone_ref[EDGE - 1], xedge_ref[EDGE - 1]))
            return (1.0 - upper) * first + upper * second

        out[4] = pack(pooled_of(low), pool_ref[up * (BLOCKS_C - 1)].astype(F32)).astype(BF16)
        out[5] = pooled_of(high).astype(BF16)


def grads_kernel(
    skip_ref, cot_ref, pool_ref, xedge_ref, xmid_ref, oedge_ref, omid_ref, ytwo_ref, yone_ref, *refs,
):
    wdec_ref, wpre_ref, wback_ref = refs[:3]
    send_out, keep_out, jskip_out, rim_out, two_out = refs[3:8]
    cells_ref, pooled_ref, joined_ref, jgrad_ref, full_ref, pre_ref = refs[8:]
    factor = 1.0 / math.sqrt(524288)
    place = places()
    xlow, xhigh = sides(place[0])
    ylow, yhigh = sides(place[1])

    def face(xside, at):
        if at < EDGE:
            return mixed(xside, oedge_ref[at], xedge_ref[at])
        return mixed(xside, omid_ref[at - EDGE], xmid_ref[at - EDGE])

    def fine(plane, row):
        if row == 0:
            return mixed(ylow, yone_ref[plane], ytwo_ref[plane])
        if row == SIZE_Y + 1:
            return mixed(yhigh, yone_ref[plane], ytwo_ref[plane])
        if plane == 0:
            return face(xlow, FACE_ROWS.index(row - 1))
        if plane == SIZE_X + 1:
            return face(xhigh, FACE_ROWS.index(row - 1))
        return cot_ref[(plane - 1) * SIZE_Y + row - 1].astype(F32)

    wide_pool = {}
    for row, weights in ((0, ylow), (BLOCKS_C + 1, yhigh)):
        wide_pool[0, row], wide_pool[1, row] = unpack_pair(mixed(weights, yone_ref[4], ytwo_ref[4]))
        wide_pool[2, row] = mixed(weights, yone_ref[5], ytwo_ref[5])
    for plane, weights in ((0, xlow), (2, xhigh)):
        wide_pool[plane, 1], wide_pool[plane, 4] = unpack_pair(face(weights, EDGE - 1))
        wide_pool[plane, 2], wide_pool[plane, 3] = unpack_pair(face(weights, FACE - 1))
    for row in range(BLOCKS_C):
        wide_pool[1, row + 1] = pool_ref[row].astype(F32)

    for plane in range(3):
        for row in range(BLOCKS_C + 2):
            for k in range(3):
                value = shifted(wide_pool[plane, row], 2 * (k - 1)).astype(BF16)
                for j in range(3):
                    if 0 <= row - j < BLOCKS_C:
                        tap = 9 * plane + 3 * j + k
                        pooled_ref[tap * SKIP : (tap + 1) * SKIP, (row - j) * LANES : (row - j + 1) * LANES] = value
    pre_b = jnp.dot(wpre_ref[...], pooled_ref[...], preferred_element_type=F32)
    sig = 1.0 / (1.0 + jnp.exp(-pre_b))
    coarse_out = (pre_b * sig).astype(BF16)
    slope = sig * (1.0 + pre_b * (1.0 - sig))
    for index in range(BLOCKS):
        at = (index % SIZE_Y) // 2
        joined_ref[:COARSE, index * LANES : (index + 1) * LANES] = coarse_out[:, at * LANES : (at + 1) * LANES]
        joined_ref[COARSE:, index * LANES : (index + 1) * LANES] = skip_ref[index]
    for plane in range(SIZE_X + 2):
        for row in range(SIZE_Y + 2):
            wide = fine(plane, row)
            for k in range(3):
                value = shifted(wide, 1 - k).astype(BF16)
                for i in range(3):
                    for j in range(3):
                        x, y = plane - 2 + i, row - 2 + j
                        if 0 <= x < SIZE_X and 0 <= y < SIZE_Y:
                            tap, at = 9 * i + 3 * j + k, x * SIZE_Y + y
                            cells_ref[tap * SKIP : (tap + 1) * SKIP, at * LANES : (at + 1) * LANES] = value
    jgrad_ref[...] = jnp.dot(wdec_ref[...], cells_ref[...], preferred_element_type=F32)
    for index in range(BLOCKS):
        jskip_out[index] = jgrad_ref[COARSE:, index * LANES : (index + 1) * LANES]
    pre_parts = []
    for at in range(BLOCKS_C):
        total = None
        for index in (2 * at, 2 * at + 1, SIZE_Y + 2 * at, SIZE_Y + 2 * at + 1):
            part = jgrad_ref[:COARSE, index * LANES : (index + 1) * LANES]
            total = part if total is None else total + part
        pre_part = (paired(total) * slope[:, at * LANES : (at + 1) * LANES]).astype(BF16)
        pre_parts.append(pre_part)
        wide = pre_part.astype(F32)
        for k in range(3):
            pre_ref[k * COARSE : (k + 1) * COARSE, at * LANES : (at + 1) * LANES] = shifted(wide, 2 * (1 - k)).astype(BF16)
    pre_grad = jnp.concatenate(pre_parts, axis=1)

    terms = jnp.dot(wback_ref[...], pre_ref[...], preferred_element_type=F32) * 0.125

    def rim_row(i, row):
        total = None
        for j in range(3):
            if 0 <= row - j < BLOCKS_C:
                first = (3 * i + j) * SKIP
                part = terms[first : first + SKIP, (row - j) * LANES : (row - j + 1) * LANES]
                total = part if total is None else total + part
        return total

    for row in range(BLOCKS_C + 2):
        rim_out[row] = rim_row(1, row)
    odd = (place[0] & 1).astype(F32)
    for index in range(RIM):
        down, up = (pack(rim_row(i, 2 * index), rim_row(i, 2 * index + 1)) for i in (0, 2))
        first = SENT + index * SKIP
        send_out[first : first + SKIP] = ((1.0 - odd) * up + odd * down).astype(BF16)
        two_out[index] = ((1.0 - odd) * down + odd * up).astype(BF16)

    across = (((1,), (1,)), ((), ()))
    dec = lax.dot_general(cells_ref[...], joined_ref[...], across, preferred_element_type=F32) * factor
    full_ref[:DEC] = dec[:, :LANES]
    full_ref[DEC : DEC + DEC // 2] = jnp.concatenate([dec[: DEC // 2, LANES:], dec[DEC // 2 :, LANES:]], axis=1)
    full_ref[DEC + DEC // 2 : PACKED] = lax.dot_general(
        pooled_ref[...], pre_grad, across, preferred_element_type=F32
    ) * (0.5 * factor)
    full_ref[PACKED:] = jnp.zeros((CHUNKS * ROWS - PACKED, LANES), F32)
    half, y, x = half_of(place), (place[1] >> 1) & 3, place[0] & 3
    for yr in range(4):
        leave = []
        for xr in range(4):
            at = (y ^ yr) * 4 + (x ^ xr)
            row = pl.multiple_of((at + 16 * half) * ROWS, ROWS)
            keep_out[yr, xr] = full_ref[pl.ds(row, ROWS), :]
            row = pl.multiple_of((at + 16 * (1 - half)) * ROWS, ROWS)
            leave.append(full_ref[pl.ds(row, ROWS), :])
        send_out[4 * yr * ROWS : 4 * (yr + 1) * ROWS] = jnp.concatenate(leave).astype(BF16)


def fold_kernel(rim_ref, xone_ref, xtwo_ref, rows_out, one_out, two_out):
    place = places()
    low, high = sides(place[0])
    weights = (low[0] + high[0], low[1] + high[1])
    rows = []
    for index in range(RIM):
        first, second = unpack_pair(mixed(weights, xone_ref[index], xtwo_ref[index]))
        rows += [rim_ref[2 * index] + first, rim_ref[2 * index + 1] + second]
    for row in range(BLOCKS_C):
        rows_out[row] = rows[row + 1]
    odd = (place[1] & 1).astype(F32)
    down, up = rows[0], rows[-1]
    one_out[...] = ((1.0 - odd) * up + odd * down).astype(BF16)
    two_out[...] = ((1.0 - odd) * down + odd * up).astype(BF16)


def skip_kernel(rows_ref, yone_ref, ytwo_ref, jskip_ref, out_ref, cells_ref):
    low, high = sides(places()[1])
    for at in range(BLOCKS_C):
        total = rows_ref[at]
        if at == 0:
            total = total + mixed(low, yone_ref[...], ytwo_ref[...])
        if at == BLOCKS_C - 1:
            total = total + mixed(high, yone_ref[...], ytwo_ref[...])
        for index in (2 * at, 2 * at + 1, SIZE_Y + 2 * at, SIZE_Y + 2 * at + 1):
            cells_ref[pl.ds(index, SKIP, stride=BLOCKS), :] = jskip_ref[index] + total
    out_ref[...] = cells_ref[...].reshape(SKIP, SIZE_X, SIZE_Y, LANES).astype(BF16)


def unpack_kernel(a0_ref, a1_ref, b0_ref, b1_ref, near_ref, far_ref, dec_hbm, coarse_hbm, full_ref, dec_ref, sent):
    place = places()
    half, y, x = half_of(place), (place[1] >> 1) & 3, place[0] & 3
    for side, (refs, order) in enumerate((((a0_ref, a1_ref), ORDER_A), ((b0_ref, b1_ref), ORDER_B))):
        for index, yr in enumerate(order):
            for xr in range(2):
                at = (y ^ yr) * 4 + (x ^ (2 * side + xr))
                row = pl.multiple_of((at + 16 * half) * ROWS, ROWS)
                full_ref[pl.ds(row, ROWS), :] = refs[index // 2][index % 2, xr].astype(F32)
                row = pl.multiple_of((at + 16 * (1 - half)) * ROWS, ROWS)
                full_ref[pl.ds(row, ROWS), :] = (near_ref, far_ref)[index // 2][2 * side + index % 2, xr].astype(F32)
    middle, part = LANES // 2, DEC // 2
    copies = [pltpu.make_async_copy(full_ref.at[pl.ds(DEC + part, DEC)], coarse_hbm, sent.at[0])]
    copies[0].start()
    for index in range(2):
        rows = slice(index * part, (index + 1) * part)
        dec_ref[rows, :LANES] = full_ref[rows]
        dec_ref[rows, LANES:] = full_ref[DEC : DEC + part, index * middle : (index + 1) * middle]
        window = pl.ds(index * part, part)
        copies.append(pltpu.make_async_copy(dec_ref.at[window], dec_hbm.at[window], sent.at[1 + index]))
        copies[-1].start()
    for copy in copies:
        copy.wait()


def swap(value, axis, flip):
    return lax.ppermute(value, axis, [(i, i ^ flip) for i in range(lax.axis_size(axis))])


def in_hbm(*operands):
    return [pltpu.with_memory_space_constraint(operand, pltpu.HBM) for operand in operands]


def partner(index, which, count):
    return index ^ 1 if which == 0 else (index + 2 * (index % 2) - 1) % count


def swap_side(value, axis, which):
    count = lax.axis_size(axis)
    return lax.ppermute(value, axis, [(i, partner(i, which, count)) for i in range(count)])


together = lax.optimization_barrier


A_FIRST, A_SECOND = 1, 3
B_FIRST, B_SECOND = 3, 1
ORDER_A = (0, A_SECOND, A_FIRST, 2)
ORDER_B = (0, B_SECOND, B_FIRST, 2)


def swap_y(value, flip):
    return swap(value, "gy", 2 * flip + 1)


def swap_far(value, flip_x, cross):
    size_x, size_y = lax.axis_size("gx"), lax.axis_size("gy")
    pairs = [(i * size_y + j, (i ^ flip_x) * size_y + (j ^ cross)) for i in range(size_x) for j in range(size_y)]
    return lax.ppermute(value, ("gx", "gy"), pairs)


def swap_x(value, flip):
    return swap_far(value, flip, flip & 1)


def swap_z(value, flip):
    return swap_far(value, 4 * flip, flip & 1)


def wide(value):
    return value.astype(F32)


def body(skip_feat, cotangent, w_coarse, w_dec):
    w_join, w_pre, w_back = call(
        weights_kernel, "lay_weights",
        (((JOINED, DEC), BF16), ((COARSE, DEC), BF16), ((9 * SKIP, 3 * COARSE), BF16)),
        (((DEC, JOINED), BF16), ((DEC, COARSE), BF16), pltpu.SemaphoreType.DMA((2,))), 16, (1_000_000, 2_500_000),
        *in_hbm(w_dec.transpose(0, 2, 1).reshape(DEC, JOINED), w_coarse.reshape(DEC, COARSE)), held=(pltpu.HBM,) * 2,
    )

    block = (SKIP, LANES)
    face_y, rim = (FACE_Y,) + block, (RIM,) + block
    fine = (BLOCKS,) + block
    skip, cot, pooled, xedge, xmid, oedge, omid = call(
        split_kernel, "split_blocks",
        (
            (fine, BF16), (fine, BF16), ((BLOCKS_C,) + block, BF16),
            *(((rows,) + block, BF16) for rows in (EDGE, FACE - EDGE, EDGE, FACE - EDGE)),
        ),
        (
            (skip_feat.shape, BF16), (skip_feat.shape, BF16), ((SKIP * BLOCKS, LANES), F32),
            pltpu.SemaphoreType.DMA((2,)),
        ),
        8, (1_000_000, 1_500_000), *in_hbm(skip_feat, cotangent),
        held=(pltpu.HBM,) * 2,
    )
    xedge, xmid = swap_side(xedge, "gx", 1), swap_side(xmid, "gx", 1)
    oedge, omid = swap_side(oedge, "gx", 0), swap_side(omid, "gx", 0)
    yone, ytwo = call(
        faces_kernel, "row_faces", ((face_y, BF16), (face_y, BF16)), (), 8, (100_000, 400_000),
        cot, pooled, xedge, oedge, w_join, w_pre, w_back, held=(pltpu.VMEM,) * 4 + (pl.ANY,) * 3,
    )
    yone, ytwo = swap_side(yone, "gy", 0), swap_side(ytwo, "gy", 1)
    chunks = (4, 4, ROWS, LANES)
    send, keep, jskip, own, rtwo = call(
        grads_kernel, "local_grads",
        (
            ((SENT + RIM * SKIP, LANES), BF16), (chunks, F32), (fine, F32),
            ((BLOCKS_C + 2,) + block, F32), (rim, BF16),
        ),
        (
            ((DEC, BLOCKS * LANES), BF16),
            ((DEC, BLOCKS_C * LANES), BF16),
            ((JOINED, BLOCKS * LANES), BF16),
            ((JOINED, BLOCKS * LANES), F32),
            ((CHUNKS * ROWS, LANES), F32),
            ((3 * COARSE, BLOCKS_C * LANES), BF16),
        ),
        36, (3_000_000_000, 8_000_000), skip, cot, pooled, xedge, xmid, oedge, omid, ytwo, yone,
        w_join, w_pre, w_back,
    )

    send = swap(send, "gy", 1)
    part = keep + wide(send[:SENT].reshape(chunks))
    a, b = part[:, :2], part[:, 2:]
    a_got = swap_y(jnp.stack([a[A_FIRST], a[2]]).astype(BF16), A_FIRST)
    b_got = swap_y(jnp.stack([b[B_FIRST], b[2]]).astype(BF16), B_FIRST)
    a_got, b_got = together((a_got, b_got))
    a_own, a_leave = a[0] + wide(a_got[0]), a[A_SECOND] + wide(a_got[1])
    b_own, b_leave = b[0] + wide(b_got[0]), b[B_SECOND] + wide(b_got[1])
    a_got, b_got = swap_y(a_leave.astype(BF16), A_SECOND), swap_y(b_leave.astype(BF16), B_SECOND)
    a_got, b_got = together((a_got, b_got))
    rtwo = swap_side(rtwo, "gx", 1)
    part = jnp.concatenate([a_own + wide(a_got), b_own + wide(b_got)])
    leave = part.astype(BF16)
    got = swap_x(jnp.concatenate([leave[1], send[SENT:]]), 1)
    got = [got[:ROWS], swap_x(leave[2], 2), swap_x(leave[3], 3), got[ROWS:].reshape(rim)]
    *got, rone, rtwo = together((*got, rtwo))
    rows, qone, qtwo = call(
        fold_kernel, "fold_rim", (((BLOCKS_C,) + block, F32), (block, BF16), (block, BF16)), (), 8, (100_000, 600_000),
        own, rone, rtwo,
    )
    part = (part[0] + wide(got[0])) + (wide(got[1]) + wide(got[2]))
    mine = part.astype(BF16)
    got = [swap_z(mine, flip) for flip in (1, 2, 3)]
    *got, rows, qone, qtwo = together((*got, rows, qone, qtwo))
    part = (wide(mine) + wide(got[0])) + (wide(got[1]) + wide(got[2]))
    part = (part + swap(part, "gy", 9)).astype(BF16)
    got = together([swap_x(part, flip) for flip in (1, 3, 2)])
    part = jnp.stack([part, got[0], got[2], got[1]])
    a, b = part[:2], part[2:]
    a_got, b_got, qone, qtwo = together(
        (swap_y(a, A_SECOND), swap_y(b, B_SECOND), swap_side(qone, "gy", 0), swap_side(qtwo, "gy", 1))
    )
    a_near, b_near = jnp.stack([a, a_got]), jnp.stack([b, b_got])
    a_far, b_far = together((swap_y(a_near, A_FIRST), swap_y(b_near, B_FIRST)))
    near = swap(jnp.concatenate([a_near, b_near]), "gy", 1)
    far = swap(jnp.concatenate([a_far, b_far]), "gy", 1)
    (skip_grad,) = call(
        skip_kernel, "skip_gradient", (((SKIP, SIZE_X, SIZE_Y, LANES), BF16),), (((SKIP * BLOCKS, LANES), F32),),
        8, (1_000_000, 1_000_000), rows, qone, qtwo, jskip,
    )
    dec, coarse = call(
        unpack_kernel, "unpack", (((DEC, JOINED), F32), ((DEC, COARSE), F32)),
        (((CHUNKS * ROWS, LANES), F32), ((DEC, JOINED), F32), pltpu.SemaphoreType.DMA((3,))),
        16, (1_000_000, 5_000_000), a_near, a_far, b_near, b_far, near, far, gives=pltpu.HBM,
    )
    return (
        skip_grad,
        dec.reshape(TAPS, SKIP, JOINED).transpose(0, 2, 1),
        coarse.reshape(TAPS, SKIP, COARSE),
    )


def solution(mesh):
    placed = (P(None, "gx", "gy", None), P(None, "gx", "gy", None), P(), P())
    return jax.shard_map(
        body,
        mesh=mesh,
        in_specs=placed,
        out_specs=(P(None, "gx", "gy", None), P(), P()),
        check_vma=False,
    )
```
